32 devices in a mesh: gx: 4 (over x, core), gy: 2 (over y), gz: 4 (over z).
Axes of the slice: x: 2, y: 2, z: 4, core: 2. Of those that a mesh axis runs over, the one named last changes fastest.
Arguments:
- features: bfloat16 [4, 2, 4, 128, 128], P('gx', 'gy', 'gz'), may hold values from -6 to 6
- positions: float32 [4, 2, 4, 3, 128], P('gx', 'gy', 'gz'), may hold values from 0 to 1
- counts: int32 [4, 2, 4], P('gx', 'gy', 'gz'), may hold values from 1 to 128, as said below
- w_proj: bfloat16 [4, 128, 128], replicated, may hold values from -0.5 to 0.5
- w_mix: bfloat16 [128, 128], replicated, may hold values from -0.5 to 0.5
- w_long: bfloat16 [64, 128], replicated, may hold values from -0.75 to 0.75
- w_charge: bfloat16 [64, 128], replicated, may hold values from -0.5 to 0.5
- charge_bias: float32 [64], replicated, may hold values from -4 to 4
- w_energy: float32 [128], replicated, may hold values from -0.5 to 0.5
- k_filter: float32 [64, 2048], replicated, may hold values from 0.1 to 1
- k_index: int32 [3, 2048], replicated, may hold values from -6 to 6
Outputs:
- updated: bfloat16 [4, 2, 4, 128, 128], P('gx', 'gy', 'gz')
- energies: float32 [4, 2, 4, 128], P('gx', 'gy', 'gz')
- forces: float32 [4, 2, 4, 3, 128], P('gx', 'gy', 'gz')
The draws below stay inside these ranges and needn't reach their ends.
Inputs may be any that keep to these rules, and one draw needn't show every extreme that they name: Slots 0 to counts[x,y,z] - 1 of cell (x,y,z) hold live atoms, the rest are padding; some cell holds 128 live atoms.
All inputs are finite; a program needn't handle non-finite values.
Results may differ from the reference program's by a relative error of at most 0.0068.
Values may be sent and summed in bfloat16 or wider, within the bound.
No kernel may reach another device: no remote copies, remote signals or barrier semaphores. Data moves between devices by JAX's collectives and lax.ppermute only.
A program may use at most 64 MiB of HBM per device.

```python
import math
import jax
import jax.numpy as jnp
from jax import lax

CHANNELS = 128
BASES = 4
CHARGE_CH = 64
WAVES = 2048
ATOMS_CELL = 128
CELLS_X = 4
CELLS_Y = 2
CELLS_Z = 4


def draw_counts(key, part):
    levels = jnp.arange(CELLS_X, dtype=jnp.int32)
    lowest = ATOMS_CELL // 3
    rising = lowest + (ATOMS_CELL - lowest) * levels // max(CELLS_X - 1, 1)
    jitter = jax.random.randint(jax.random.fold_in(key, 11), (CELLS_X, CELLS_Y, CELLS_Z), 0, ATOMS_CELL // 8 + 1)
    counted = jnp.maximum(rising[:, None, None] - jitter, 1)
    counted = counted.at[CELLS_X - 1, 0, 0].set(ATOMS_CELL)
    return counted.astype(jnp.int32)


def with_ends(entries, stream_key, low, top_value):
    dims = entries.shape
    index_at = [jax.random.randint(jax.random.fold_in(stream_key, axis), (), 0, dims[axis]) for axis in range(len(dims))]
    entries = entries.at[tuple(index_at)].set(low)
    longest = dims.index(max(dims))
    index_at[longest] = (index_at[longest] + 1) % dims[longest]
    return entries.at[tuple(index_at)].set(top_value)


def block_levels(own_key, shape, pieces, low, top_value):
    loudness = 1.0
    for axis_at, blocks in pieces:
        draws = jax.random.uniform(jax.random.fold_in(jax.random.fold_in(own_key, 6), axis_at), (blocks,), jnp.float32, low / len(pieces), top_value / len(pieces))
        loudness = loudness * jnp.repeat(jnp.exp(draws), shape[axis_at] // blocks).reshape((-1,) + (1,) * (len(shape) - 1 - axis_at))
    return loudness


def noise(own_key, dims, deviation, reach, cuts=(), held_as=jnp.bfloat16):
    result = jax.random.normal(own_key, dims, jnp.float32) * deviation
    if len(cuts) > 0:
        result = block_levels(own_key, dims, cuts, -0.22, 0.18) * result
    return jnp.clip(result, min=-reach, max=reach).astype(held_as)


def setup_inputs(seed: int = 0) -> dict:
    key_of = jax.random.split(jax.random.key(seed), 12)
    return {
        "features": noise(key_of[0], (CELLS_X, CELLS_Y, CELLS_Z, ATOMS_CELL, CHANNELS), 1.0, 6.0, ((0, 4), (1, 2), (2, 4))),
        "positions": jnp.clip(1.0 * jax.random.uniform(key_of[1], (CELLS_X, CELLS_Y, CELLS_Z, 3, ATOMS_CELL), jnp.float32) ** block_levels(key_of[1], (CELLS_X, CELLS_Y, CELLS_Z, 3, ATOMS_CELL), ((0, 4), (1, 2), (2, 4)), -0.2, 0.2), 0.0, 1.0),
        "counts": draw_counts(jax.random.fold_in(key_of[11], 71), 0),
        "w_proj": noise(key_of[3], (BASES, CHANNELS, CHANNELS), CHANNELS ** -0.5, 0.5),
        "w_mix": noise(key_of[4], (CHANNELS, CHANNELS), CHANNELS ** -0.5, 0.5),
        "w_long": noise(key_of[5], (CHARGE_CH, CHANNELS), CHARGE_CH ** -0.5, 0.75),
        "w_charge": noise(key_of[6], (CHARGE_CH, CHANNELS), CHANNELS ** -0.5, 0.5),
        "charge_bias": noise(key_of[7], (CHARGE_CH,), 1.0, 4.0, (), jnp.float32),
        "w_energy": noise(key_of[8], (CHANNELS,), CHANNELS ** -0.5, 0.5, (), jnp.float32),
        "k_filter": jnp.clip(jnp.exp(jax.random.uniform(key_of[9], (CHARGE_CH, WAVES), jnp.float32, math.log(0.1), math.log(1.0))), 0.1, 1.0),
        "k_index": with_ends(jax.random.randint(key_of[10], (3, WAVES), -6, 7), jax.random.fold_in(key_of[10], 1), -6, 6).astype(jnp.int32),
    }


CUTOFF = 0.9
GAMMAS = (1.0, 3.0, 8.0, 20.0)
PRECISE = lax.Precision.HIGHEST
CONTRACT_LAST = (((1,), (1,)), ((), ()))
CONTRACT_FIRST = (((0,), (0,)), ((), ()))

def silu_grad(values):
    sigma = jax.nn.sigmoid(values)
    return sigma * (1.0 + values * (1.0 - sigma))

def pair_geometry(centre, others, neighbour):
    cell_shift = jnp.stack([neighbour // 9, neighbour // 3 % 3, neighbour % 3]).astype(jnp.float32) - 1.0
    offset_vec = others[:, None, :] + cell_shift[:, None, None] - centre[:, :, None]
    scaled = lax.optimization_barrier(jnp.sum(offset_vec * offset_vec, axis=0)) / (CUTOFF * CUTOFF)
    atom_count = centre.shape[1]
    slot_ids = jnp.arange(atom_count, dtype=jnp.int32)
    self_pair = (slot_ids[:, None] == slot_ids[None, :]) & (neighbour == 13)
    keep_mask = jnp.where(self_pair, 0.0, 1.0).astype(jnp.float32)
    envelope_base = jnp.maximum(1.0 - scaled, 0.0)
    decay_rates = jnp.asarray(GAMMAS, dtype=jnp.float32)[None, :, None]
    decay_terms = jnp.exp(-decay_rates * scaled[:, None, :]) * keep_mask[:, None, :]
    envelope = (envelope_base * envelope_base)[:, None, :]
    radial = decay_terms * envelope
    radial_slope = decay_terms * (-decay_rates * envelope - 2.0 * envelope_base[:, None, :])
    return (offset_vec, radial, radial_slope)

def phases(absolute, wave_vec):
    phase_angle = absolute[0][:, None] * wave_vec[0][None, :] + absolute[1][:, None] * wave_vec[1][None, :] + absolute[2][:, None] * wave_vec[2][None, :]
    return (jnp.cos(phase_angle), jnp.sin(phase_angle))

def reference(features, positions, counts, w_proj, w_mix, w_long, w_charge, charge_bias, w_energy, k_filter, k_index):
    cells_first, cells_second, cells_third = (features.shape[0], features.shape[1], features.shape[2])
    atom_count = features.shape[3]
    channels = features.shape[4]
    basis_count = w_proj.shape[0]
    cell_total = cells_first * cells_second * cells_third
    waves = k_index.shape[1]
    scale_long = 4.0 / math.sqrt(atom_count * cell_total * waves)
    living = (jnp.arange(atom_count, dtype=jnp.int32)[None, None, None, :] < counts[:, :, :, None]).astype(jnp.float32)
    masked = features * living[..., None].astype(jnp.bfloat16)
    basis_values = jnp.einsum('xyzjc,bcd->xyzbjd', masked.astype(jnp.float32), w_proj.astype(jnp.float32)).astype(jnp.bfloat16)
    charges = jax.nn.silu(jnp.einsum('ec,xyzjc->xyzej', w_charge.astype(jnp.float32), masked.astype(jnp.float32)) + charge_bias[:, None]) * living[:, :, :, None, :]
    charge_mean = lax.optimization_barrier(jnp.sum(charges, axis=(0, 1, 2, 4))) / jnp.sum(living)
    neutral = (charges - charge_mean[:, None]) * living[:, :, :, None, :]
    extent = jnp.asarray([cells_first, cells_second, cells_third], dtype=jnp.float32)
    wave_vec = 2.0 * math.pi * k_index.astype(jnp.float32) / extent[:, None]
    grid_x = jnp.arange(cells_first, dtype=jnp.int32)[:, None, None] + 0 * jnp.arange(cells_second, dtype=jnp.int32)[None, :, None] + 0 * jnp.arange(cells_third, dtype=jnp.int32)[None, None, :]
    grid_y = 0 * grid_x + jnp.arange(cells_second, dtype=jnp.int32)[None, :, None]
    grid_z = 0 * grid_x + jnp.arange(cells_third, dtype=jnp.int32)[None, None, :]
    anchor = jnp.stack([grid_x, grid_y, grid_z], axis=3).astype(jnp.float32)
    absolute = positions + anchor[..., None]
    flat_abs = absolute.reshape(cell_total, 3, atom_count)
    flat_neutral = neutral.reshape(cell_total, neutral.shape[3], atom_count)
    empty = jnp.zeros((neutral.shape[3], waves), jnp.float32)

    def add_structure(carry, item):
        place, charge_rows = item
        cosine, sine_part = phases(place, wave_vec)
        return ((carry[0] + jnp.dot(charge_rows, cosine, precision=PRECISE), carry[1] + jnp.dot(charge_rows, sine_part, precision=PRECISE)), None)
    (struct_c, struct_s), _ = lax.scan(add_structure, (empty, empty), (flat_abs, flat_neutral))
    filtered_cos = k_filter * struct_c
    filtered_sin = k_filter * struct_s

    def locate(cell_id, neighbour):
        cell_x = cell_id // (cells_second * cells_third)
        cell_y = cell_id // cells_third % cells_second
        cell_z = cell_id % cells_third
        return ((cell_x + neighbour // 9 - 1) % cells_first, (cell_y + neighbour // 3 % 3 - 1) % cells_second, (cell_z + neighbour % 3 - 1) % cells_third)

    def forward_cell(carry, cell_id):
        home = locate(cell_id, 13)
        own_rows = features[home]
        centre = positions[home]
        alive_row = living[home]
        message = jnp.zeros((atom_count, channels), jnp.float32)
        for neighbour in range(27):
            near_cell = locate(cell_id, neighbour)
            offset_vec, radial, radial_slope = pair_geometry(centre, positions[near_cell], neighbour)
            message = message + jnp.dot(radial.astype(jnp.bfloat16).reshape(atom_count, -1), basis_values[near_cell].reshape(-1, channels), preferred_element_type=jnp.float32)
        cosine, sine_part = phases(flat_abs[cell_id], wave_vec)
        potential = scale_long * (lax.dot_general(filtered_cos, cosine, CONTRACT_LAST, precision=PRECISE) + lax.dot_general(filtered_sin, sine_part, CONTRACT_LAST, precision=PRECISE))
        pre_act = jnp.dot(message.astype(jnp.bfloat16), w_mix, preferred_element_type=jnp.float32) + lax.dot_general(potential.astype(jnp.bfloat16), w_long, CONTRACT_FIRST, preferred_element_type=jnp.float32)
        refined = own_rows.astype(jnp.float32) + jax.nn.silu(pre_act)
        energy = alive_row * lax.optimization_barrier(jnp.sum(jax.nn.silu(refined) * w_energy[None, :], axis=1))
        grad_new = alive_row[:, None] * w_energy[None, :] * silu_grad(refined)
        grad_pre = (grad_new * silu_grad(pre_act)).astype(jnp.bfloat16)
        adjoint = lax.dot_general(grad_pre, w_mix, CONTRACT_LAST, preferred_element_type=jnp.float32).astype(jnp.bfloat16)
        pull_back = lax.dot_general(w_long, grad_pre, CONTRACT_LAST, preferred_element_type=jnp.float32)
        carry = (carry[0] + jnp.dot(pull_back, cosine, precision=PRECISE), carry[1] + jnp.dot(pull_back, sine_part, precision=PRECISE))
        return (carry, (refined.astype(jnp.bfloat16), energy, adjoint, pull_back))
    cell_ids = jnp.arange(cell_total, dtype=jnp.int32)
    (back_c, back_s), (updated, energies, adjoints, pulls) = lax.scan(forward_cell, (empty, empty), cell_ids)
    adjoint_grid = adjoints.reshape(cells_first, cells_second, cells_third, atom_count, channels)
    weights_along = jnp.concatenate([filtered_sin, k_filter * back_s], axis=0)
    weights_across = jnp.concatenate([filtered_cos, k_filter * back_c], axis=0)

    def force_cell(cell_id):
        home = locate(cell_id, 13)
        centre = positions[home]
        local_proj = basis_values[home]
        own_adjoint = adjoint_grid[home]
        near_force = jnp.zeros((3, atom_count), jnp.float32)
        for neighbour in range(27):
            near_cell = locate(cell_id, neighbour)
            offset_vec, radial, radial_slope = pair_geometry(centre, positions[near_cell], neighbour)
            first_term = lax.dot_general(own_adjoint, basis_values[near_cell].reshape(-1, channels), CONTRACT_LAST, preferred_element_type=jnp.float32).reshape(atom_count, basis_count, atom_count)
            second_term = jnp.einsum('bic,jc->ibj', local_proj.astype(jnp.float32), adjoint_grid[near_cell].astype(jnp.float32))
            strength = lax.optimization_barrier(jnp.sum(radial_slope * (first_term + second_term), axis=1))
            near_force = near_force + 2.0 / (CUTOFF * CUTOFF) * lax.optimization_barrier(jnp.sum(strength[None, :, :] * offset_vec, axis=2))
        cosine, sine_part = phases(flat_abs[cell_id], wave_vec)
        mixing = jnp.concatenate([pulls[cell_id], flat_neutral[cell_id]], axis=0)
        along_term = lax.dot_general(mixing, weights_along, CONTRACT_FIRST, precision=PRECISE)
        across_term = lax.dot_general(mixing, weights_across, CONTRACT_FIRST, precision=PRECISE)
        ewald_grad = lax.dot_general(wave_vec, cosine * along_term - sine_part * across_term, CONTRACT_LAST, precision=PRECISE)
        return near_force - scale_long * ewald_grad
    forces = lax.map(force_cell, cell_ids)
    return (updated.reshape(features.shape), energies.reshape(cells_first, cells_second, cells_third, atom_count), forces.reshape(positions.shape))
```

```python
import itertools
import math

import jax
import jax.numpy as jnp
import numpy as np
from jax import lax
from jax.experimental import pallas as pl
from jax.experimental.pallas import tpu as pltpu
from jax.sharding import PartitionSpec as P

CUTOFF = 0.9
SCALE = 1.0 / (CUTOFF * CUTOFF)
GAMMAS = (1.0, 3.0, 8.0, 20.0)
AXES = ("gx", "gy", "gz")
ORDERS = 7
NT = (((1,), (1,)), ((), ()))
F32 = jnp.float32
BF16 = jnp.bfloat16
VMEM_BYTES = 56 * 1024 * 1024


def turn_series():
    nodes = np.cos(np.pi * (np.arange(200) + 0.5) / 200)
    r2 = (nodes + 1.0) / 8.0
    r = np.sqrt(r2)
    out = []
    for values in (np.cos(2 * np.pi * r), np.sin(2 * np.pi * r) / r):
        cheb = np.polynomial.chebyshev.Chebyshev.fit(r2, values, 7, domain=[0.0, 0.25])
        out.append([float(c) for c in cheb.convert(kind=np.polynomial.Polynomial).coef])
    return out


COS_SERIES, SIN_SERIES = turn_series()


def dot(a, b):
    return jnp.dot(a, b, preferred_element_type=F32)


def dot_nt(a, b):
    return lax.dot_general(a, b, NT, preferred_element_type=F32)


def sigmoid(v):
    return 1.0 / (1.0 + jnp.exp(-v))


def cos_sin(turns):
    r = turns - jnp.floor(turns + 0.5)
    r2 = r * r
    c = jnp.full_like(r2, COS_SERIES[-1])
    for coef in COS_SERIES[-2::-1]:
        c = c * r2 + coef
    s = jnp.full_like(r2, SIN_SERIES[-1])
    for coef in SIN_SERIES[-2::-1]:
        s = s * r2 + coef
    return c, s * r


def axis_tables(pos, anchor, sizes):
    order = lax.broadcasted_iota(jnp.int32, (8, pos.shape[1]), 0).astype(F32)
    tables = []
    for a in range(3):
        row = (pos[a : a + 1, :] + anchor[a]) * (1.0 / sizes[a])
        tables.append(cos_sin(order * row))
    return tables


def plane_table(first, second):
    rows = []
    for f in first:
        for s in second:
            for a in range(8):
                rows.append(f[a : a + 1, :] * s)
    return jnp.concatenate(rows, axis=0)


def derivative(table, size):
    order = lax.broadcasted_iota(jnp.int32, table[0].shape, 0).astype(F32) * (2.0 * math.pi / size)
    return (-order * table[1], order * table[0])


def spread(weights, third):
    rows = []
    for f in third:
        for c in range(ORDERS):
            rows.append((weights * f[c : c + 1, :]).astype(BF16))
    return jnp.concatenate(rows, axis=0)


def filtered(sums_ref, filt_ref, out_ref, charge_ch):
    for c in range(ORDERS):
        lo, hi = c * charge_ch, (c + 1) * charge_ch
        f0, gfb, fc, gfbc = (filt_ref[c, w * charge_ch : (w + 1) * charge_ch, :] for w in range(4))
        a_c, b_c = sums_ref[lo:hi, 0:128], sums_ref[lo:hi, 128:256]
        shift = ORDERS * charge_ch
        a_s, b_s = (
            sums_ref[shift + lo : shift + hi, 0:128],
            sums_ref[shift + lo : shift + hi, 128:256],
        )
        ra_c, rb_c, ra_s, rb_s = (pltpu.roll(v, 64, 1) for v in (a_c, b_c, a_s, b_s))
        out_ref[lo:hi, 0:128] = (f0 * a_c + gfbc * ra_s - fc * b_s + gfb * rb_c).astype(BF16)
        out_ref[lo:hi, 128:256] = (f0 * b_c - gfb * ra_c + fc * a_s + gfbc * rb_s).astype(BF16)
        out_ref[shift + lo : shift + hi, 0:128] = (
            f0 * a_s + fc * b_c - gfbc * ra_c + gfb * rb_s
        ).astype(BF16)
        out_ref[shift + lo : shift + hi, 128:256] = (
            f0 * b_s - fc * a_c - gfb * ra_s - gfbc * rb_c
        ).astype(BF16)


def field_slope(field, tables, sizes, weights, charge_ch):
    tx, ty, tz = tables
    n = tx[0].shape[1]
    planes = jnp.concatenate(
        [
            plane_table(derivative(tx, sizes[0]), ty).astype(BF16),
            plane_table(tx, derivative(ty, sizes[1])).astype(BF16),
            plane_table(tx, ty).astype(BF16),
        ],
        axis=1,
    )
    spread_field = dot(field, planes)
    slope_z = derivative(tz, sizes[2])
    total = [jnp.zeros((charge_ch, n), F32) for _ in range(3)]
    for kind in range(2):
        for c in range(ORDERS):
            lo = (kind * ORDERS + c) * charge_ch
            part = spread_field[lo : lo + charge_ch, :]
            zrow, drow = tz[kind][c : c + 1, :], slope_z[kind][c : c + 1, :]
            total[0] = total[0] + zrow * part[:, 0:n]
            total[1] = total[1] + zrow * part[:, n : 2 * n]
            total[2] = total[2] + drow * part[:, 2 * n : 3 * n]
    return [jnp.sum(t * weights, axis=0, keepdims=True) for t in total]


def place_of(meta_ref, m, half, sizes):
    nx, ny, nz = sizes
    dz = lax.rem(m, nz)
    dy = lax.rem(m // nz, ny)
    dx = m // (nz * ny)
    start = meta_ref[0] if half == 0 else meta_ref[0] + 1 - 2 * lax.rem(meta_ref[0], 2)
    cx = lax.rem(start - 2 * dx + nx, nx)
    cy = lax.rem(meta_ref[1] - dy + ny, ny)
    cz = lax.rem(meta_ref[2] - dz + nz, nz)
    return (cx.astype(F32), cy.astype(F32), cz.astype(F32))


def blocks_of(sizes):
    options = [((0, False), (1, True)) if n == 2 else ((0, False), (-1, False), (1, False)) for n in sizes]
    return list(itertools.product(*options))


def offsets(own_cols, others, block):
    result = []
    for a, (step, nearest) in enumerate(block):
        if nearest:
            d = others[a] - own_cols[a]
            d = d - jnp.where(d > 0.0, 1.0, -1.0)
        else:
            d = (others[a] + float(step)) - own_cols[a]
        result.append(d)
    return result


def pair_terms(offs, block, first_row):
    s = (offs[0] * offs[0] + offs[1] * offs[1] + offs[2] * offs[2]) * SCALE
    u = jnp.maximum(1.0 - s, 0.0)
    if all(step == 0 for step, _ in block):
        rows = lax.broadcasted_iota(jnp.int32, s.shape, 0) + first_row
        cols = lax.broadcasted_iota(jnp.int32, s.shape, 1)
        u = jnp.where(rows == cols, 0.0, u)
    e1 = jnp.exp(-s)
    e2 = e1 * e1
    e3 = e2 * e1
    e4 = e2 * e2
    e8 = e4 * e4
    e20 = e8 * e8 * e4
    return u, (e1, e3, e8, e20)


def columns(pos, n):
    return [jnp.transpose(jnp.broadcast_to(pos[a : a + 1, :], (n, n))) for a in range(3)]


def pack_kernel(count_ref, features_ref, positions_ref, out_ref):
    n, channels = features_ref.shape
    live_col = lax.broadcasted_iota(jnp.int32, (n, channels), 0) < count_ref[0]
    rows = features_ref[...].astype(F32)
    out_ref[0:n, :] = jnp.where(live_col, rows, 0.0).astype(BF16)
    pos = positions_ref[...]
    coarse = pos.astype(BF16).astype(F32)
    fine = pos - coarse
    living = (lax.broadcasted_iota(jnp.int32, (1, n), 1) < count_ref[0]).astype(F32)
    blank = jnp.zeros((4, n), F32)
    tail = jnp.concatenate([coarse, living, blank, fine, jnp.zeros((5, n), F32)], axis=0)
    out_ref[n : n + 16, :] = tail.astype(BF16)


def fold_kernel(scale, filter_ref, index_ref, out_ref):
    waves = filter_ref.shape[1]
    k = index_ref[...]
    positive = [jnp.where(k[a : a + 1, :] >= 0, 1.0, -1.0) for a in range(3)]
    sign_b = positive[0] * positive[1]
    sign_c = positive[0] * positive[2]
    size = jnp.abs(k)
    plane = size[0:1, :] * 8 + size[1:2, :]
    f = filter_ref[...] * scale
    stacked = jnp.concatenate([f, f * sign_b, f * sign_c, f * (sign_b * sign_c)], axis=0).astype(BF16)
    rows = lax.broadcasted_iota(jnp.int32, (64, waves), 0)
    charge_ch = filter_ref.shape[0]
    turn = jnp.where(lax.broadcasted_iota(jnp.int32, (charge_ch, 128), 1) < 64, -1.0, 1.0)
    for c in range(ORDERS):
        key = jnp.where(size[2:3, :] == c, plane, -1)
        chosen = jnp.where(rows == key, 1.0, 0.0).astype(BF16)
        part = dot_nt(stacked, jnp.concatenate([chosen, chosen], axis=0))
        for w in range(4):
            piece = part[w * charge_ch : (w + 1) * charge_ch, :]
            out_ref[c, w * charge_ch : (w + 1) * charge_ch, :] = piece * turn if w % 2 == 1 else piece


def forward_kernel(
    sizes,
    group,
    count_ref,
    meta_ref,
    near_ref,
    far_ref,
    features_ref,
    w_proj_ref,
    w_mix_ref,
    w_long_ref,
    w_charge_ref,
    bias_ref,
    w_energy_ref,
    filt_ref,
    updated_ref,
    energy_ref,
    grad_ref,
    field_ref,
    neutral_ref,
    places_ref,
    xcat_ref,
    charge_scr,
    sums_scr,
    radial_scr,
):
    n, channels = features_ref.shape
    charge_ch = w_charge_ref.shape[0]
    half_cells = near_ref.shape[0]
    groups = half_cells // group
    halves = (near_ref, far_ref)
    w_charge = w_charge_ref[...]
    bias = bias_ref[...]

    total = jnp.zeros((charge_ch, 1), F32)
    live_total = jnp.zeros((1, 1), F32)
    for half in range(2):
        ref = halves[half]

        def add_charges(g, carry, ref=ref, half=half):
            total, live_total = carry
            for j in range(group):
                m = g * group + j
                tail = ref[m, n : n + 16, :].astype(F32)
                pos = tail[0:8, :] + tail[8:16, :]
                places_ref[half * half_cells + m] = pos
                live = pos[3:4, :]
                v = dot_nt(w_charge, ref[m, 0:n, :]) + bias
                q = v * sigmoid(v) * live
                charge_scr[half * half_cells + m] = q
                total = total + jnp.sum(q, axis=1, keepdims=True)
                live_total = live_total + jnp.sum(live, axis=1, keepdims=True)
            return total, live_total

        total, live_total = lax.fori_loop(0, groups, add_charges, (total, live_total))
    mean = total / live_total

    sums_scr[...] = jnp.zeros_like(sums_scr)
    for half in range(2):

        def add_structure(g, _, half=half):
            left, right = [], []
            for j in range(group):
                m = g * group + j
                pos = places_ref[half * half_cells + m]
                tx, ty, tz = axis_tables(pos, place_of(meta_ref, m, half, sizes), sizes)
                neutral = (charge_scr[half * half_cells + m] - mean) * pos[3:4, :]
                left.append(spread(neutral, tz))
                right.append(plane_table(tx, ty).astype(BF16))
            sums_scr[...] += dot_nt(jnp.concatenate(left, axis=1), jnp.concatenate(right, axis=1))
            return 0

        lax.fori_loop(0, groups, add_structure, 0)

    filtered(sums_scr, filt_ref, field_ref, charge_ch)
    own = places_ref[0]
    live_row = own[3:4, :]
    neutral_ref[...] = (charge_scr[0] - mean) * live_row
    tx, ty, tz = axis_tables(own, place_of(meta_ref, 0, 0, sizes), sizes)
    lifted = dot(field_ref[...], plane_table(tx, ty).astype(BF16))
    potential = jnp.zeros((charge_ch, n), F32)
    for kind in range(2):
        for c in range(ORDERS):
            lo = (kind * ORDERS + c) * charge_ch
            potential = potential + tz[kind][c : c + 1, :] * lifted[lo : lo + charge_ch, :]

    nx, ny, nz = sizes
    odd = lax.rem(meta_ref[0], 2)
    own_cols = columns(own, n)
    for t, block in enumerate(blocks_of(sizes)):
        half = 0 if block[0][0] == 0 else 1
        dy, dz = (-block[1][0]) % ny, (-block[2][0]) % nz
        if half == 0:
            dx = 0
        elif block[0][0] == 1:
            dx = odd * (nx // 2 - 1)
        else:
            dx = (1 - odd) * (1 % (nx // 2))
        m = (dx * ny + dy) * nz + dz
        xcat_ref[t * n : (t + 1) * n, :] = halves[half][m, 0:n, :]
        pos = places_ref[half * half_cells + m]
        others = [pos[a : a + 1, :] for a in range(3)]
        for first in range(0, n, 32):
            cols = [c[first : first + 32, :] for c in own_cols]
            u, decays = pair_terms(offsets(cols, others, block), block, first)
            u2 = u * u
            for b in range(len(GAMMAS)):
                radial_scr[b * n + first : b * n + first + 32, t * n : (t + 1) * n] = (
                    decays[b] * u2
                ).astype(BF16)
    gathered = dot(radial_scr[...], xcat_ref[...]).astype(BF16)
    message = jnp.zeros((n, channels), F32)
    for b in range(len(GAMMAS)):
        message = message + dot(gathered[b * n : (b + 1) * n, :], w_proj_ref[b])

    pre_act = dot(message.astype(BF16), w_mix_ref[...]) + dot(
        jnp.transpose(potential).astype(BF16), w_long_ref[...]
    )
    sig = sigmoid(pre_act)
    refined = features_ref[...].astype(F32) + pre_act * sig
    updated_ref[...] = refined.astype(BF16)
    sig_r = sigmoid(refined)
    w_energy = w_energy_ref[...]
    energy_ref[...] = live_row * jnp.sum(
        jnp.transpose(refined * sig_r * w_energy), axis=0, keepdims=True
    )
    live_rows = lax.broadcasted_iota(jnp.int32, (n, channels), 0) < count_ref[0]
    grad = (
        w_energy
        * (sig_r * (1.0 + refined * (1.0 - sig_r)))
        * (sig * (1.0 + pre_act * (1.0 - sig)))
    )
    grad_ref[...] = jnp.where(live_rows, grad, 0.0).astype(BF16)


def pair_force(sizes, own, neighbour_pos, strengths_ref, n):
    own_cols = columns(own, n)
    blocks = blocks_of(sizes)
    parts = [[], [], []]
    for first in range(0, n, 32):
        cols = [c[first : first + 32, :] for c in own_cols]
        acc = [jnp.zeros((32, n), F32) for _ in range(3)]
        for t, block in enumerate(blocks):
            pos = neighbour_pos(t)
            offs = offsets(cols, [pos[a : a + 1, :] for a in range(3)], block)
            u, decays = pair_terms(offs, block, first)
            strength = jnp.zeros((32, n), F32)
            for b, g in enumerate(GAMMAS):
                part = strengths_ref[b * n + first : b * n + first + 32, t * n : (t + 1) * n]
                strength = strength + decays[b] * (g * u + 2.0) * part
            strength = strength * u
            for a in range(3):
                acc[a] = acc[a] + strength * offs[a]
        for a in range(3):
            parts[a].append(acc[a])
    return [
        (-2.0 * SCALE)
        * jnp.sum(jnp.transpose(jnp.concatenate(parts[a], axis=0)), axis=0, keepdims=True)
        for a in range(3)
    ]


def block_place(sizes, odd, block):
    nx, ny, nz = sizes
    half_cells = nx // 2 * ny * nz
    dy, dz = (-block[1][0]) % ny, (-block[2][0]) % nz
    if block[0][0] == 0:
        return dy * nz + dz
    dx = odd * (nx // 2 - 1) if block[0][0] == 1 else (1 - odd) * (1 % (nx // 2))
    return half_cells + (dx * ny + dy) * nz + dz


def own_kernel(
    sizes,
    meta_ref,
    grad_ref,
    field_ref,
    places_ref,
    xcat_ref,
    w_proj_ref,
    w_mix_ref,
    w_long_ref,
    force_ref,
    lifted_ref,
    strength_scr,
):
    n = grad_ref.shape[0]
    charge_ch = w_long_ref.shape[0]
    grad = grad_ref[...]
    adjoint = dot_nt(grad, w_mix_ref[...]).astype(BF16)
    rows, lifted = [], []
    for b in range(len(GAMMAS)):
        rows.append(dot_nt(adjoint, w_proj_ref[b]).astype(BF16))
        basis = dot(xcat_ref[0:n, :], w_proj_ref[b]).astype(BF16)
        lifted.append(dot(basis, w_mix_ref[...]).astype(BF16))
    lifted_ref[...] = jnp.concatenate(lifted, axis=0)
    strength_scr[...] = dot_nt(jnp.concatenate(rows, axis=0), xcat_ref[...])
    odd = lax.rem(meta_ref[0], 2)
    blocks = blocks_of(sizes)
    own = places_ref[0]
    near = pair_force(
        sizes, own, lambda t: places_ref[block_place(sizes, odd, blocks[t])], strength_scr, n
    )
    pull = dot_nt(w_long_ref[...], grad)
    tables = axis_tables(own, place_of(meta_ref, 0, 0, sizes), sizes)
    slope = field_slope(field_ref[...], tables, sizes, pull, charge_ch)
    force_ref[...] = jnp.concatenate([near[a] - slope[a] for a in range(3)], axis=0)


def backward_kernel(
    sizes,
    group,
    meta_ref,
    near_ref,
    far_ref,
    places_ref,
    neutral_ref,
    lifted_ref,
    force_ref,
    w_long_ref,
    filt_ref,
    out_ref,
    sums_scr,
    field_scr,
    gcat_scr,
    strength_scr,
):
    n = neutral_ref.shape[1]
    charge_ch = w_long_ref.shape[0]
    half_cells = near_ref.shape[0]
    groups = half_cells // group
    halves = (near_ref, far_ref)
    sums_scr[...] = jnp.zeros_like(sums_scr)
    for half in range(2):

        def add_structure(g, _, half=half):
            left, right = [], []
            for j in range(group):
                m = g * group + j
                pos = places_ref[half * half_cells + m]
                tx, ty, tz = axis_tables(pos, place_of(meta_ref, m, half, sizes), sizes)
                left.append(spread(dot_nt(w_long_ref[...], halves[half][m]), tz))
                right.append(plane_table(tx, ty).astype(BF16))
            sums_scr[...] += dot_nt(jnp.concatenate(left, axis=1), jnp.concatenate(right, axis=1))
            return 0

        lax.fori_loop(0, groups, add_structure, 0)
    filtered(sums_scr, filt_ref, field_scr, charge_ch)
    own = places_ref[0]
    tables = axis_tables(own, place_of(meta_ref, 0, 0, sizes), sizes)
    slope = field_slope(field_scr[...], tables, sizes, neutral_ref[...], charge_ch)

    odd = lax.rem(meta_ref[0], 2)
    blocks = blocks_of(sizes)
    for t, block in enumerate(blocks):
        place = block_place(sizes, odd, block)
        half = 0 if block[0][0] == 0 else 1
        gcat_scr[t * n : (t + 1) * n, :] = halves[half][place - half * half_cells]
    strength_scr[...] = dot_nt(lifted_ref[...], gcat_scr[...])
    near = pair_force(
        sizes, own, lambda t: places_ref[block_place(sizes, odd, blocks[t])], strength_scr, n
    )
    out_ref[...] = force_ref[...] + jnp.concatenate([near[a] - slope[a] for a in range(3)], axis=0)


def gather_cells(rows, sizes):
    nx, ny, nz = sizes
    pairs = nx // 2

    def shifted(value, dx, dy):
        moves = []
        for i in range(nx):
            for j in range(ny):
                moves.append((i * ny + j, (i + 2 * dx) % nx * ny + (j + dy) % ny))
        return lax.ppermute(value, ("gx", "gy"), moves)

    value = rows[None]
    value = jnp.concatenate(
        [value]
        + [
            lax.ppermute(value, "gz", [(i, (i + s) % nz) for i in range(nz)])
            for s in range(1, nz)
        ],
        axis=0,
    )
    if pairs * ny <= 4:
        steps = [(dx, dy) for dx in range(pairs) for dy in range(ny)]
        value = jnp.concatenate(
            [value] + [shifted(value, dx, dy) for dx, dy in steps[1:]], axis=0
        )
    else:
        value = jnp.concatenate([value] + [shifted(value, 0, dy) for dy in range(1, ny)], axis=0)
        value = jnp.concatenate([value] + [shifted(value, dx, 0) for dx in range(1, pairs)], axis=0)
    other = lax.ppermute(value, "gx", [(i, i ^ 1) for i in range(nx)])
    return value, other


def call(kernel, name, outs, scratch, smem, operands, flops):
    n_in = len(operands)
    specs = [pl.BlockSpec(memory_space=pltpu.SMEM)] * smem + [
        pl.BlockSpec(memory_space=pltpu.VMEM)
    ] * (n_in - smem)
    return pl.pallas_call(
        kernel,
        name=name,
        out_shape=outs,
        in_specs=specs,
        out_specs=[pl.BlockSpec(memory_space=pltpu.VMEM)] * len(outs),
        scratch_shapes=scratch,
        compiler_params=pltpu.CompilerParams(vmem_limit_bytes=VMEM_BYTES),
        cost_estimate=pl.CostEstimate(flops=flops, bytes_accessed=2_000_000, transcendentals=0),
    )(*operands)


def shards(
    features,
    positions,
    counts,
    w_proj,
    w_mix,
    w_long,
    w_charge,
    charge_bias,
    w_energy,
    k_filter,
    k_index,
):
    own_rows = features[0, 0, 0]
    n, channels = own_rows.shape
    charge_ch = w_charge.shape[0]
    waves = k_index.shape[1]
    bases = w_proj.shape[0]
    sizes = tuple(lax.axis_size(a) for a in AXES)
    cells = sizes[0] * sizes[1] * sizes[2]
    half_cells = cells // 2
    group = max(g for g in (8, 4, 2, 1) if half_cells % g == 0)
    blocks = len(blocks_of(sizes))
    scale_long = 4.0 / math.sqrt(n * cells * waves)
    count = counts.reshape(1)
    meta = jnp.stack([lax.axis_index(a) for a in AXES]).astype(jnp.int32)
    shape = jax.ShapeDtypeStruct
    wide = 2 * ORDERS * charge_ch

    (packed,) = call(
        pack_kernel,
        "pack",
        [shape((n + 16, channels), BF16)],
        [],
        1,
        [count, own_rows, positions[0, 0, 0]],
        1000,
    )
    near, far = gather_cells(packed, sizes)
    (filt,) = call(
        lambda *refs: fold_kernel(scale_long, *refs),
        "fold_filter",
        [shape((ORDERS, 4 * charge_ch, 128), F32)],
        [],
        0,
        [k_filter, k_index],
        1_000_000_000,
    )
    updated, energy, grad, field, neutral, places, xcat = call(
        lambda *refs: forward_kernel(sizes, group, *refs),
        "forward",
        [
            shape((n, channels), BF16),
            shape((1, n), F32),
            shape((n, channels), BF16),
            shape((wide, 256), BF16),
            shape((charge_ch, n), F32),
            shape((cells, 8, n), F32),
            shape((blocks * n, channels), BF16),
        ],
        [
            pltpu.VMEM((cells, charge_ch, n), F32),
            pltpu.VMEM((wide, 256), F32),
            pltpu.VMEM((bases * n, blocks * n), BF16),
        ],
        2,
        [
            count,
            meta,
            near,
            far,
            own_rows,
            w_proj,
            w_mix,
            w_long,
            w_charge,
            charge_bias[:, None],
            w_energy[None, :],
            filt,
        ],
        5_000_000_000,
    )
    grad_near, grad_far = gather_cells(grad, sizes)
    force, lifted = call(
        lambda *refs: own_kernel(sizes, *refs),
        "own_forces",
        [shape((3, n), F32), shape((bases * n, channels), BF16)],
        [pltpu.VMEM((bases * n, blocks * n), F32)],
        1,
        [meta, grad, field, places, xcat, w_proj, w_mix, w_long],
        5_000_000_000,
    )
    (forces,) = call(
        lambda *refs: backward_kernel(sizes, group, *refs),
        "backward",
        [shape((3, n), F32)],
        [
            pltpu.VMEM((wide, 256), F32),
            pltpu.VMEM((wide, 256), BF16),
            pltpu.VMEM((blocks * n, channels), BF16),
            pltpu.VMEM((bases * n, blocks * n), F32),
        ],
        1,
        [meta, grad_near, grad_far, places, neutral, lifted, force, w_long, filt],
        5_000_000_000,
    )
    return (
        updated[None, None, None],
        energy[None, None],
        forces[None, None, None],
    )


def solution(mesh):
    cell = ("gx", "gy", "gz")
    in_specs = (P(*cell, None, None), P(*cell, None, None), P(*cell)) + (P(),) * 8
    out_specs = (P(*cell, None, None), P(*cell, None), P(*cell, None, None))
    return jax.shard_map(shards, mesh=mesh, in_specs=in_specs, out_specs=out_specs, check_vma=False)
```

```python
import itertools
import math

import jax
import jax.numpy as jnp
import numpy as np
from jax import lax
from jax.experimental import pallas as pl
from jax.experimental.pallas import tpu as pltpu
from jax.sharding import PartitionSpec as P

CUTOFF = 0.9
SCALE = 1.0 / (CUTOFF * CUTOFF)
GAMMAS = (1.0, 3.0, 8.0, 20.0)
AXES = ("gx", "gy", "gz")
ORDERS = 7
NT = (((1,), (1,)), ((), ()))
F32 = jnp.float32
BF16 = jnp.bfloat16
VMEM_BYTES = 56 * 1024 * 1024


def turn_series():
    nodes = np.cos(np.pi * (np.arange(200) + 0.5) / 200)
    r2 = (nodes + 1.0) / 8.0
    r = np.sqrt(r2)
    out = []
    for values in (np.cos(2 * np.pi * r), np.sin(2 * np.pi * r) / r):
        cheb = np.polynomial.chebyshev.Chebyshev.fit(r2, values, 7, domain=[0.0, 0.25])
        out.append([float(c) for c in cheb.convert(kind=np.polynomial.Polynomial).coef])
    return out


COS_SERIES, SIN_SERIES = turn_series()


def dot(a, b):
    return jnp.dot(a, b, preferred_element_type=F32)


def dot_nt(a, b):
    return lax.dot_general(a, b, NT, preferred_element_type=F32)


def sigmoid(v):
    return 1.0 / (1.0 + jnp.exp(-v))


def cos_sin(turns):
    r = turns - jnp.floor(turns + 0.5)
    r2 = r * r
    c = jnp.full_like(r2, COS_SERIES[-1])
    for coef in COS_SERIES[-2::-1]:
        c = c * r2 + coef
    s = jnp.full_like(r2, SIN_SERIES[-1])
    for coef in SIN_SERIES[-2::-1]:
        s = s * r2 + coef
    return c, s * r


def axis_tables(pos, anchor, sizes):
    order = lax.broadcasted_iota(jnp.int32, (8, pos.shape[1]), 0).astype(F32)
    tables = []
    for a in range(3):
        row = (pos[a : a + 1, :] + anchor[a]) * (1.0 / sizes[a])
        tables.append(cos_sin(order * row))
    return tables


def plane_table(first, second):
    rows = []
    for f in first:
        for s in second:
            for a in range(8):
                rows.append(f[a : a + 1, :] * s)
    return jnp.concatenate(rows, axis=0)


def derivative(table, size):
    order = lax.broadcasted_iota(jnp.int32, table[0].shape, 0).astype(F32) * (2.0 * math.pi / size)
    return (-order * table[1], order * table[0])


def spread(weights, third):
    rows = []
    for f in third:
        for c in range(ORDERS):
            rows.append((weights * f[c : c + 1, :]).astype(BF16))
    return jnp.concatenate(rows, axis=0)


def filtered(sums_ref, filt_ref, out_ref, charge_ch):
    for c in range(ORDERS):
        lo, hi = c * charge_ch, (c + 1) * charge_ch
        f0, gfb, fc, gfbc = (filt_ref[c, w * charge_ch : (w + 1) * charge_ch, :] for w in range(4))
        a_c, b_c = sums_ref[lo:hi, 0:128], sums_ref[lo:hi, 128:256]
        shift = ORDERS * charge_ch
        a_s, b_s = (
            sums_ref[shift + lo : shift + hi, 0:128],
            sums_ref[shift + lo : shift + hi, 128:256],
        )
        ra_c, rb_c, ra_s, rb_s = (pltpu.roll(v, 64, 1) for v in (a_c, b_c, a_s, b_s))
        out_ref[lo:hi, 0:128] = (f0 * a_c + gfbc * ra_s - fc * b_s + gfb * rb_c).astype(BF16)
        out_ref[lo:hi, 128:256] = (f0 * b_c - gfb * ra_c + fc * a_s + gfbc * rb_s).astype(BF16)
        out_ref[shift + lo : shift + hi, 0:128] = (
            f0 * a_s + fc * b_c - gfbc * ra_c + gfb * rb_s
        ).astype(BF16)
        out_ref[shift + lo : shift + hi, 128:256] = (
            f0 * b_s - fc * a_c - gfb * ra_s - gfbc * rb_c
        ).astype(BF16)


def field_slope(field, tables, sizes, weights, charge_ch):
    tx, ty, tz = tables
    n = tx[0].shape[1]
    planes = jnp.concatenate(
        [
            plane_table(derivative(tx, sizes[0]), ty).astype(BF16),
            plane_table(tx, derivative(ty, sizes[1])).astype(BF16),
            plane_table(tx, ty).astype(BF16),
        ],
        axis=1,
    )
    spread_field = dot(field, planes)
    slope_z = derivative(tz, sizes[2])
    total = [jnp.zeros((charge_ch, n), F32) for _ in range(3)]
    for kind in range(2):
        for c in range(ORDERS):
            lo = (kind * ORDERS + c) * charge_ch
            part = spread_field[lo : lo + charge_ch, :]
            zrow, drow = tz[kind][c : c + 1, :], slope_z[kind][c : c + 1, :]
            total[0] = total[0] + zrow * part[:, 0:n]
            total[1] = total[1] + zrow * part[:, n : 2 * n]
            total[2] = total[2] + drow * part[:, 2 * n : 3 * n]
    return [jnp.sum(t * weights, axis=0, keepdims=True) for t in total]


def place_of(meta_ref, m, half, sizes):
    nx, ny, nz = sizes
    dz = lax.rem(m, nz)
    dy = lax.rem(m // nz, ny)
    dx = m // (nz * ny)
    start = meta_ref[0] if half == 0 else meta_ref[0] + 1 - 2 * lax.rem(meta_ref[0], 2)
    cx = lax.rem(start - 2 * dx + nx, nx)
    cy = lax.rem(meta_ref[1] - dy + ny, ny)
    cz = lax.rem(meta_ref[2] - dz + nz, nz)
    return (cx.astype(F32), cy.astype(F32), cz.astype(F32))


def blocks_of(sizes):
    options = [((0, False), (1, True)) if n == 2 else ((0, False), (-1, False), (1, False)) for n in sizes]
    return list(itertools.product(*options))


def offsets(own_cols, others, block):
    result = []
    for a, (step, nearest) in enumerate(block):
        if nearest:
            d = others[a] - own_cols[a]
            d = d - jnp.where(d > 0.0, 1.0, -1.0)
        else:
            d = (others[a] + float(step)) - own_cols[a]
        result.append(d)
    return result


def pair_terms(offs, block, first_row):
    s = (offs[0] * offs[0] + offs[1] * offs[1] + offs[2] * offs[2]) * SCALE
    u = jnp.maximum(1.0 - s, 0.0)
    if all(step == 0 for step, _ in block):
        rows = lax.broadcasted_iota(jnp.int32, s.shape, 0) + first_row
        cols = lax.broadcasted_iota(jnp.int32, s.shape, 1)
        u = jnp.where(rows == cols, 0.0, u)
    e1 = jnp.exp(-s)
    e2 = e1 * e1
    e3 = e2 * e1
    e4 = e2 * e2
    e8 = e4 * e4
    e20 = e8 * e8 * e4
    return u, (e1, e3, e8, e20)


def columns(pos, n):
    return [jnp.transpose(jnp.broadcast_to(pos[a : a + 1, :], (n, n))) for a in range(3)]


def pack_kernel(count_ref, features_ref, positions_ref, out_ref):
    n, channels = features_ref.shape
    live_col = lax.broadcasted_iota(jnp.int32, (n, channels), 0) < count_ref[0]
    rows = features_ref[...].astype(F32)
    out_ref[0:n, :] = jnp.where(live_col, rows, 0.0).astype(BF16)
    pos = jnp.concatenate([positions_ref[a] for a in range(3)], axis=0)
    coarse = pos.astype(BF16).astype(F32)
    fine = pos - coarse
    living = (lax.broadcasted_iota(jnp.int32, (1, n), 1) < count_ref[0]).astype(F32)
    blank = jnp.zeros((4, n), F32)
    tail = jnp.concatenate([coarse, living, blank, fine, jnp.zeros((5, n), F32)], axis=0)
    out_ref[n : n + 16, :] = tail.astype(BF16)


def fold_kernel(scale, filter_ref, index_ref, out_ref):
    waves = filter_ref.shape[1]
    k = index_ref[...]
    positive = [jnp.where(k[a : a + 1, :] >= 0, 1.0, -1.0) for a in range(3)]
    sign_b = positive[0] * positive[1]
    sign_c = positive[0] * positive[2]
    size = jnp.abs(k)
    plane = size[0:1, :] * 8 + size[1:2, :]
    f = filter_ref[...] * scale
    stacked = jnp.concatenate([f, f * sign_b, f * sign_c, f * (sign_b * sign_c)], axis=0).astype(BF16)
    rows = lax.broadcasted_iota(jnp.int32, (64, waves), 0)
    charge_ch = filter_ref.shape[0]
    turn = jnp.where(lax.broadcasted_iota(jnp.int32, (charge_ch, 128), 1) < 64, -1.0, 1.0)
    for c in range(ORDERS):
        key = jnp.where(size[2:3, :] == c, plane, -1)
        chosen = jnp.where(rows == key, 1.0, 0.0).astype(BF16)
        part = dot_nt(stacked, jnp.concatenate([chosen, chosen], axis=0))
        for w in range(4):
            piece = part[w * charge_ch : (w + 1) * charge_ch, :]
            out_ref[c, w * charge_ch : (w + 1) * charge_ch, :] = piece * turn if w % 2 == 1 else piece


def forward_kernel(
    sizes,
    group,
    count_ref,
    meta_ref,
    near_ref,
    far_ref,
    features_ref,
    w_proj_ref,
    w_mix_ref,
    w_long_ref,
    w_charge_ref,
    bias_ref,
    w_energy_ref,
    filt_ref,
    updated_ref,
    energy_ref,
    grad_ref,
    field_ref,
    neutral_ref,
    places_ref,
    xcat_ref,
    charge_scr,
    sums_scr,
    radial_scr,
):
    n, channels = features_ref.shape
    charge_ch = w_charge_ref.shape[0]
    half_cells = near_ref.shape[0]
    groups = half_cells // group
    halves = (near_ref, far_ref)
    w_charge = w_charge_ref[...]
    diagonal = lax.broadcasted_iota(jnp.int32, (charge_ch, charge_ch), 0) == (
        lax.broadcasted_iota(jnp.int32, (charge_ch, charge_ch), 1)
    )
    bias = jnp.sum(jnp.where(diagonal, bias_ref[...], 0.0), axis=1, keepdims=True)

    total = jnp.zeros((charge_ch, 1), F32)
    live_total = jnp.zeros((1, 1), F32)
    for half in range(2):
        ref = halves[half]

        def add_charges(g, carry, ref=ref, half=half):
            total, live_total = carry
            for j in range(group):
                m = g * group + j
                tail = ref[m, n : n + 16, :].astype(F32)
                pos = tail[0:8, :] + tail[8:16, :]
                places_ref[half * half_cells + m] = pos
                live = pos[3:4, :]
                v = dot_nt(w_charge, ref[m, 0:n, :]) + bias
                q = v * sigmoid(v) * live
                charge_scr[half * half_cells + m] = q
                total = total + jnp.sum(q, axis=1, keepdims=True)
                live_total = live_total + jnp.sum(live, axis=1, keepdims=True)
            return total, live_total

        total, live_total = lax.fori_loop(0, groups, add_charges, (total, live_total))
    mean = total / live_total

    sums_scr[...] = jnp.zeros_like(sums_scr)
    for half in range(2):

        def add_structure(g, _, half=half):
            left, right = [], []
            for j in range(group):
                m = g * group + j
                pos = places_ref[half * half_cells + m]
                tx, ty, tz = axis_tables(pos, place_of(meta_ref, m, half, sizes), sizes)
                neutral = (charge_scr[half * half_cells + m] - mean) * pos[3:4, :]
                left.append(spread(neutral, tz))
                right.append(plane_table(tx, ty).astype(BF16))
            sums_scr[...] += dot_nt(jnp.concatenate(left, axis=1), jnp.concatenate(right, axis=1))
            return 0

        lax.fori_loop(0, groups, add_structure, 0)

    filtered(sums_scr, filt_ref, field_ref, charge_ch)
    own = places_ref[0]
    live_row = own[3:4, :]
    neutral_ref[...] = (charge_scr[0] - mean) * live_row
    tx, ty, tz = axis_tables(own, place_of(meta_ref, 0, 0, sizes), sizes)
    lifted = dot(field_ref[...], plane_table(tx, ty).astype(BF16))
    potential = jnp.zeros((charge_ch, n), F32)
    for kind in range(2):
        for c in range(ORDERS):
            lo = (kind * ORDERS + c) * charge_ch
            potential = potential + tz[kind][c : c + 1, :] * lifted[lo : lo + charge_ch, :]

    nx, ny, nz = sizes
    odd = lax.rem(meta_ref[0], 2)
    own_cols = columns(own, n)
    for t, block in enumerate(blocks_of(sizes)):
        half = 0 if block[0][0] == 0 else 1
        dy, dz = (-block[1][0]) % ny, (-block[2][0]) % nz
        if half == 0:
            dx = 0
        elif block[0][0] == 1:
            dx = odd * (nx // 2 - 1)
        else:
            dx = (1 - odd) * (1 % (nx // 2))
        m = (dx * ny + dy) * nz + dz
        xcat_ref[t * n : (t + 1) * n, :] = halves[half][m, 0:n, :]
        pos = places_ref[half * half_cells + m]
        others = [pos[a : a + 1, :] for a in range(3)]
        for first in range(0, n, 32):
            cols = [c[first : first + 32, :] for c in own_cols]
            u, decays = pair_terms(offsets(cols, others, block), block, first)
            u2 = u * u
            for b in range(len(GAMMAS)):
                radial_scr[b * n + first : b * n + first + 32, t * n : (t + 1) * n] = (
                    decays[b] * u2
                ).astype(BF16)
    gathered = dot(radial_scr[...], xcat_ref[...]).astype(BF16)
    message = jnp.zeros((n, channels), F32)
    for b in range(len(GAMMAS)):
        message = message + dot(gathered[b * n : (b + 1) * n, :], w_proj_ref[b])

    pre_act = dot(message.astype(BF16), w_mix_ref[...]) + dot(
        jnp.transpose(potential).astype(BF16), w_long_ref[...]
    )
    sig = sigmoid(pre_act)
    refined = features_ref[...].astype(F32) + pre_act * sig
    updated_ref[...] = refined.astype(BF16)
    sig_r = sigmoid(refined)
    w_energy = w_energy_ref[...]
    energy_ref[...] = live_row * jnp.sum(
        jnp.transpose(refined * sig_r * w_energy), axis=0, keepdims=True
    )
    live_rows = lax.broadcasted_iota(jnp.int32, (n, channels), 0) < count_ref[0]
    grad = (
        w_energy
        * (sig_r * (1.0 + refined * (1.0 - sig_r)))
        * (sig * (1.0 + pre_act * (1.0 - sig)))
    )
    grad_ref[...] = jnp.where(live_rows, grad, 0.0).astype(BF16)


def pair_force(sizes, own, neighbour_pos, strengths_ref, n):
    own_cols = columns(own, n)
    blocks = blocks_of(sizes)
    parts = [[], [], []]
    for first in range(0, n, 32):
        cols = [c[first : first + 32, :] for c in own_cols]
        acc = [jnp.zeros((32, n), F32) for _ in range(3)]
        for t, block in enumerate(blocks):
            pos = neighbour_pos(t)
            offs = offsets(cols, [pos[a : a + 1, :] for a in range(3)], block)
            u, decays = pair_terms(offs, block, first)
            strength = jnp.zeros((32, n), F32)
            for b, g in enumerate(GAMMAS):
                part = strengths_ref[b * n + first : b * n + first + 32, t * n : (t + 1) * n]
                strength = strength + decays[b] * (g * u + 2.0) * part
            strength = strength * u
            for a in range(3):
                acc[a] = acc[a] + strength * offs[a]
        for a in range(3):
            parts[a].append(acc[a])
    return [
        (-2.0 * SCALE)
        * jnp.sum(jnp.transpose(jnp.concatenate(parts[a], axis=0)), axis=0, keepdims=True)
        for a in range(3)
    ]


def block_place(sizes, odd, block):
    nx, ny, nz = sizes
    half_cells = nx // 2 * ny * nz
    dy, dz = (-block[1][0]) % ny, (-block[2][0]) % nz
    if block[0][0] == 0:
        return dy * nz + dz
    dx = odd * (nx // 2 - 1) if block[0][0] == 1 else (1 - odd) * (1 % (nx // 2))
    return half_cells + (dx * ny + dy) * nz + dz


def own_kernel(
    sizes,
    meta_ref,
    grad_ref,
    field_ref,
    places_ref,
    xcat_ref,
    w_proj_ref,
    w_mix_ref,
    w_long_ref,
    force_ref,
    lifted_ref,
    strength_scr,
):
    n = grad_ref.shape[0]
    charge_ch = w_long_ref.shape[0]
    grad = grad_ref[...]
    adjoint = dot_nt(grad, w_mix_ref[...]).astype(BF16)
    rows, lifted = [], []
    for b in range(len(GAMMAS)):
        rows.append(dot_nt(adjoint, w_proj_ref[b]).astype(BF16))
        basis = dot(xcat_ref[0:n, :], w_proj_ref[b]).astype(BF16)
        lifted.append(dot(basis, w_mix_ref[...]).astype(BF16))
    lifted_ref[...] = jnp.concatenate(lifted, axis=0)
    strength_scr[...] = dot_nt(jnp.concatenate(rows, axis=0), xcat_ref[...])
    odd = lax.rem(meta_ref[0], 2)
    blocks = blocks_of(sizes)
    own = places_ref[0]
    near = pair_force(
        sizes, own, lambda t: places_ref[block_place(sizes, odd, blocks[t])], strength_scr, n
    )
    pull = dot_nt(w_long_ref[...], grad)
    tables = axis_tables(own, place_of(meta_ref, 0, 0, sizes), sizes)
    slope = field_slope(field_ref[...], tables, sizes, pull, charge_ch)
    force_ref[...] = jnp.concatenate([near[a] - slope[a] for a in range(3)], axis=0)


def backward_kernel(
    sizes,
    group,
    meta_ref,
    near_ref,
    far_ref,
    places_ref,
    neutral_ref,
    lifted_ref,
    force_ref,
    w_long_ref,
    filt_ref,
    out_ref,
    sums_scr,
    field_scr,
    gcat_scr,
    strength_scr,
):
    n = neutral_ref.shape[1]
    charge_ch = w_long_ref.shape[0]
    half_cells = near_ref.shape[0]
    groups = half_cells // group
    halves = (near_ref, far_ref)
    sums_scr[...] = jnp.zeros_like(sums_scr)
    for half in range(2):

        def add_structure(g, _, half=half):
            left, right = [], []
            for j in range(group):
                m = g * group + j
                pos = places_ref[half * half_cells + m]
                tx, ty, tz = axis_tables(pos, place_of(meta_ref, m, half, sizes), sizes)
                left.append(spread(dot_nt(w_long_ref[...], halves[half][m]), tz))
                right.append(plane_table(tx, ty).astype(BF16))
            sums_scr[...] += dot_nt(jnp.concatenate(left, axis=1), jnp.concatenate(right, axis=1))
            return 0

        lax.fori_loop(0, groups, add_structure, 0)
    filtered(sums_scr, filt_ref, field_scr, charge_ch)
    own = places_ref[0]
    tables = axis_tables(own, place_of(meta_ref, 0, 0, sizes), sizes)
    slope = field_slope(field_scr[...], tables, sizes, neutral_ref[...], charge_ch)

    odd = lax.rem(meta_ref[0], 2)
    blocks = blocks_of(sizes)
    for t, block in enumerate(blocks):
        place = block_place(sizes, odd, block)
        half = 0 if block[0][0] == 0 else 1
        gcat_scr[t * n : (t + 1) * n, :] = halves[half][place - half * half_cells]
    strength_scr[...] = dot_nt(lifted_ref[...], gcat_scr[...])
    near = pair_force(
        sizes, own, lambda t: places_ref[block_place(sizes, odd, blocks[t])], strength_scr, n
    )
    for a in range(3):
        out_ref[a] = force_ref[a : a + 1, :] + near[a] - slope[a]


def gather_cells(rows, sizes, beside):
    nx, ny, nz = sizes
    pairs = nx // 2

    def shifted(value, dx, dy):
        moves = []
        for i in range(nx):
            for j in range(ny):
                moves.append((i * ny + j, (i + 2 * dx) % nx * ny + (j + dy) % ny))
        return lax.ppermute(value, ("gx", "gy"), moves)

    value = rows[None]
    value = jnp.concatenate(
        [value]
        + [
            lax.ppermute(value, "gz", [(i, (i + s) % nz) for i in range(nz)])
            for s in range(1, nz)
        ],
        axis=0,
    )
    if pairs * ny <= 4:
        steps = [(dx, dy) for dx in range(pairs) for dy in range(ny)]
        value = jnp.concatenate(
            [value] + [shifted(value, dx, dy) for dx, dy in steps[1:]], axis=0
        )
    else:
        value = jnp.concatenate([value] + [shifted(value, 0, dy) for dy in range(1, ny)], axis=0)
        value = jnp.concatenate([value] + [shifted(value, dx, 0) for dx in range(1, pairs)], axis=0)
    value, *beside = lax.optimization_barrier((value, *beside))
    other = lax.ppermute(value, "gx", [(i, i ^ 1) for i in range(nx)])
    return value, other, *beside


def call(kernel, name, outs, scratch, smem, operands, flops):
    n_in = len(operands)
    specs = [pl.BlockSpec(memory_space=pltpu.SMEM)] * smem + [
        pl.BlockSpec(memory_space=pltpu.VMEM)
    ] * (n_in - smem)
    return pl.pallas_call(
        kernel,
        name=name,
        out_shape=outs,
        in_specs=specs,
        out_specs=[pl.BlockSpec(memory_space=pltpu.VMEM)] * len(outs),
        scratch_shapes=scratch,
        compiler_params=pltpu.CompilerParams(vmem_limit_bytes=VMEM_BYTES),
        cost_estimate=pl.CostEstimate(flops=flops, bytes_accessed=2_000_000, transcendentals=0),
    )(*operands)


def shards(
    features,
    positions,
    counts,
    w_proj,
    w_mix,
    w_long,
    w_charge,
    charge_bias,
    w_energy,
    k_filter,
    k_index,
):
    own_rows = features[0, 0, 0]
    n, channels = own_rows.shape
    charge_ch = w_charge.shape[0]
    waves = k_index.shape[1]
    bases = w_proj.shape[0]
    sizes = tuple(lax.axis_size(a) for a in AXES)
    cells = sizes[0] * sizes[1] * sizes[2]
    half_cells = cells // 2
    group = max(g for g in (8, 4, 2, 1) if half_cells % g == 0)
    blocks = len(blocks_of(sizes))
    scale_long = 4.0 / math.sqrt(n * cells * waves)
    count = counts.reshape(1)
    meta = jnp.stack([lax.axis_index(a) for a in AXES]).astype(jnp.int32)
    shape = jax.ShapeDtypeStruct
    wide = 2 * ORDERS * charge_ch

    (packed,) = call(
        pack_kernel,
        "pack",
        [shape((n + 16, channels), BF16)],
        [],
        1,
        [count, own_rows, positions.reshape(3, 1, n)],
        1000,
    )
    (filt,) = call(
        lambda *refs: fold_kernel(scale_long, *refs),
        "fold_filter",
        [shape((ORDERS, 4 * charge_ch, 128), F32)],
        [],
        0,
        [k_filter, k_index],
        1_000_000_000,
    )
    near, far, filt = gather_cells(packed, sizes, (filt,))
    updated, energy, grad, field, neutral, places, xcat = call(
        lambda *refs: forward_kernel(sizes, group, *refs),
        "forward",
        [
            shape((n, channels), BF16),
            shape((1, n), F32),
            shape((n, channels), BF16),
            shape((wide, 256), BF16),
            shape((charge_ch, n), F32),
            shape((cells, 8, n), F32),
            shape((blocks * n, channels), BF16),
        ],
        [
            pltpu.VMEM((cells, charge_ch, n), F32),
            pltpu.VMEM((wide, 256), F32),
            pltpu.VMEM((bases * n, blocks * n), BF16),
        ],
        2,
        [
            count,
            meta,
            near,
            far,
            own_rows,
            w_proj,
            w_mix,
            w_long,
            w_charge,
            charge_bias[None, :],
            w_energy[None, :],
            filt,
        ],
        5_000_000_000,
    )
    force, lifted = call(
        lambda *refs: own_kernel(sizes, *refs),
        "own_forces",
        [shape((3, n), F32), shape((bases * n, channels), BF16)],
        [pltpu.VMEM((bases * n, blocks * n), F32)],
        1,
        [meta, grad, field, places, xcat, w_proj, w_mix, w_long],
        5_000_000_000,
    )
    grad_near, grad_far, force, lifted = gather_cells(grad, sizes, (force, lifted))
    (forces,) = call(
        lambda *refs: backward_kernel(sizes, group, *refs),
        "backward",
        [shape((3, 1, n), F32)],
        [
            pltpu.VMEM((wide, 256), F32),
            pltpu.VMEM((wide, 256), BF16),
            pltpu.VMEM((blocks * n, channels), BF16),
            pltpu.VMEM((bases * n, blocks * n), F32),
        ],
        1,
        [meta, grad_near, grad_far, places, neutral, lifted, force, w_long, filt],
        5_000_000_000,
    )
    return (
        updated[None, None, None],
        energy[None, None],
        forces.reshape(positions.shape),
    )


def solution(mesh):
    cell = ("gx", "gy", "gz")
    in_specs = (P(*cell, None, None), P(*cell, None, None), P(*cell)) + (P(),) * 8
    out_specs = (P(*cell, None, None), P(*cell, None), P(*cell, None, None))
    return jax.shard_map(shards, mesh=mesh, in_specs=in_specs, out_specs=out_specs, check_vma=False)
```

```python
import itertools
import math

import jax
import jax.numpy as jnp
import numpy as np
from jax import lax
from jax.experimental import pallas as pl
from jax.experimental.pallas import tpu as pltpu
from jax.sharding import PartitionSpec as P

CUTOFF = 0.9
SCALE = 1.0 / (CUTOFF * CUTOFF)
GAMMAS = (1.0, 3.0, 8.0, 20.0)
AXES = ("gx", "gy", "gz")
ORDERS = 7
NT = (((1,), (1,)), ((), ()))
F32 = jnp.float32
BF16 = jnp.bfloat16


def turn_series():
    nodes = np.cos(np.pi * (np.arange(200) + 0.5) / 200)
    r2 = (nodes + 1.0) / 8.0
    r = np.sqrt(r2)
    out = []
    for values in (np.cos(2 * np.pi * r), np.sin(2 * np.pi * r) / r):
        cheb = np.polynomial.chebyshev.Chebyshev.fit(r2, values, 7, domain=[0.0, 0.25])
        out.append([float(c) for c in cheb.convert(kind=np.polynomial.Polynomial).coef])
    return out


COS_SERIES, SIN_SERIES = turn_series()


def dot(a, b):
    return jnp.dot(a, b, preferred_element_type=F32)


def dot_nt(a, b):
    return lax.dot_general(a, b, NT, preferred_element_type=F32)


def sigmoid(v):
    return 1.0 / (1.0 + jnp.exp(-v))


def cos_sin(turns):
    r = turns - jnp.floor(turns + 0.5)
    r2 = r * r
    c = jnp.full_like(r2, COS_SERIES[-1])
    for coef in COS_SERIES[-2::-1]:
        c = c * r2 + coef
    s = jnp.full_like(r2, SIN_SERIES[-1])
    for coef in SIN_SERIES[-2::-1]:
        s = s * r2 + coef
    return c, s * r


def axis_tables(pos, anchor, sizes):
    order = lax.broadcasted_iota(jnp.int32, (8, pos.shape[1]), 0).astype(F32)
    tables = []
    for a in range(3):
        row = (pos[a : a + 1, :] + anchor[a]) * (1.0 / sizes[a])
        tables.append(cos_sin(order * row))
    return tables


def plane_table(first, second):
    rows = []
    for f in first:
        for s in second:
            for a in range(8):
                rows.append(f[a : a + 1, :] * s)
    return jnp.concatenate(rows, axis=0)


def derivative(table, size):
    order = lax.broadcasted_iota(jnp.int32, table[0].shape, 0).astype(F32) * (2.0 * math.pi / size)
    return (-order * table[1], order * table[0])


def spread(weights, third):
    rows = []
    for f in third:
        for c in range(ORDERS):
            rows.append((weights * f[c : c + 1, :]).astype(BF16))
    return jnp.concatenate(rows, axis=0)


def filtered(load, filt_ref, out_ref, charge_ch):
    shift = ORDERS * charge_ch
    for c in range(ORDERS):
        lo, hi = c * charge_ch, (c + 1) * charge_ch
        f0, gfb, fc, gfbc = (filt_ref[c, w * charge_ch : (w + 1) * charge_ch, :] for w in range(4))
        cos_part, sin_part = load(0, c), load(1, c)
        a_c, b_c = cos_part[:, 0:128], cos_part[:, 128:256]
        a_s, b_s = sin_part[:, 0:128], sin_part[:, 128:256]
        ra_c, rb_c, ra_s, rb_s = (pltpu.roll(v, 64, 1) for v in (a_c, b_c, a_s, b_s))
        out_ref[lo:hi, 0:128] = (f0 * a_c + gfbc * ra_s - fc * b_s + gfb * rb_c).astype(BF16)
        out_ref[lo:hi, 128:256] = (f0 * b_c - gfb * ra_c + fc * a_s + gfbc * rb_s).astype(BF16)
        out_ref[shift + lo : shift + hi, 0:128] = (
            f0 * a_s + fc * b_c - gfbc * ra_c + gfb * rb_s
        ).astype(BF16)
        out_ref[shift + lo : shift + hi, 128:256] = (
            f0 * b_s - fc * a_c - gfb * ra_s - gfbc * rb_c
        ).astype(BF16)


def field_slope(field, tables, sizes, weights, charge_ch):
    tx, ty, tz = tables
    n = tx[0].shape[1]
    planes = jnp.concatenate(
        [
            plane_table(derivative(tx, sizes[0]), ty).astype(BF16),
            plane_table(tx, derivative(ty, sizes[1])).astype(BF16),
            plane_table(tx, ty).astype(BF16),
        ],
        axis=1,
    )
    spread_field = dot(field, planes)
    slope_z = derivative(tz, sizes[2])
    total = [jnp.zeros((charge_ch, n), F32) for _ in range(3)]
    for kind in range(2):
        for c in range(ORDERS):
            lo = (kind * ORDERS + c) * charge_ch
            part = spread_field[lo : lo + charge_ch, :]
            zrow, drow = tz[kind][c : c + 1, :], slope_z[kind][c : c + 1, :]
            total[0] = total[0] + zrow * part[:, 0:n]
            total[1] = total[1] + zrow * part[:, n : 2 * n]
            total[2] = total[2] + drow * part[:, 2 * n : 3 * n]
    return [jnp.sum(t * weights, axis=0, keepdims=True) for t in total]


def place_of(meta_ref, m, half, sizes):
    nx, ny, nz = sizes
    dz = lax.rem(m, nz)
    dy = lax.rem(m // nz, ny)
    dx = m // (nz * ny)
    start = meta_ref[0] if half == 0 else meta_ref[0] + 1 - 2 * lax.rem(meta_ref[0], 2)
    cx = lax.rem(start - 2 * dx + nx, nx)
    cy = lax.rem(meta_ref[1] - dy + ny, ny)
    cz = lax.rem(meta_ref[2] - dz + nz, nz)
    return (cx.astype(F32), cy.astype(F32), cz.astype(F32))


def blocks_of(sizes):
    options = [((0, False), (1, True)) if n == 2 else ((0, False), (-1, False), (1, False)) for n in sizes]
    return list(itertools.product(*options))


def offsets(own_cols, others, block):
    result = []
    for a, (step, nearest) in enumerate(block):
        if nearest:
            d = others[a] - own_cols[a]
            d = d - jnp.where(d > 0.0, 1.0, -1.0)
        else:
            d = (others[a] + float(step)) - own_cols[a]
        result.append(d)
    return result


def pair_terms(offs, block, first_row):
    s = (offs[0] * offs[0] + offs[1] * offs[1] + offs[2] * offs[2]) * SCALE
    u = jnp.maximum(1.0 - s, 0.0)
    if all(step == 0 for step, _ in block):
        rows = lax.broadcasted_iota(jnp.int32, s.shape, 0) + first_row
        cols = lax.broadcasted_iota(jnp.int32, s.shape, 1)
        u = jnp.where(rows == cols, 0.0, u)
    e1 = jnp.exp(-s)
    e2 = e1 * e1
    e3 = e2 * e1
    e4 = e2 * e2
    e8 = e4 * e4
    e20 = e8 * e8 * e4
    return u, (e1, e3, e8, e20)


def columns(pos, n):
    return [jnp.transpose(jnp.broadcast_to(pos[a : a + 1, :], (n, n))) for a in range(3)]


def pack_kernel(count_ref, features_ref, positions_ref, out_ref):
    n, channels = features_ref.shape
    live_col = lax.broadcasted_iota(jnp.int32, (n, channels), 0) < count_ref[0]
    rows = features_ref[...].astype(F32)
    out_ref[0:n, :] = jnp.where(live_col, rows, 0.0).astype(BF16)
    pos = jnp.concatenate([positions_ref[a] for a in range(3)], axis=0)
    coarse = pos.astype(BF16).astype(F32)
    fine = pos - coarse
    living = (lax.broadcasted_iota(jnp.int32, (1, n), 1) < count_ref[0]).astype(F32)
    blank = jnp.zeros((4, n), F32)
    tail = jnp.concatenate([coarse, living, blank, fine, jnp.zeros((5, n), F32)], axis=0)
    out_ref[n : n + 16, :] = tail.astype(BF16)


def fold_kernel(scale, filter_ref, index_ref, bias_ref, energy_ref, out_ref, column_ref, row_ref):
    waves = filter_ref.shape[1]
    k = index_ref[...]
    positive = [jnp.where(k[a : a + 1, :] >= 0, 1.0, -1.0) for a in range(3)]
    sign_b = positive[0] * positive[1]
    sign_c = positive[0] * positive[2]
    size = jnp.abs(k)
    plane = size[0:1, :] * 8 + size[1:2, :]
    f = filter_ref[...] * scale
    stacked = jnp.concatenate([f, f * sign_b, f * sign_c, f * (sign_b * sign_c)], axis=0).astype(BF16)
    rows = lax.broadcasted_iota(jnp.int32, (64, waves), 0)
    charge_ch = filter_ref.shape[0]
    row_ref[...] = energy_ref[...]
    diagonal = lax.broadcasted_iota(jnp.int32, (charge_ch, charge_ch), 0) == (
        lax.broadcasted_iota(jnp.int32, (charge_ch, charge_ch), 1)
    )
    column = jnp.sum(jnp.where(diagonal, bias_ref[...], 0.0), axis=1, keepdims=True)
    column_ref[...] = jnp.broadcast_to(column, column_ref.shape)
    turn = jnp.where(lax.broadcasted_iota(jnp.int32, (charge_ch, 128), 1) < 64, -1.0, 1.0)
    for c in range(ORDERS):
        key = jnp.where(size[2:3, :] == c, plane, -1)
        chosen = jnp.where(rows == key, 1.0, 0.0).astype(BF16)
        part = dot_nt(stacked, jnp.concatenate([chosen, chosen], axis=0))
        for w in range(4):
            piece = part[w * charge_ch : (w + 1) * charge_ch, :]
            out_ref[c, w * charge_ch : (w + 1) * charge_ch, :] = piece * turn if w % 2 == 1 else piece


def block_place(sizes, odd, block):
    nx, ny, nz = sizes
    dy, dz = (-block[1][0]) % ny, (-block[2][0]) % nz
    if block[0][0] == 0:
        return 0, dy * nz + dz
    dx = odd * (nx // 2 - 1) if block[0][0] == 1 else (1 - odd) * (1 % (nx // 2))
    return 1, (dx * ny + dy) * nz + dz


def charge_kernel(
    sizes,
    group,
    meta_ref,
    near_ref,
    w_charge_ref,
    bias_ref,
    sums_ref,
    part_ref,
    places_ref,
    charge_ref,
    charge_scr,
):
    charge_ch, channels = w_charge_ref.shape
    cells = near_ref.shape[0]
    n = near_ref.shape[1] - 16
    wide = 2 * ORDERS * charge_ch
    groups = cells // group
    w_charge = w_charge_ref[...]
    bias = bias_ref[...]

    def add_charges(g, carry):
        total, live_total = carry
        for j in range(group):
            m = g * group + j
            tail = near_ref[m, n : n + 16, :].astype(F32)
            pos = tail[0:8, :] + tail[8:16, :]
            places_ref[m] = pos
            live = pos[3:4, :]
            v = dot_nt(w_charge, near_ref[m, 0:n, :]) + bias
            q = v * sigmoid(v) * live
            charge_scr[m] = q
            total = total + q
            live_total = live_total + live
        return total, live_total

    start = (jnp.zeros((charge_ch, n), F32), jnp.zeros((1, n), F32))
    total, live_total = lax.fori_loop(0, groups, add_charges, start)
    mean = jnp.sum(total, axis=1, keepdims=True) / jnp.sum(live_total, axis=1, keepdims=True)
    mean = mean.astype(BF16).astype(F32)
    charge_ref[...] = charge_scr[0]

    def structure(g):
        left, right = [], []
        for j in range(group):
            m = g * group + j
            pos = places_ref[m]
            tx, ty, tz = axis_tables(pos, place_of(meta_ref, m, 0, sizes), sizes)
            live = pos[3:4, :]
            living = jnp.concatenate([tz[0] * live, tz[1] * live], axis=0).astype(BF16)
            left.append(
                jnp.concatenate([spread((charge_scr[m] - mean) * live, tz), living], axis=0)
            )
            right.append(plane_table(tx, ty).astype(BF16))
        return dot_nt(jnp.concatenate(left, axis=1), jnp.concatenate(right, axis=1))

    sums_ref[...] = structure(0)

    def add_structure(g, _):
        sums_ref[...] += structure(g)
        return 0

    lax.fori_loop(1, groups, add_structure, 0)
    part_ref[0 : wide + 16, :] = sums_ref[...].astype(BF16)
    part_ref[wide + 16 : wide + 16 + charge_ch, :] = jnp.broadcast_to(mean, (charge_ch, 256)).astype(
        BF16
    )


def message_kernel(
    sizes,
    meta_ref,
    near_ref,
    far_ref,
    near_places_ref,
    w_proj_ref,
    w_mix_ref,
    short_ref,
    far_places_ref,
    xcat_ref,
    radial_scr,
):
    channels = near_ref.shape[2]
    n = near_ref.shape[1] - 16
    halves = (near_ref, far_ref)
    places = (near_places_ref, far_places_ref)

    def add_place(m, _):
        tail = far_ref[m, n : n + 16, :].astype(F32)
        far_places_ref[m] = tail[0:8, :] + tail[8:16, :]
        return 0

    lax.fori_loop(0, far_ref.shape[0], add_place, 0, unroll=4)
    odd = lax.rem(meta_ref[0], 2)
    own_cols = columns(near_places_ref[0], n)
    for t, block in enumerate(blocks_of(sizes)):
        half, m = block_place(sizes, odd, block)
        xcat_ref[t * n : (t + 1) * n, :] = halves[half][m, 0:n, :]
        pos = places[half][m]
        others = [pos[a : a + 1, :] for a in range(3)]
        for first in range(0, n, 32):
            cols = [c[first : first + 32, :] for c in own_cols]
            u, decays = pair_terms(offsets(cols, others, block), block, first)
            u2 = u * u
            for b in range(len(GAMMAS)):
                radial_scr[b * n + first : b * n + first + 32, t * n : (t + 1) * n] = (
                    decays[b] * u2
                ).astype(BF16)
    gathered = dot(radial_scr[...], xcat_ref[...]).astype(BF16)
    message = jnp.zeros((n, channels), F32)
    for b in range(len(GAMMAS)):
        message = message + dot(gathered[b * n : (b + 1) * n, :], w_proj_ref[b])
    short_ref[...] = dot(message.astype(BF16), w_mix_ref[...])


def cotangent_kernel(
    sizes,
    count_ref,
    meta_ref,
    sums_ref,
    part_ref,
    far_part_ref,
    places_ref,
    far_places_ref,
    charge_ref,
    short_ref,
    features_ref,
    w_long_ref,
    w_energy_ref,
    filt_ref,
    grad_ref,
    refined_ref,
    field_ref,
    neutral_ref,
):
    n, channels = features_ref.shape
    charge_ch = w_long_ref.shape[0]
    wide = 2 * ORDERS * charge_ch
    own = places_ref[0]
    live_row = own[3:4, :]

    lives = [jnp.sum(r[...], axis=0)[3:4, :] for r in (places_ref, far_places_ref)]
    lives = [jnp.sum(v, axis=1, keepdims=True) for v in lives]
    tail = wide + 16
    bases = [r[tail : tail + charge_ch, 0:1].astype(F32) for r in (part_ref, far_part_ref)]
    rests = [sums_ref[0:charge_ch, 0:1], far_part_ref[0:charge_ch, 0:1].astype(F32)]
    mean = (bases[0] * lives[0] + rests[0] + bases[1] * lives[1] + rests[1]) / (lives[0] + lives[1])
    gaps = [b - mean for b in bases]
    far_living = far_part_ref[wide : wide + 16, :].astype(F32)

    def load(kind, c):
        lo = (kind * ORDERS + c) * charge_ch
        row = kind * 8 + c
        return (
            sums_ref[lo : lo + charge_ch, :]
            + far_part_ref[lo : lo + charge_ch, :].astype(F32)
            + gaps[0] * sums_ref[wide + row : wide + row + 1, :]
            + gaps[1] * far_living[row : row + 1, :]
        )

    filtered(load, filt_ref, field_ref, charge_ch)
    neutral_ref[...] = (charge_ref[...] - mean) * live_row
    tx, ty, tz = axis_tables(own, place_of(meta_ref, 0, 0, sizes), sizes)
    lifted = dot(field_ref[...], plane_table(tx, ty).astype(BF16))
    potential = jnp.zeros((charge_ch, n), F32)
    for kind in range(2):
        for c in range(ORDERS):
            lo = (kind * ORDERS + c) * charge_ch
            potential = potential + tz[kind][c : c + 1, :] * lifted[lo : lo + charge_ch, :]
    pre_act = short_ref[...] + dot(jnp.transpose(potential).astype(BF16), w_long_ref[...])
    sig = sigmoid(pre_act)
    refined = features_ref[...].astype(F32) + pre_act * sig
    refined_ref[...] = refined
    sig_r = sigmoid(refined)
    live_rows = lax.broadcasted_iota(jnp.int32, (n, channels), 0) < count_ref[0]
    grad = (
        w_energy_ref[...]
        * (sig_r * (1.0 + refined * (1.0 - sig_r)))
        * (sig * (1.0 + pre_act * (1.0 - sig)))
    )
    grad_ref[...] = jnp.where(live_rows, grad, 0.0).astype(BF16)


def pair_force(sizes, meta_ref, places, strengths_ref, n):
    own_cols = columns(places[0][0], n)
    odd = lax.rem(meta_ref[0], 2)
    blocks = blocks_of(sizes)
    parts = [[], [], []]
    for first in range(0, n, 32):
        cols = [c[first : first + 32, :] for c in own_cols]
        acc = [jnp.zeros((32, n), F32) for _ in range(3)]
        for t, block in enumerate(blocks):
            half, m = block_place(sizes, odd, block)
            pos = places[half][m]
            offs = offsets(cols, [pos[a : a + 1, :] for a in range(3)], block)
            u, decays = pair_terms(offs, block, first)
            strength = jnp.zeros((32, n), F32)
            for b, g in enumerate(GAMMAS):
                part = strengths_ref[b * n + first : b * n + first + 32, t * n : (t + 1) * n]
                strength = strength + decays[b] * (g * u + 2.0) * part
            strength = strength * u
            for a in range(3):
                acc[a] = acc[a] + strength * offs[a]
        for a in range(3):
            parts[a].append(acc[a])
    return [
        (-2.0 * SCALE)
        * jnp.sum(jnp.transpose(jnp.concatenate(parts[a], axis=0)), axis=0, keepdims=True)
        for a in range(3)
    ]


def own_kernel(
    sizes,
    meta_ref,
    grad_ref,
    field_ref,
    places_ref,
    far_places_ref,
    xcat_ref,
    refined_ref,
    w_proj_ref,
    w_mix_ref,
    w_long_ref,
    w_energy_ref,
    updated_ref,
    energy_ref,
    force_ref,
    lifted_ref,
    strength_scr,
):
    n = grad_ref.shape[0]
    charge_ch = w_long_ref.shape[0]
    own = places_ref[0]
    refined = refined_ref[...]
    updated_ref[...] = refined.astype(BF16)
    energy_ref[...] = own[3:4, :] * jnp.sum(
        jnp.transpose(refined * sigmoid(refined) * w_energy_ref[...]), axis=0, keepdims=True
    )
    grad = grad_ref[...]
    adjoint = dot_nt(grad, w_mix_ref[...]).astype(BF16)
    rows, lifted = [], []
    for b in range(len(GAMMAS)):
        rows.append(dot_nt(adjoint, w_proj_ref[b]).astype(BF16))
        basis = dot(xcat_ref[0:n, :], w_proj_ref[b]).astype(BF16)
        lifted.append(dot(basis, w_mix_ref[...]).astype(BF16))
    lifted_ref[...] = jnp.concatenate(lifted, axis=0)
    strength_scr[...] = dot_nt(jnp.concatenate(rows, axis=0), xcat_ref[...])
    near = pair_force(sizes, meta_ref, (places_ref, far_places_ref), strength_scr, n)
    pull = dot_nt(w_long_ref[...], grad)
    tables = axis_tables(own, place_of(meta_ref, 0, 0, sizes), sizes)
    slope = field_slope(field_ref[...], tables, sizes, pull, charge_ch)
    force_ref[...] = jnp.concatenate([near[a] - slope[a] for a in range(3)], axis=0)


def pull_kernel(sizes, group, meta_ref, near_ref, places_ref, w_long_ref, sums_ref, part_ref):
    groups = near_ref.shape[0] // group

    def structure(g):
        left, right = [], []
        for j in range(group):
            m = g * group + j
            pos = places_ref[m]
            tx, ty, tz = axis_tables(pos, place_of(meta_ref, m, 0, sizes), sizes)
            left.append(spread(dot_nt(w_long_ref[...], near_ref[m]), tz))
            right.append(plane_table(tx, ty).astype(BF16))
        return dot_nt(jnp.concatenate(left, axis=1), jnp.concatenate(right, axis=1))

    sums_ref[...] = structure(0)

    def add_structure(g, _):
        sums_ref[...] += structure(g)
        return 0

    lax.fori_loop(1, groups, add_structure, 0)
    part_ref[...] = sums_ref[...].astype(BF16)


def react_kernel(
    sizes,
    meta_ref,
    near_ref,
    far_ref,
    places_ref,
    far_places_ref,
    lifted_ref,
    force_ref,
    out_ref,
    gcat_scr,
    strength_scr,
):
    n = lifted_ref.shape[1]
    halves = (near_ref, far_ref)
    odd = lax.rem(meta_ref[0], 2)
    for t, block in enumerate(blocks_of(sizes)):
        half, m = block_place(sizes, odd, block)
        gcat_scr[t * n : (t + 1) * n, :] = halves[half][m]
    strength_scr[...] = dot_nt(lifted_ref[...], gcat_scr[...])
    near = pair_force(sizes, meta_ref, (places_ref, far_places_ref), strength_scr, n)
    out_ref[...] = force_ref[...] + jnp.concatenate(near, axis=0)


def finish_kernel(
    sizes,
    meta_ref,
    sums_ref,
    far_part_ref,
    places_ref,
    neutral_ref,
    force_ref,
    filt_ref,
    out_ref,
    field_scr,
):
    charge_ch = neutral_ref.shape[0]

    def load(kind, c):
        lo = (kind * ORDERS + c) * charge_ch
        return sums_ref[lo : lo + charge_ch, :] + far_part_ref[lo : lo + charge_ch, :].astype(F32)

    filtered(load, filt_ref, field_scr, charge_ch)
    tables = axis_tables(places_ref[0], place_of(meta_ref, 0, 0, sizes), sizes)
    slope = field_slope(field_scr[...], tables, sizes, neutral_ref[...], charge_ch)
    for a in range(3):
        out_ref[a] = force_ref[a : a + 1, :] - slope[a]


def gather_cells(rows, sizes, beside):
    nx, ny, nz = sizes
    pairs = nx // 2

    def shifted(value, dx, dy):
        moves = []
        for i in range(nx):
            for j in range(ny):
                moves.append((i * ny + j, (i + 2 * dx) % nx * ny + (j + dy) % ny))
        return lax.ppermute(value, ("gx", "gy"), moves)

    value = rows[None]
    value = jnp.concatenate(
        [value]
        + [
            lax.ppermute(value, "gz", [(i, (i + s) % nz) for i in range(nz)])
            for s in range(1, nz)
        ],
        axis=0,
    )
    if pairs * ny <= 4:
        steps = [(dx, dy) for dx in range(pairs) for dy in range(ny)]
        value = jnp.concatenate(
            [value] + [shifted(value, dx, dy) for dx, dy in steps[1:]], axis=0
        )
    else:
        value = jnp.concatenate([value] + [shifted(value, 0, dy) for dy in range(1, ny)], axis=0)
        value = jnp.concatenate([value] + [shifted(value, dx, 0) for dx in range(1, pairs)], axis=0)
    value, *beside = lax.optimization_barrier((value, *beside))
    return value, *beside


def from_other_core(value):
    return lax.ppermute(value, "gx", [(i, i ^ 1) for i in range(lax.axis_size("gx"))])


def call(kernel, name, outs, scratch, smem, operands, kept, limit, flops):
    n_in = len(operands)
    first = n_in - kept
    operands = [
        pltpu.with_memory_space_constraint(o, pltpu.VMEM) if i >= first else o
        for i, o in enumerate(operands)
    ]
    specs = [pl.BlockSpec(memory_space=pltpu.SMEM)] * smem + [
        pl.BlockSpec(memory_space=pltpu.VMEM)
    ] * (n_in - smem)
    return pl.pallas_call(
        kernel,
        name=name,
        out_shape=outs,
        in_specs=specs,
        out_specs=[pl.BlockSpec(memory_space=pltpu.VMEM)] * len(outs),
        scratch_shapes=scratch,
        compiler_params=pltpu.CompilerParams(vmem_limit_bytes=limit),
        cost_estimate=pl.CostEstimate(flops=flops, bytes_accessed=2_000_000, transcendentals=0),
    )(*operands)


def shards(
    features,
    positions,
    counts,
    w_proj,
    w_mix,
    w_long,
    w_charge,
    charge_bias,
    w_energy,
    k_filter,
    k_index,
):
    own_rows = features[0, 0, 0]
    n, channels = own_rows.shape
    charge_ch = w_charge.shape[0]
    waves = k_index.shape[1]
    bases = w_proj.shape[0]
    sizes = tuple(lax.axis_size(a) for a in AXES)
    cells = sizes[0] * sizes[1] * sizes[2]
    half_cells = cells // 2
    group = max(g for g in (8, 4, 2, 1) if half_cells % g == 0)
    blocks = len(blocks_of(sizes))
    scale_long = 4.0 / math.sqrt(n * cells * waves)
    count = counts.reshape(1)
    meta = jnp.stack([lax.axis_index(a) for a in AXES]).astype(jnp.int32)
    shape = jax.ShapeDtypeStruct
    wide = 2 * ORDERS * charge_ch
    fits = cells <= 64
    limit = (24 if fits else 56) * 1024 * 1024
    held = pltpu.VMEM if fits else shape

    def run(kernel, name, outs, scratch, smem, operands, kept, flops):
        kept = kept if fits else 0
        return call(kernel, name, outs, scratch, smem, operands, kept, limit, flops)

    (packed,) = run(
        pack_kernel,
        "pack",
        [held((n + 16, channels), BF16)],
        [],
        1,
        [count, own_rows, positions.reshape(3, 1, n)],
        0,
        1000,
    )
    filt, bias, energy_row = run(
        lambda *refs: fold_kernel(scale_long, *refs),
        "fold_filter",
        [
            held((ORDERS, 4 * charge_ch, 128), F32),
            held((charge_ch, n), F32),
            held((1, channels), F32),
        ],
        [],
        0,
        [k_filter, k_index, charge_bias[None, :], w_energy[None, :]],
        0,
        1_000_000_000,
    )
    near, filt, bias, energy_row = gather_cells(packed, sizes, (filt, bias, energy_row))
    far = from_other_core(near)
    sums, part, places, charge = run(
        lambda *refs: charge_kernel(sizes, group, *refs),
        "charge_sums",
        [
            held((wide + 16, 256), F32),
            held((wide + 16 + charge_ch, 256), BF16),
            held((half_cells, 8, n), F32),
            held((charge_ch, n), F32),
        ],
        [pltpu.VMEM((half_cells, charge_ch, n), F32)],
        1,
        [meta, near, w_charge, bias],
        3,
        3_000_000_000,
    )
    far_part = from_other_core(part)
    short, far_places, xcat = run(
        lambda *refs: message_kernel(sizes, *refs),
        "message",
        [
            held((n, channels), F32),
            held((half_cells, 8, n), F32),
            held((blocks * n, channels), BF16),
        ],
        [pltpu.VMEM((bases * n, blocks * n), BF16)],
        1,
        [meta, near, far, places, w_proj, w_mix],
        5,
        3_000_000_000,
    )
    grad, refined, field, neutral = run(
        lambda *refs: cotangent_kernel(sizes, *refs),
        "cotangents",
        [
            held((n, channels), BF16),
            held((n, channels), F32),
            held((wide, 256), BF16),
            held((charge_ch, n), F32),
        ],
        [],
        2,
        [
            count,
            meta,
            sums,
            part,
            far_part,
            places,
            far_places,
            charge,
            short,
            own_rows,
            w_long,
            energy_row,
            filt,
        ],
        11,
        3_000_000_000,
    )
    updated, energy, force, lifted = run(
        lambda *refs: own_kernel(sizes, *refs),
        "own_terms",
        [
            shape((n, channels), BF16),
            shape((1, n), F32),
            held((3, n), F32),
            held((bases * n, channels), BF16),
        ],
        [pltpu.VMEM((bases * n, blocks * n), F32)],
        1,
        [
            meta,
            grad,
            field,
            places,
            far_places,
            xcat,
            refined,
            w_proj,
            w_mix,
            w_long,
            energy_row,
        ],
        10,
        4_000_000_000,
    )
    grad_near, force, lifted = gather_cells(grad, sizes, (force, lifted))
    grad_far = from_other_core(grad_near)
    back, back_part = run(
        lambda *refs: pull_kernel(sizes, group, *refs),
        "pull_sums",
        [held((wide, 256), F32), held((wide, 256), BF16)],
        [],
        1,
        [meta, grad_near, places, w_long],
        3,
        3_000_000_000,
    )
    far_back = from_other_core(back_part)
    (force,) = run(
        lambda *refs: react_kernel(sizes, *refs),
        "react",
        [held((3, n), F32)],
        [
            pltpu.VMEM((blocks * n, channels), BF16),
            pltpu.VMEM((bases * n, blocks * n), F32),
        ],
        1,
        [meta, grad_near, grad_far, places, far_places, lifted, force],
        6,
        3_000_000_000,
    )
    (forces,) = run(
        lambda *refs: finish_kernel(sizes, *refs),
        "finish",
        [shape((3, 1, n), F32)],
        [pltpu.VMEM((wide, 256), BF16)],
        1,
        [meta, back, far_back, places, neutral, force, filt],
        6,
        2_000_000_000,
    )
    return (
        updated[None, None, None],
        energy[None, None],
        forces.reshape(positions.shape),
    )


def solution(mesh):
    cell = ("gx", "gy", "gz")
    in_specs = (P(*cell, None, None), P(*cell, None, None), P(*cell)) + (P(),) * 8
    out_specs = (P(*cell, None, None), P(*cell, None), P(*cell, None, None))
    return jax.shard_map(shards, mesh=mesh, in_specs=in_specs, out_specs=out_specs, check_vma=False)
```

```python
import itertools
import math

import jax
import jax.numpy as jnp
import numpy as np
from jax import lax
from jax.experimental import pallas as pl
from jax.experimental.pallas import tpu as pltpu
from jax.sharding import PartitionSpec as P

CUTOFF = 0.9
SCALE = 1.0 / (CUTOFF * CUTOFF)
GAMMAS = (1.0, 3.0, 8.0, 20.0)
AXES = ("gx", "gy", "gz")
ORDERS = 7
NT = (((1,), (1,)), ((), ()))
F32 = jnp.float32
BF16 = jnp.bfloat16


def turn_series():
    nodes = np.cos(np.pi * (np.arange(200) + 0.5) / 200)
    r2 = (nodes + 1.0) / 8.0
    r = np.sqrt(r2)
    out = []
    for values in (np.cos(2 * np.pi * r), np.sin(2 * np.pi * r) / r):
        cheb = np.polynomial.chebyshev.Chebyshev.fit(r2, values, 6, domain=[0.0, 0.25])
        out.append([float(c) for c in cheb.convert(kind=np.polynomial.Polynomial).coef])
    return out


COS_SERIES, SIN_SERIES = turn_series()


def dot(a, b):
    return jnp.dot(a, b, preferred_element_type=F32)


def dot_nt(a, b):
    return lax.dot_general(a, b, NT, preferred_element_type=F32)


def sigmoid(v):
    return 1.0 / (1.0 + jnp.exp(-v))


def cos_sin(turns):
    r = turns - jnp.floor(turns + 0.5)
    r2 = r * r
    c = jnp.full_like(r2, COS_SERIES[-1])
    for coef in COS_SERIES[-2::-1]:
        c = c * r2 + coef
    s = jnp.full_like(r2, SIN_SERIES[-1])
    for coef in SIN_SERIES[-2::-1]:
        s = s * r2 + coef
    return c, s * r


def axis_tables(pos, anchor, sizes):
    order = lax.broadcasted_iota(jnp.int32, (8, pos.shape[1]), 0).astype(F32)
    tables = []
    for a in range(3):
        row = (pos[a : a + 1, :] + anchor[a]) * (1.0 / sizes[a])
        tables.append(cos_sin(order * row))
    return tables


def plane_table(first, second):
    rows = []
    for f in first:
        for s in second:
            for a in range(8):
                rows.append(f[a : a + 1, :] * s)
    return jnp.concatenate(rows, axis=0)


def derivative(table, size):
    order = lax.broadcasted_iota(jnp.int32, table[0].shape, 0).astype(F32) * (2.0 * math.pi / size)
    return (-order * table[1], order * table[0])


def spread(weights, third):
    rows = []
    for f in third:
        for c in range(ORDERS):
            rows.append((weights * f[c : c + 1, :]).astype(BF16))
    return jnp.concatenate(rows, axis=0)


def filtered(load, filt_ref, out_ref, charge_ch):
    shift = ORDERS * charge_ch
    for c in range(ORDERS):
        lo, hi = c * charge_ch, (c + 1) * charge_ch
        f0, gfb, fc, gfbc = (filt_ref[c, w * charge_ch : (w + 1) * charge_ch, :] for w in range(4))
        cos_part, sin_part = load(0, c), load(1, c)
        a_c, b_c = cos_part[:, 0:128], cos_part[:, 128:256]
        a_s, b_s = sin_part[:, 0:128], sin_part[:, 128:256]
        ra_c, rb_c, ra_s, rb_s = (pltpu.roll(v, 64, 1) for v in (a_c, b_c, a_s, b_s))
        out_ref[lo:hi, 0:128] = (f0 * a_c + gfbc * ra_s - fc * b_s + gfb * rb_c).astype(BF16)
        out_ref[lo:hi, 128:256] = (f0 * b_c - gfb * ra_c + fc * a_s + gfbc * rb_s).astype(BF16)
        out_ref[shift + lo : shift + hi, 0:128] = (
            f0 * a_s + fc * b_c - gfbc * ra_c + gfb * rb_s
        ).astype(BF16)
        out_ref[shift + lo : shift + hi, 128:256] = (
            f0 * b_s - fc * a_c - gfb * ra_s - gfbc * rb_c
        ).astype(BF16)


def field_slope(field, tables, sizes, weights, charge_ch):
    tx, ty, tz = tables
    n = tx[0].shape[1]
    planes = jnp.concatenate(
        [
            plane_table(derivative(tx, sizes[0]), ty).astype(BF16),
            plane_table(tx, derivative(ty, sizes[1])).astype(BF16),
            plane_table(tx, ty).astype(BF16),
        ],
        axis=1,
    )
    spread_field = dot(field, planes)
    slope_z = derivative(tz, sizes[2])
    total = [jnp.zeros((charge_ch, n), F32) for _ in range(3)]
    for kind in range(2):
        for c in range(ORDERS):
            lo = (kind * ORDERS + c) * charge_ch
            part = spread_field[lo : lo + charge_ch, :]
            zrow, drow = tz[kind][c : c + 1, :], slope_z[kind][c : c + 1, :]
            total[0] = total[0] + zrow * part[:, 0:n]
            total[1] = total[1] + zrow * part[:, n : 2 * n]
            total[2] = total[2] + drow * part[:, 2 * n : 3 * n]
    return [jnp.sum(t * weights, axis=0, keepdims=True) for t in total]


def place_of(meta_ref, m, half, sizes):
    nx, ny, nz = sizes
    dz = lax.rem(m, nz)
    dy = lax.rem(m // nz, ny)
    dx = m // (nz * ny)
    start = meta_ref[0] if half == 0 else meta_ref[0] + 1 - 2 * lax.rem(meta_ref[0], 2)
    cx = lax.rem(start - 2 * dx + nx, nx)
    cy = lax.rem(meta_ref[1] - dy + ny, ny)
    cz = lax.rem(meta_ref[2] - dz + nz, nz)
    return (cx.astype(F32), cy.astype(F32), cz.astype(F32))


def blocks_of(sizes):
    options = [((0, False), (1, True)) if n == 2 else ((0, False), (-1, False), (1, False)) for n in sizes]
    return list(itertools.product(*options))


def offsets(own_cols, others, block):
    result = []
    for a, (step, nearest) in enumerate(block):
        if nearest:
            d = others[a] - own_cols[a]
            d = d - jnp.where(d > 0.0, 1.0, -1.0)
        else:
            d = (others[a] + float(step)) - own_cols[a]
        result.append(d)
    return result


def pair_terms(offs, block, first_row):
    s = (offs[0] * offs[0] + offs[1] * offs[1] + offs[2] * offs[2]) * SCALE
    u = jnp.maximum(1.0 - s, 0.0)
    if all(step == 0 for step, _ in block):
        rows = lax.broadcasted_iota(jnp.int32, s.shape, 0) + first_row
        cols = lax.broadcasted_iota(jnp.int32, s.shape, 1)
        u = jnp.where(rows == cols, 0.0, u)
    e1 = jnp.exp(-s)
    e2 = e1 * e1
    e3 = e2 * e1
    e4 = e2 * e2
    e8 = e4 * e4
    e20 = e8 * e8 * e4
    return u, (e1, e3, e8, e20)


def columns(pos, n):
    return [jnp.transpose(jnp.broadcast_to(pos[a : a + 1, :], (n, n))) for a in range(3)]


def pack_kernel(count_ref, features_ref, positions_ref, out_ref):
    n, channels = features_ref.shape
    live_col = lax.broadcasted_iota(jnp.int32, (n, channels), 0) < count_ref[0]
    rows = features_ref[...].astype(F32)
    out_ref[0:n, :] = jnp.where(live_col, rows, 0.0).astype(BF16)
    pos = jnp.concatenate([positions_ref[a] for a in range(3)], axis=0)
    coarse = pos.astype(BF16).astype(F32)
    fine = pos - coarse
    living = (lax.broadcasted_iota(jnp.int32, (1, n), 1) < count_ref[0]).astype(F32)
    blank = jnp.zeros((4, n), F32)
    tail = jnp.concatenate([coarse, living, blank, fine, jnp.zeros((5, n), F32)], axis=0)
    out_ref[n : n + 16, :] = tail.astype(BF16)


def fold_kernel(scale, filter_ref, index_ref, bias_ref, energy_ref, out_ref, column_ref, row_ref):
    waves = filter_ref.shape[1]
    k = index_ref[...]
    positive = [jnp.where(k[a : a + 1, :] >= 0, 1.0, -1.0) for a in range(3)]
    sign_b = positive[0] * positive[1]
    sign_c = positive[0] * positive[2]
    size = jnp.abs(k)
    plane = size[0:1, :] * 8 + size[1:2, :]
    f = filter_ref[...] * scale
    stacked = jnp.concatenate([f, f * sign_b, f * sign_c, f * (sign_b * sign_c)], axis=0).astype(BF16)
    rows = lax.broadcasted_iota(jnp.int32, (64, waves), 0)
    charge_ch = filter_ref.shape[0]
    row_ref[...] = energy_ref[...]
    diagonal = lax.broadcasted_iota(jnp.int32, (charge_ch, charge_ch), 0) == (
        lax.broadcasted_iota(jnp.int32, (charge_ch, charge_ch), 1)
    )
    column = jnp.sum(jnp.where(diagonal, bias_ref[...], 0.0), axis=1, keepdims=True)
    column_ref[...] = jnp.broadcast_to(column, column_ref.shape)
    turn = jnp.where(lax.broadcasted_iota(jnp.int32, (charge_ch, 128), 1) < 64, -1.0, 1.0)
    for c in range(ORDERS):
        key = jnp.where(size[2:3, :] == c, plane, -1)
        chosen = jnp.where(rows == key, 1.0, 0.0).astype(BF16)
        part = dot_nt(stacked, jnp.concatenate([chosen, chosen], axis=0))
        for w in range(4):
            piece = part[w * charge_ch : (w + 1) * charge_ch, :]
            out_ref[c, w * charge_ch : (w + 1) * charge_ch, :] = piece * turn if w % 2 == 1 else piece


def block_place(sizes, odd, block):
    nx, ny, nz = sizes
    dy, dz = (-block[1][0]) % ny, (-block[2][0]) % nz
    if block[0][0] == 0:
        return 0, dy * nz + dz
    dx = odd * (nx // 2 - 1) if block[0][0] == 1 else (1 - odd) * (1 % (nx // 2))
    return 1, (dx * ny + dy) * nz + dz


def add_groups(structure, groups, sums_ref):
    if groups <= 4:
        total = structure(0)
        for g in range(1, groups):
            total = total + structure(g)
        sums_ref[...] = total
        return
    sums_ref[...] = structure(0)

    def add_structure(g, _):
        sums_ref[...] += structure(g)
        return 0

    lax.fori_loop(1, groups, add_structure, 0)


def charge_kernel(
    sizes,
    group,
    meta_ref,
    near_ref,
    w_charge_ref,
    bias_ref,
    sums_ref,
    part_ref,
    places_ref,
    charge_ref,
    *rest,
):
    *kept, charge_scr = rest
    charge_ch, channels = w_charge_ref.shape
    cells = near_ref.shape[0]
    n = near_ref.shape[1] - 16
    wide = 2 * ORDERS * charge_ch
    groups = cells // group
    w_charge = w_charge_ref[...]
    bias = bias_ref[...]

    def add_charges(g, carry):
        total, live_total = carry
        for j in range(group):
            m = g * group + j
            tail = near_ref[m, n : n + 16, :].astype(F32)
            pos = tail[0:8, :] + tail[8:16, :]
            places_ref[m] = pos
            live = pos[3:4, :]
            v = dot_nt(w_charge, near_ref[m, 0:n, :]) + bias
            q = v * sigmoid(v) * live
            charge_scr[m] = q
            total = total + q
            live_total = live_total + live
        return total, live_total

    start = (jnp.zeros((charge_ch, n), F32), jnp.zeros((1, n), F32))
    if groups <= 4:
        for g in range(groups):
            start = add_charges(g, start)
        total, live_total = start
    else:
        total, live_total = lax.fori_loop(0, groups, add_charges, start)
    mean = jnp.sum(total, axis=1, keepdims=True) / jnp.sum(live_total, axis=1, keepdims=True)
    mean = mean.astype(BF16).astype(F32)
    charge_ref[...] = charge_scr[0]

    def structure(g):
        left, right = [], []
        for j in range(group):
            m = g * group + j
            pos = places_ref[m]
            tx, ty, tz = axis_tables(pos, place_of(meta_ref, m, 0, sizes), sizes)
            live = pos[3:4, :]
            living = jnp.concatenate([tz[0] * live, tz[1] * live], axis=0).astype(BF16)
            plane = plane_table(tx, ty).astype(BF16)
            if kept:
                kept[0][m] = plane
                kept[1][m] = jnp.concatenate(tz, axis=0)
            left.append(
                jnp.concatenate([spread((charge_scr[m] - mean) * live, tz), living], axis=0)
            )
            right.append(plane)
        return dot_nt(jnp.concatenate(left, axis=1), jnp.concatenate(right, axis=1))

    add_groups(structure, groups, sums_ref)
    part_ref[0 : wide + 16, :] = sums_ref[...].astype(BF16)
    part_ref[wide + 16 : wide + 16 + charge_ch, :] = jnp.broadcast_to(mean, (charge_ch, 256)).astype(
        BF16
    )


def message_kernel(
    sizes,
    meta_ref,
    near_ref,
    far_ref,
    near_places_ref,
    w_proj_ref,
    w_mix_ref,
    short_ref,
    far_places_ref,
    xcat_ref,
    radial_scr,
):
    channels = near_ref.shape[2]
    n = near_ref.shape[1] - 16
    halves = (near_ref, far_ref)
    places = (near_places_ref, far_places_ref)

    def add_place(m, _):
        tail = far_ref[m, n : n + 16, :].astype(F32)
        far_places_ref[m] = tail[0:8, :] + tail[8:16, :]
        return 0

    lax.fori_loop(0, far_ref.shape[0], add_place, 0, unroll=4)
    odd = lax.rem(meta_ref[0], 2)
    own_cols = columns(near_places_ref[0], n)
    for t, block in enumerate(blocks_of(sizes)):
        half, m = block_place(sizes, odd, block)
        xcat_ref[t * n : (t + 1) * n, :] = halves[half][m, 0:n, :]
        pos = places[half][m]
        others = [pos[a : a + 1, :] for a in range(3)]
        for first in range(0, n, 32):
            cols = [c[first : first + 32, :] for c in own_cols]
            u, decays = pair_terms(offsets(cols, others, block), block, first)
            u2 = u * u
            for b in range(len(GAMMAS)):
                radial_scr[b * n + first : b * n + first + 32, t * n : (t + 1) * n] = (
                    decays[b] * u2
                ).astype(BF16)
    gathered = dot(radial_scr[...], xcat_ref[...]).astype(BF16)
    message = jnp.zeros((n, channels), F32)
    for b in range(len(GAMMAS)):
        message = message + dot(gathered[b * n : (b + 1) * n, :], w_proj_ref[b])
    short_ref[...] = dot(message.astype(BF16), w_mix_ref[...])


def cotangent_kernel(
    sizes,
    count_ref,
    meta_ref,
    sums_ref,
    part_ref,
    far_part_ref,
    places_ref,
    far_places_ref,
    charge_ref,
    short_ref,
    features_ref,
    w_long_ref,
    w_energy_ref,
    filt_ref,
    grad_ref,
    refined_ref,
    field_ref,
    neutral_ref,
):
    n, channels = features_ref.shape
    charge_ch = w_long_ref.shape[0]
    wide = 2 * ORDERS * charge_ch
    own = places_ref[0]
    live_row = own[3:4, :]

    lives = [jnp.sum(r[...], axis=0)[3:4, :] for r in (places_ref, far_places_ref)]
    lives = [jnp.sum(v, axis=1, keepdims=True) for v in lives]
    tail = wide + 16
    bases = [r[tail : tail + charge_ch, 0:1].astype(F32) for r in (part_ref, far_part_ref)]
    rests = [sums_ref[0:charge_ch, 0:1], far_part_ref[0:charge_ch, 0:1].astype(F32)]
    mean = (bases[0] * lives[0] + rests[0] + bases[1] * lives[1] + rests[1]) / (lives[0] + lives[1])
    gaps = [b - mean for b in bases]
    far_living = far_part_ref[wide : wide + 16, :].astype(F32)

    def load(kind, c):
        lo = (kind * ORDERS + c) * charge_ch
        row = kind * 8 + c
        return (
            sums_ref[lo : lo + charge_ch, :]
            + far_part_ref[lo : lo + charge_ch, :].astype(F32)
            + gaps[0] * sums_ref[wide + row : wide + row + 1, :]
            + gaps[1] * far_living[row : row + 1, :]
        )

    filtered(load, filt_ref, field_ref, charge_ch)
    neutral_ref[...] = (charge_ref[...] - mean) * live_row
    tx, ty, tz = axis_tables(own, place_of(meta_ref, 0, 0, sizes), sizes)
    lifted = dot(field_ref[...], plane_table(tx, ty).astype(BF16))
    potential = jnp.zeros((charge_ch, n), F32)
    for kind in range(2):
        for c in range(ORDERS):
            lo = (kind * ORDERS + c) * charge_ch
            potential = potential + tz[kind][c : c + 1, :] * lifted[lo : lo + charge_ch, :]
    pre_act = short_ref[...] + dot(jnp.transpose(potential).astype(BF16), w_long_ref[...])
    sig = sigmoid(pre_act)
    refined = features_ref[...].astype(F32) + pre_act * sig
    refined_ref[...] = refined
    sig_r = sigmoid(refined)
    live_rows = lax.broadcasted_iota(jnp.int32, (n, channels), 0) < count_ref[0]
    grad = (
        w_energy_ref[...]
        * (sig_r * (1.0 + refined * (1.0 - sig_r)))
        * (sig * (1.0 + pre_act * (1.0 - sig)))
    )
    grad_ref[...] = jnp.where(live_rows, grad, 0.0).astype(BF16)


def pair_force(sizes, meta_ref, places, strengths_ref, n, slopes_to=None, slopes_from=None):
    own_cols = columns(places[0][0], n)
    odd = lax.rem(meta_ref[0], 2)
    blocks = blocks_of(sizes)
    parts = [[], [], []]
    for first in range(0, n, 32):
        cols = [c[first : first + 32, :] for c in own_cols]
        acc = [jnp.zeros((32, n), F32) for _ in range(3)]
        for t, block in enumerate(blocks):
            half, m = block_place(sizes, odd, block)
            pos = places[half][m]
            offs = offsets(cols, [pos[a : a + 1, :] for a in range(3)], block)
            if slopes_from is None:
                u, decays = pair_terms(offs, block, first)
            strength = jnp.zeros((32, n), F32)
            for b, g in enumerate(GAMMAS):
                lo = b * n + first
                part = strengths_ref[lo : lo + 32, t * n : (t + 1) * n]
                if slopes_from is None:
                    slope = decays[b] * (g * u + 2.0) * u
                else:
                    slope = slopes_from[lo : lo + 32, t * n : (t + 1) * n]
                if slopes_to is not None:
                    slopes_to[lo : lo + 32, t * n : (t + 1) * n] = slope
                strength = strength + slope * part
            for a in range(3):
                acc[a] = acc[a] + strength * offs[a]
        for a in range(3):
            parts[a].append(acc[a])
    return [
        (-2.0 * SCALE)
        * jnp.sum(jnp.transpose(jnp.concatenate(parts[a], axis=0)), axis=0, keepdims=True)
        for a in range(3)
    ]


def own_kernel(
    sizes,
    meta_ref,
    grad_ref,
    field_ref,
    places_ref,
    far_places_ref,
    xcat_ref,
    refined_ref,
    w_proj_ref,
    w_mix_ref,
    w_long_ref,
    w_energy_ref,
    updated_ref,
    energy_ref,
    force_ref,
    lifted_ref,
    *rest,
):
    *slopes, strength_scr = rest
    n = grad_ref.shape[0]
    charge_ch = w_long_ref.shape[0]
    own = places_ref[0]
    refined = refined_ref[...]
    updated_ref[...] = refined.astype(BF16)
    energy_ref[...] = own[3:4, :] * jnp.sum(
        jnp.transpose(refined * sigmoid(refined) * w_energy_ref[...]), axis=0, keepdims=True
    )
    grad = grad_ref[...]
    adjoint = dot_nt(grad, w_mix_ref[...]).astype(BF16)
    rows, lifted = [], []
    for b in range(len(GAMMAS)):
        rows.append(dot_nt(adjoint, w_proj_ref[b]).astype(BF16))
        basis = dot(xcat_ref[0:n, :], w_proj_ref[b]).astype(BF16)
        lifted.append(dot(basis, w_mix_ref[...]).astype(BF16))
    lifted_ref[...] = jnp.concatenate(lifted, axis=0)
    strength_scr[...] = dot_nt(jnp.concatenate(rows, axis=0), xcat_ref[...])
    places = (places_ref, far_places_ref)
    near = pair_force(sizes, meta_ref, places, strength_scr, n, slopes[0] if slopes else None)
    pull = dot_nt(w_long_ref[...], grad)
    tables = axis_tables(own, place_of(meta_ref, 0, 0, sizes), sizes)
    slope = field_slope(field_ref[...], tables, sizes, pull, charge_ch)
    force_ref[...] = jnp.concatenate([near[a] - slope[a] for a in range(3)], axis=0)


def pull_kernel(sizes, group, meta_ref, near_ref, places_ref, w_long_ref, *rest):
    *kept, sums_ref, part_ref = rest
    n = near_ref.shape[1]
    groups = near_ref.shape[0] // group

    def structure(g):
        left, right = [], []
        rows = jnp.concatenate([near_ref[g * group + j] for j in range(group)], axis=0)
        pulls = dot_nt(w_long_ref[...], rows)
        for j in range(group):
            m = g * group + j
            if kept:
                tz = (kept[1][m, 0:8, :], kept[1][m, 8:16, :])
                right.append(kept[0][m])
            else:
                pos = places_ref[m]
                tx, ty, tz = axis_tables(pos, place_of(meta_ref, m, 0, sizes), sizes)
                right.append(plane_table(tx, ty).astype(BF16))
            left.append(spread(pulls[:, j * n : (j + 1) * n], tz))
        return dot_nt(jnp.concatenate(left, axis=1), jnp.concatenate(right, axis=1))

    add_groups(structure, groups, sums_ref)
    part_ref[...] = sums_ref[...].astype(BF16)


def react_kernel(
    sizes,
    meta_ref,
    near_ref,
    far_ref,
    places_ref,
    far_places_ref,
    lifted_ref,
    force_ref,
    *rest,
):
    *slopes, out_ref, gcat_scr, strength_scr = rest
    n = lifted_ref.shape[1]
    halves = (near_ref, far_ref)
    odd = lax.rem(meta_ref[0], 2)
    for t, block in enumerate(blocks_of(sizes)):
        half, m = block_place(sizes, odd, block)
        gcat_scr[t * n : (t + 1) * n, :] = halves[half][m]
    strength_scr[...] = dot_nt(lifted_ref[...], gcat_scr[...])
    places = (places_ref, far_places_ref)
    near = pair_force(sizes, meta_ref, places, strength_scr, n, None, slopes[0] if slopes else None)
    out_ref[...] = force_ref[...] + jnp.concatenate(near, axis=0)


def finish_kernel(
    sizes,
    meta_ref,
    sums_ref,
    far_part_ref,
    places_ref,
    neutral_ref,
    force_ref,
    filt_ref,
    out_ref,
    field_scr,
):
    charge_ch = neutral_ref.shape[0]

    def load(kind, c):
        lo = (kind * ORDERS + c) * charge_ch
        return sums_ref[lo : lo + charge_ch, :] + far_part_ref[lo : lo + charge_ch, :].astype(F32)

    filtered(load, filt_ref, field_scr, charge_ch)
    tables = axis_tables(places_ref[0], place_of(meta_ref, 0, 0, sizes), sizes)
    slope = field_slope(field_scr[...], tables, sizes, neutral_ref[...], charge_ch)
    for a in range(3):
        out_ref[a] = force_ref[a : a + 1, :] - slope[a]


def gather_line(rows, nz):
    value = rows[None]
    return jnp.concatenate(
        [value]
        + [
            lax.ppermute(value, "gz", [(i, (i + s) % nz) for i in range(nz)])
            for s in range(1, nz)
        ],
        axis=0,
    )


def gather_cells(value, sizes, beside):
    nx, ny, nz = sizes
    pairs = nx // 2

    def shifted(value, dx, dy):
        moves = []
        for i in range(nx):
            for j in range(ny):
                moves.append((i * ny + j, (i + 2 * dx) % nx * ny + (j + dy) % ny))
        return lax.ppermute(value, ("gx", "gy"), moves)

    if pairs * ny <= 4:
        steps = [(dx, dy) for dx in range(pairs) for dy in range(ny)]
        value = jnp.concatenate(
            [value] + [shifted(value, dx, dy) for dx, dy in steps[1:]], axis=0
        )
    else:
        value = jnp.concatenate([value] + [shifted(value, 0, dy) for dy in range(1, ny)], axis=0)
        value = jnp.concatenate([value] + [shifted(value, dx, 0) for dx in range(1, pairs)], axis=0)
    value, *beside = lax.optimization_barrier((value, *beside))
    return value, *beside


def from_other_core(value):
    return lax.ppermute(value, "gx", [(i, i ^ 1) for i in range(lax.axis_size("gx"))])


def call(kernel, name, outs, scratch, smem, operands, kept, limit, flops):
    n_in = len(operands)
    first = n_in - kept
    operands = [
        pltpu.with_memory_space_constraint(o, pltpu.VMEM) if i >= first else o
        for i, o in enumerate(operands)
    ]
    specs = [pl.BlockSpec(memory_space=pltpu.SMEM)] * smem + [
        pl.BlockSpec(memory_space=pltpu.VMEM)
    ] * (n_in - smem)
    return pl.pallas_call(
        kernel,
        name=name,
        out_shape=outs,
        in_specs=specs,
        out_specs=[pl.BlockSpec(memory_space=pltpu.VMEM)] * len(outs),
        scratch_shapes=scratch,
        compiler_params=pltpu.CompilerParams(vmem_limit_bytes=limit),
        cost_estimate=pl.CostEstimate(flops=flops, bytes_accessed=2_000_000, transcendentals=0),
    )(*operands)


def shards(
    features,
    positions,
    counts,
    w_proj,
    w_mix,
    w_long,
    w_charge,
    charge_bias,
    w_energy,
    k_filter,
    k_index,
):
    own_rows = features[0, 0, 0]
    n, channels = own_rows.shape
    charge_ch = w_charge.shape[0]
    waves = k_index.shape[1]
    bases = w_proj.shape[0]
    sizes = tuple(lax.axis_size(a) for a in AXES)
    cells = sizes[0] * sizes[1] * sizes[2]
    half_cells = cells // 2
    group = max(g for g in (8, 4, 2, 1) if half_cells % g == 0)
    blocks = len(blocks_of(sizes))
    scale_long = 4.0 / math.sqrt(n * cells * waves)
    count = counts.reshape(1)
    meta = jnp.stack([lax.axis_index(a) for a in AXES]).astype(jnp.int32)
    shape = jax.ShapeDtypeStruct
    wide = 2 * ORDERS * charge_ch
    fits = cells <= 64
    limit = (24 if fits else 56) * 1024 * 1024
    held = pltpu.VMEM if fits else shape

    def run(kernel, name, outs, scratch, smem, operands, kept, flops):
        kept = kept if fits else 0
        return call(kernel, name, outs, scratch, smem, operands, kept, limit, flops)

    (packed,) = run(
        pack_kernel,
        "pack",
        [held((n + 16, channels), BF16)],
        [],
        1,
        [count, own_rows, positions.reshape(3, 1, n)],
        0,
        1000,
    )
    line, k_filter, k_index = lax.optimization_barrier((gather_line(packed, sizes[2]), k_filter, k_index))
    filt, bias, energy_row = run(
        lambda *refs: fold_kernel(scale_long, *refs),
        "fold_filter",
        [
            held((ORDERS, 4 * charge_ch, 128), F32),
            held((charge_ch, n), F32),
            held((1, channels), F32),
        ],
        [],
        0,
        [k_filter, k_index, charge_bias[None, :], w_energy[None, :]],
        0,
        1_000_000_000,
    )
    near, filt, bias, energy_row = gather_cells(line, sizes, (filt, bias, energy_row))
    far = from_other_core(near)
    sums, part, places, charge, *kept = run(
        lambda *refs: charge_kernel(sizes, group, *refs),
        "charge_sums",
        [
            held((wide + 16, 256), F32),
            held((wide + 16 + charge_ch, 256), BF16),
            held((half_cells, 8, n), F32),
            held((charge_ch, n), F32),
        ]
        + ([held((half_cells, 256, n), BF16), held((half_cells, 16, n), F32)] if fits else []),
        [pltpu.VMEM((half_cells, charge_ch, n), F32)],
        1,
        [meta, near, w_charge, bias],
        3,
        3_000_000_000,
    )
    far_part = from_other_core(part)
    short, far_places, xcat = run(
        lambda *refs: message_kernel(sizes, *refs),
        "message",
        [
            held((n, channels), F32),
            held((half_cells, 8, n), F32),
            held((blocks * n, channels), BF16),
        ],
        [pltpu.VMEM((bases * n, blocks * n), BF16)],
        1,
        [meta, near, far, places, w_proj, w_mix],
        5,
        3_000_000_000,
    )
    grad, refined, field, neutral = run(
        lambda *refs: cotangent_kernel(sizes, *refs),
        "cotangents",
        [
            held((n, channels), BF16),
            held((n, channels), F32),
            held((wide, 256), BF16),
            held((charge_ch, n), F32),
        ],
        [],
        2,
        [
            count,
            meta,
            sums,
            part,
            far_part,
            places,
            far_places,
            charge,
            short,
            own_rows,
            w_long,
            energy_row,
            filt,
        ],
        11,
        3_000_000_000,
    )
    grad_line, grad = lax.optimization_barrier((gather_line(grad, sizes[2]), grad))
    updated, energy, force, lifted, *slopes = run(
        lambda *refs: own_kernel(sizes, *refs),
        "own_terms",
        [
            shape((n, channels), BF16),
            shape((1, n), F32),
            held((3, n), F32),
            held((bases * n, channels), BF16),
        ]
        + ([held((bases * n, blocks * n), F32)] if fits else []),
        [pltpu.VMEM((bases * n, blocks * n), F32)],
        1,
        [
            meta,
            grad,
            field,
            places,
            far_places,
            xcat,
            refined,
            w_proj,
            w_mix,
            w_long,
            energy_row,
        ],
        10,
        4_000_000_000,
    )
    grad_near, force, lifted = gather_cells(grad_line, sizes, (force, lifted))
    grad_far = from_other_core(grad_near)
    back, back_part = run(
        lambda *refs: pull_kernel(sizes, group, *refs),
        "pull_sums",
        [held((wide, 256), F32), held((wide, 256), BF16)],
        [],
        1,
        [meta, grad_near, places, w_long, *kept],
        3 + len(kept),
        3_000_000_000,
    )
    far_back = from_other_core(back_part)
    (force,) = run(
        lambda *refs: react_kernel(sizes, *refs),
        "react",
        [held((3, n), F32)],
        [
            pltpu.VMEM((blocks * n, channels), BF16),
            pltpu.VMEM((bases * n, blocks * n), F32),
        ],
        1,
        [meta, grad_near, grad_far, places, far_places, lifted, force, *slopes],
        6 + len(slopes),
        3_000_000_000,
    )
    (forces,) = run(
        lambda *refs: finish_kernel(sizes, *refs),
        "finish",
        [shape((3, 1, n), F32)],
        [pltpu.VMEM((wide, 256), BF16)],
        1,
        [meta, back, far_back, places, neutral, force, filt],
        6,
        2_000_000_000,
    )
    return (
        updated[None, None, None],
        energy[None, None],
        forces.reshape(positions.shape),
    )


def solution(mesh):
    cell = ("gx", "gy", "gz")
    in_specs = (P(*cell, None, None), P(*cell, None, None), P(*cell)) + (P(),) * 8
    out_specs = (P(*cell, None, None), P(*cell, None), P(*cell, None, None))
    return jax.shard_map(shards, mesh=mesh, in_specs=in_specs, out_specs=out_specs, check_vma=False)
```

```python
import itertools
import math

import jax
import jax.numpy as jnp
import numpy as np
from jax import lax
from jax.experimental import pallas as pl
from jax.experimental.pallas import tpu as pltpu
from jax.sharding import PartitionSpec as P

CUTOFF = 0.9
SCALE = 1.0 / (CUTOFF * CUTOFF)
GAMMAS = (1.0, 3.0, 8.0, 20.0)
AXES = ("gx", "gy", "gz")
ORDERS = 7
NT = (((1,), (1,)), ((), ()))
F32 = jnp.float32
BF16 = jnp.bfloat16


def turn_series():
    nodes = np.cos(np.pi * (np.arange(200) + 0.5) / 200)
    r2 = (nodes + 1.0) / 8.0
    r = np.sqrt(r2)
    out = []
    for values in (np.cos(2 * np.pi * r), np.sin(2 * np.pi * r) / r):
        cheb = np.polynomial.chebyshev.Chebyshev.fit(r2, values, 6, domain=[0.0, 0.25])
        out.append([float(c) for c in cheb.convert(kind=np.polynomial.Polynomial).coef])
    return out


COS_SERIES, SIN_SERIES = turn_series()


def dot(a, b):
    return jnp.dot(a, b, preferred_element_type=F32)


def dot_nt(a, b):
    return lax.dot_general(a, b, NT, preferred_element_type=F32)


def sigmoid(v):
    return 1.0 / (1.0 + jnp.exp(-v))


def cos_sin(turns):
    r = turns - jnp.floor(turns + 0.5)
    r2 = r * r
    c = jnp.full_like(r2, COS_SERIES[-1])
    for coef in COS_SERIES[-2::-1]:
        c = c * r2 + coef
    s = jnp.full_like(r2, SIN_SERIES[-1])
    for coef in SIN_SERIES[-2::-1]:
        s = s * r2 + coef
    return c, s * r


def axis_tables(pos, anchor, sizes):
    order = lax.broadcasted_iota(jnp.int32, (8, pos.shape[1]), 0).astype(F32)
    tables = []
    for a in range(3):
        row = (pos[a : a + 1, :] + anchor[a]) * (1.0 / sizes[a])
        tables.append(cos_sin(order * row))
    return tables


def plane_table(first, second):
    rows = []
    for f in first:
        for s in second:
            for a in range(8):
                rows.append(f[a : a + 1, :] * s)
    return jnp.concatenate(rows, axis=0)


def derivative(table, size):
    order = lax.broadcasted_iota(jnp.int32, table[0].shape, 0).astype(F32) * (2.0 * math.pi / size)
    return (-order * table[1], order * table[0])


def spread(weights, third):
    rows = []
    for f in third:
        for c in range(ORDERS):
            rows.append((weights * f[c : c + 1, :]).astype(BF16))
    return jnp.concatenate(rows, axis=0)


def filtered(load, filt_ref, out_ref, charge_ch):
    shift = ORDERS * charge_ch
    for c in range(ORDERS):
        lo, hi = c * charge_ch, (c + 1) * charge_ch
        f0, gfb, fc, gfbc = (filt_ref[c, w * charge_ch : (w + 1) * charge_ch, :] for w in range(4))
        cos_part, sin_part = load(0, c), load(1, c)
        a_c, b_c = cos_part[:, 0:128], cos_part[:, 128:256]
        a_s, b_s = sin_part[:, 0:128], sin_part[:, 128:256]
        ra_c, rb_c, ra_s, rb_s = (pltpu.roll(v, 64, 1) for v in (a_c, b_c, a_s, b_s))
        out_ref[lo:hi, 0:128] = (f0 * a_c + gfbc * ra_s - fc * b_s + gfb * rb_c).astype(BF16)
        out_ref[lo:hi, 128:256] = (f0 * b_c - gfb * ra_c + fc * a_s + gfbc * rb_s).astype(BF16)
        out_ref[shift + lo : shift + hi, 0:128] = (
            f0 * a_s + fc * b_c - gfbc * ra_c + gfb * rb_s
        ).astype(BF16)
        out_ref[shift + lo : shift + hi, 128:256] = (
            f0 * b_s - fc * a_c - gfb * ra_s - gfbc * rb_c
        ).astype(BF16)


def slope_planes(tables, sizes):
    tx, ty, _ = tables
    return jnp.concatenate(
        [
            plane_table(derivative(tx, sizes[0]), ty).astype(BF16),
            plane_table(tx, derivative(ty, sizes[1])).astype(BF16),
            plane_table(tx, ty).astype(BF16),
        ],
        axis=1,
    )


def field_slope(field, planes, tz, sizes, weights, charge_ch):
    n = tz[0].shape[1]
    spread_field = dot(field, planes)
    slope_z = derivative(tz, sizes[2])
    total = [jnp.zeros((charge_ch, n), F32) for _ in range(3)]
    for kind in range(2):
        for c in range(ORDERS):
            lo = (kind * ORDERS + c) * charge_ch
            part = spread_field[lo : lo + charge_ch, :]
            zrow, drow = tz[kind][c : c + 1, :], slope_z[kind][c : c + 1, :]
            total[0] = total[0] + zrow * part[:, 0:n]
            total[1] = total[1] + zrow * part[:, n : 2 * n]
            total[2] = total[2] + drow * part[:, 2 * n : 3 * n]
    return [jnp.sum(t * weights, axis=0, keepdims=True) for t in total]


def place_of(meta_ref, m, half, sizes):
    nx, ny, nz = sizes
    dz = lax.rem(m, nz)
    dy = lax.rem(m // nz, ny)
    dx = m // (nz * ny)
    start = meta_ref[0] if half == 0 else meta_ref[0] + 1 - 2 * lax.rem(meta_ref[0], 2)
    cx = lax.rem(start - 2 * dx + nx, nx)
    cy = lax.rem(meta_ref[1] - dy + ny, ny)
    cz = lax.rem(meta_ref[2] - dz + nz, nz)
    return (cx.astype(F32), cy.astype(F32), cz.astype(F32))


def blocks_of(sizes):
    options = [((0, False), (1, True)) if n == 2 else ((0, False), (-1, False), (1, False)) for n in sizes]
    return list(itertools.product(*options))


def offsets(own_cols, others, block):
    result = []
    for a, (step, nearest) in enumerate(block):
        if nearest:
            d = others[a] - own_cols[a]
            d = d - jnp.where(d > 0.0, 1.0, -1.0)
        else:
            d = (others[a] + float(step)) - own_cols[a]
        result.append(d)
    return result


def pair_terms(offs, block, first_row):
    s = (offs[0] * offs[0] + offs[1] * offs[1] + offs[2] * offs[2]) * SCALE
    u = jnp.maximum(1.0 - s, 0.0)
    if all(step == 0 for step, _ in block):
        rows = lax.broadcasted_iota(jnp.int32, s.shape, 0) + first_row
        cols = lax.broadcasted_iota(jnp.int32, s.shape, 1)
        u = jnp.where(rows == cols, 0.0, u)
    e1 = jnp.exp(-s)
    e2 = e1 * e1
    e3 = e2 * e1
    e4 = e2 * e2
    e8 = e4 * e4
    e20 = e8 * e8 * e4
    return u, (e1, e3, e8, e20)


def columns(pos, n):
    return [jnp.transpose(jnp.broadcast_to(pos[a : a + 1, :], (n, n))) for a in range(3)]


def fetch(sources, places, sems):
    copies = [pltpu.make_async_copy(s, p, sems.at[i]) for i, (s, p) in enumerate(zip(sources, places))]
    for c in copies:
        c.start()
    for c in copies:
        c.wait()


def pack_kernel(count_ref, features_hbm, positions_hbm, out_ref, features_ref, positions_ref, sems):
    fetch((features_hbm, positions_hbm), (features_ref, positions_ref), sems)
    n, channels = features_ref.shape
    live_col = lax.broadcasted_iota(jnp.int32, (n, channels), 0) < count_ref[0]
    rows = features_ref[...].astype(F32)
    out_ref[0:n, :] = jnp.where(live_col, rows, 0.0).astype(BF16)
    pos = jnp.concatenate([positions_ref[a] for a in range(3)], axis=0)
    coarse = pos.astype(BF16).astype(F32)
    fine = pos - coarse
    living = (lax.broadcasted_iota(jnp.int32, (1, n), 1) < count_ref[0]).astype(F32)
    blank = jnp.zeros((4, n), F32)
    tail = jnp.concatenate([coarse, living, blank, fine, jnp.zeros((5, n), F32)], axis=0)
    out_ref[n : n + 16, :] = tail.astype(BF16)


def fold_kernel(
    scale,
    filter_hbm,
    index_hbm,
    bias_hbm,
    energy_hbm,
    proj_hbm,
    mix_hbm,
    out_ref,
    column_ref,
    row_ref,
    mixed_ref,
    filter_ref,
    index_ref,
    bias_ref,
    energy_ref,
    proj_ref,
    mix_ref,
    sems,
):
    fetch(
        (filter_hbm, index_hbm, bias_hbm, energy_hbm, proj_hbm, mix_hbm),
        (filter_ref, index_ref, bias_ref, energy_ref, proj_ref, mix_ref),
        sems,
    )
    waves = filter_ref.shape[1]
    charge_ch = filter_ref.shape[0]
    row_ref[...] = energy_ref[...]
    diagonal = lax.broadcasted_iota(jnp.int32, (charge_ch, charge_ch), 0) == (
        lax.broadcasted_iota(jnp.int32, (charge_ch, charge_ch), 1)
    )
    column = jnp.sum(jnp.where(diagonal, bias_ref[...], 0.0), axis=1, keepdims=True)
    column_ref[...] = jnp.broadcast_to(column, column_ref.shape)
    mixed_ref[...] = dot(proj_ref[...], mix_ref[...]).astype(BF16)
    k = index_ref[...]
    positive = [jnp.where(k[a : a + 1, :] >= 0, 1.0, -1.0) for a in range(3)]
    sign_b = positive[0] * positive[1]
    sign_c = positive[0] * positive[2]
    size = jnp.abs(k)
    key = size[2:3, :] * 64 + size[0:1, :] * 8 + size[1:2, :]
    f = filter_ref[...] * scale
    stacked = jnp.concatenate([f, f * sign_b, f * sign_c, f * (sign_b * sign_c)], axis=0).astype(BF16)
    rows = lax.broadcasted_iota(jnp.int32, (ORDERS * 64, waves), 0)
    parts = dot_nt(stacked, jnp.where(rows == key, 1.0, 0.0).astype(BF16))
    turn = jnp.where(lax.broadcasted_iota(jnp.int32, (charge_ch, 128), 1) < 64, -1.0, 1.0)
    for c in range(ORDERS):
        part = parts[:, c * 64 : (c + 1) * 64]
        part = jnp.concatenate([part, part], axis=1)
        for w in range(4):
            piece = part[w * charge_ch : (w + 1) * charge_ch, :]
            out_ref[c, w * charge_ch : (w + 1) * charge_ch, :] = piece * turn if w % 2 == 1 else piece


def block_place(sizes, odd, block):
    nx, ny, nz = sizes
    dy, dz = (-block[1][0]) % ny, (-block[2][0]) % nz
    if block[0][0] == 0:
        return 0, dy * nz + dz
    dx = odd * (nx // 2 - 1) if block[0][0] == 1 else (1 - odd) * (1 % (nx // 2))
    return 1, (dx * ny + dy) * nz + dz


def add_groups(structure, groups, sums_ref):
    if groups <= 4:
        total = structure(0)
        for g in range(1, groups):
            total = total + structure(g)
        sums_ref[...] = total
        return
    sums_ref[...] = structure(0)

    def add_structure(g, _):
        sums_ref[...] += structure(g)
        return 0

    lax.fori_loop(1, groups, add_structure, 0)


def charge_kernel(
    sizes,
    group,
    meta_ref,
    near_ref,
    w_charge_ref,
    bias_ref,
    sums_ref,
    part_ref,
    places_ref,
    charge_ref,
    *rest,
):
    *kept, charge_scr = rest
    charge_ch, channels = w_charge_ref.shape
    cells = near_ref.shape[0]
    n = near_ref.shape[1] - 16
    wide = 2 * ORDERS * charge_ch
    groups = cells // group
    w_charge = w_charge_ref[...]
    bias = bias_ref[...]

    def add_charges(g, carry):
        total, live_total = carry
        for j in range(group):
            m = g * group + j
            tail = near_ref[m, n : n + 16, :].astype(F32)
            pos = tail[0:8, :] + tail[8:16, :]
            places_ref[m] = pos
            live = pos[3:4, :]
            v = dot_nt(w_charge, near_ref[m, 0:n, :]) + bias
            q = v * sigmoid(v) * live
            charge_scr[m] = q
            total = total + q
            live_total = live_total + live
        return total, live_total

    start = (jnp.zeros((charge_ch, n), F32), jnp.zeros((1, n), F32))
    if groups <= 4:
        for g in range(groups):
            start = add_charges(g, start)
        total, live_total = start
    else:
        total, live_total = lax.fori_loop(0, groups, add_charges, start)
    mean = jnp.sum(total, axis=1, keepdims=True) / jnp.sum(live_total, axis=1, keepdims=True)
    mean = mean.astype(BF16).astype(F32)
    charge_ref[...] = charge_scr[0]

    def structure(g):
        left, right = [], []
        for j in range(group):
            m = g * group + j
            pos = places_ref[m]
            tx, ty, tz = axis_tables(pos, place_of(meta_ref, m, 0, sizes), sizes)
            live = pos[3:4, :]
            living = jnp.concatenate([tz[0] * live, tz[1] * live], axis=0).astype(BF16)
            plane = plane_table(tx, ty).astype(BF16)
            if kept:
                kept[0][m] = plane
                kept[1][m] = jnp.concatenate(tz, axis=0)
            left.append(
                jnp.concatenate([spread((charge_scr[m] - mean) * live, tz), living], axis=0)
            )
            right.append(plane)
        return dot_nt(jnp.concatenate(left, axis=1), jnp.concatenate(right, axis=1))

    add_groups(structure, groups, sums_ref)
    part_ref[0 : wide + 16, :] = sums_ref[...].astype(BF16)
    part_ref[wide + 16 : wide + 16 + charge_ch, :] = jnp.broadcast_to(mean, (charge_ch, 256)).astype(
        BF16
    )


def message_kernel(
    sizes,
    meta_ref,
    near_ref,
    far_ref,
    near_places_ref,
    mixed_ref,
    short_ref,
    far_places_ref,
    xcat_ref,
    radial_scr,
):
    n = near_ref.shape[1] - 16
    halves = (near_ref, far_ref)
    places = (near_places_ref, far_places_ref)

    def add_place(m, _):
        tail = far_ref[m, n : n + 16, :].astype(F32)
        far_places_ref[m] = tail[0:8, :] + tail[8:16, :]
        return 0

    lax.fori_loop(0, far_ref.shape[0], add_place, 0, unroll=4)
    odd = lax.rem(meta_ref[0], 2)
    own_cols = columns(near_places_ref[0], n)
    for t, block in enumerate(blocks_of(sizes)):
        half, m = block_place(sizes, odd, block)
        xcat_ref[t * n : (t + 1) * n, :] = halves[half][m, 0:n, :]
        pos = places[half][m]
        others = [pos[a : a + 1, :] for a in range(3)]
        for first in range(0, n, 32):
            cols = [c[first : first + 32, :] for c in own_cols]
            u, decays = pair_terms(offsets(cols, others, block), block, first)
            u2 = u * u
            for b in range(len(GAMMAS)):
                radial_scr[b * n + first : b * n + first + 32, t * n : (t + 1) * n] = (
                    decays[b] * u2
                ).astype(BF16)
    gathered = dot(radial_scr[...], xcat_ref[...]).astype(BF16)
    gathered = jnp.concatenate([gathered[b * n : (b + 1) * n, :] for b in range(len(GAMMAS))], axis=1)
    short_ref[...] = dot(gathered, mixed_ref[...])


def cotangent_kernel(
    sizes,
    count_ref,
    meta_ref,
    sums_ref,
    part_ref,
    far_part_ref,
    places_ref,
    far_places_ref,
    charge_ref,
    short_ref,
    features_ref,
    w_long_ref,
    w_energy_ref,
    filt_ref,
    *rest,
):
    *kept, grad_ref, refined_ref, field_ref, neutral_ref = rest
    n, channels = features_ref.shape
    charge_ch = w_long_ref.shape[0]
    wide = 2 * ORDERS * charge_ch
    own = places_ref[0]
    live_row = own[3:4, :]

    lives = [jnp.sum(r[...], axis=0)[3:4, :] for r in (places_ref, far_places_ref)]
    lives = [jnp.sum(v, axis=1, keepdims=True) for v in lives]
    tail = wide + 16
    bases = [r[tail : tail + charge_ch, 0:1].astype(F32) for r in (part_ref, far_part_ref)]
    rests = [sums_ref[0:charge_ch, 0:1], far_part_ref[0:charge_ch, 0:1].astype(F32)]
    mean = (bases[0] * lives[0] + rests[0] + bases[1] * lives[1] + rests[1]) / (lives[0] + lives[1])
    gaps = [b - mean for b in bases]
    far_living = far_part_ref[wide : wide + 16, :].astype(F32)

    def load(kind, c):
        lo = (kind * ORDERS + c) * charge_ch
        row = kind * 8 + c
        return (
            sums_ref[lo : lo + charge_ch, :]
            + far_part_ref[lo : lo + charge_ch, :].astype(F32)
            + gaps[0] * sums_ref[wide + row : wide + row + 1, :]
            + gaps[1] * far_living[row : row + 1, :]
        )

    filtered(load, filt_ref, field_ref, charge_ch)
    neutral_ref[...] = (charge_ref[...] - mean) * live_row
    if kept:
        plane = kept[0][0]
        tz = (kept[1][0, 0:8, :], kept[1][0, 8:16, :])
    else:
        tx, ty, tz = axis_tables(own, place_of(meta_ref, 0, 0, sizes), sizes)
        plane = plane_table(tx, ty).astype(BF16)
    lifted = dot(field_ref[...], plane)
    potential = jnp.zeros((charge_ch, n), F32)
    for kind in range(2):
        for c in range(ORDERS):
            lo = (kind * ORDERS + c) * charge_ch
            potential = potential + tz[kind][c : c + 1, :] * lifted[lo : lo + charge_ch, :]
    pre_act = short_ref[...] + dot(jnp.transpose(potential).astype(BF16), w_long_ref[...])
    sig = sigmoid(pre_act)
    refined = features_ref[...].astype(F32) + pre_act * sig
    refined_ref[...] = refined
    sig_r = sigmoid(refined)
    live_rows = lax.broadcasted_iota(jnp.int32, (n, channels), 0) < count_ref[0]
    grad = (
        w_energy_ref[...]
        * (sig_r * (1.0 + refined * (1.0 - sig_r)))
        * (sig * (1.0 + pre_act * (1.0 - sig)))
    )
    grad_ref[...] = jnp.where(live_rows, grad, 0.0).astype(BF16)


def pair_force(sizes, meta_ref, places, strengths_ref, n, slopes_to=None, slopes_from=None):
    own_cols = columns(places[0][0], n)
    odd = lax.rem(meta_ref[0], 2)
    blocks = blocks_of(sizes)
    parts = [[], [], []]
    for first in range(0, n, 32):
        cols = [c[first : first + 32, :] for c in own_cols]
        acc = [jnp.zeros((32, n), F32) for _ in range(3)]
        for t, block in enumerate(blocks):
            half, m = block_place(sizes, odd, block)
            pos = places[half][m]
            offs = offsets(cols, [pos[a : a + 1, :] for a in range(3)], block)
            if slopes_from is None:
                u, decays = pair_terms(offs, block, first)
            strength = jnp.zeros((32, n), F32)
            for b, g in enumerate(GAMMAS):
                lo = b * n + first
                part = strengths_ref[lo : lo + 32, t * n : (t + 1) * n]
                if slopes_from is None:
                    slope = decays[b] * (g * u + 2.0) * u
                else:
                    slope = slopes_from[lo : lo + 32, t * n : (t + 1) * n]
                if slopes_to is not None:
                    slopes_to[lo : lo + 32, t * n : (t + 1) * n] = slope
                strength = strength + slope * part
            for a in range(3):
                acc[a] = acc[a] + strength * offs[a]
        for a in range(3):
            parts[a].append(acc[a])
    return [
        (-2.0 * SCALE)
        * jnp.sum(jnp.transpose(jnp.concatenate(parts[a], axis=0)), axis=0, keepdims=True)
        for a in range(3)
    ]


def own_kernel(
    sizes,
    meta_ref,
    grad_ref,
    field_ref,
    places_ref,
    far_places_ref,
    xcat_ref,
    refined_ref,
    mixed_ref,
    w_long_ref,
    w_energy_ref,
    updated_ref,
    energy_ref,
    force_ref,
    lifted_ref,
    planes_ref,
    levels_ref,
    *rest,
):
    *slopes, strength_scr = rest
    n = grad_ref.shape[0]
    charge_ch = w_long_ref.shape[0]
    own = places_ref[0]
    refined = refined_ref[...]
    updated_ref[...] = refined.astype(BF16)
    energy_ref[...] = own[3:4, :] * jnp.sum(
        jnp.transpose(refined * sigmoid(refined) * w_energy_ref[...]), axis=0, keepdims=True
    )
    grad = grad_ref[...]
    channels = grad.shape[1]
    rows, lifted = [], []
    for b in range(len(GAMMAS)):
        mixed = mixed_ref[b * channels : (b + 1) * channels, :]
        rows.append(dot_nt(grad, mixed).astype(BF16))
        lifted.append(dot(xcat_ref[0:n, :], mixed).astype(BF16))
    lifted_ref[...] = jnp.concatenate(lifted, axis=0)
    strength_scr[...] = dot_nt(jnp.concatenate(rows, axis=0), xcat_ref[...])
    places = (places_ref, far_places_ref)
    near = pair_force(sizes, meta_ref, places, strength_scr, n, slopes[0] if slopes else None)
    pull = dot_nt(w_long_ref[...], grad)
    tables = axis_tables(own, place_of(meta_ref, 0, 0, sizes), sizes)
    planes = slope_planes(tables, sizes)
    planes_ref[...] = planes
    levels_ref[...] = jnp.concatenate(tables[2], axis=0)
    slope = field_slope(field_ref[...], planes, tables[2], sizes, pull, charge_ch)
    force_ref[...] = jnp.concatenate([near[a] - slope[a] for a in range(3)], axis=0)


def pull_kernel(sizes, group, meta_ref, near_ref, places_ref, w_long_ref, *rest):
    *kept, sums_ref, part_ref = rest
    n = near_ref.shape[1]
    groups = near_ref.shape[0] // group

    def structure(g):
        left, right = [], []
        rows = jnp.concatenate([near_ref[g * group + j] for j in range(group)], axis=0)
        pulls = dot_nt(w_long_ref[...], rows)
        for j in range(group):
            m = g * group + j
            if kept:
                tz = (kept[1][m, 0:8, :], kept[1][m, 8:16, :])
                right.append(kept[0][m])
            else:
                pos = places_ref[m]
                tx, ty, tz = axis_tables(pos, place_of(meta_ref, m, 0, sizes), sizes)
                right.append(plane_table(tx, ty).astype(BF16))
            left.append(spread(pulls[:, j * n : (j + 1) * n], tz))
        return dot_nt(jnp.concatenate(left, axis=1), jnp.concatenate(right, axis=1))

    add_groups(structure, groups, sums_ref)
    part_ref[...] = sums_ref[...].astype(BF16)


def react_kernel(
    sizes,
    meta_ref,
    near_ref,
    far_ref,
    places_ref,
    far_places_ref,
    lifted_ref,
    force_ref,
    *rest,
):
    *slopes, out_ref, gcat_scr, strength_scr = rest
    n = lifted_ref.shape[1]
    halves = (near_ref, far_ref)
    odd = lax.rem(meta_ref[0], 2)
    for t, block in enumerate(blocks_of(sizes)):
        half, m = block_place(sizes, odd, block)
        gcat_scr[t * n : (t + 1) * n, :] = halves[half][m]
    strength_scr[...] = dot_nt(lifted_ref[...], gcat_scr[...])
    places = (places_ref, far_places_ref)
    near = pair_force(sizes, meta_ref, places, strength_scr, n, None, slopes[0] if slopes else None)
    out_ref[...] = force_ref[...] + jnp.concatenate(near, axis=0)


def finish_kernel(
    sizes,
    sums_ref,
    far_part_ref,
    planes_ref,
    levels_ref,
    neutral_ref,
    force_ref,
    filt_ref,
    out_ref,
    field_scr,
):
    charge_ch = neutral_ref.shape[0]

    def load(kind, c):
        lo = (kind * ORDERS + c) * charge_ch
        return sums_ref[lo : lo + charge_ch, :] + far_part_ref[lo : lo + charge_ch, :].astype(F32)

    filtered(load, filt_ref, field_scr, charge_ch)
    tz = (levels_ref[0:8, :], levels_ref[8:16, :])
    slope = field_slope(field_scr[...], planes_ref[...], tz, sizes, neutral_ref[...], charge_ch)
    for a in range(3):
        out_ref[a] = force_ref[a : a + 1, :] - slope[a]


def gather_line(rows, nz):
    value = rows[None]
    return jnp.concatenate(
        [value]
        + [
            lax.ppermute(value, "gz", [(i, (i + s) % nz) for i in range(nz)])
            for s in range(1, nz)
        ],
        axis=0,
    )


def gather_cells(value, sizes, beside):
    nx, ny, nz = sizes
    pairs = nx // 2

    def shifted(value, dx, dy):
        moves = []
        for i in range(nx):
            for j in range(ny):
                moves.append((i * ny + j, (i + 2 * dx) % nx * ny + (j + dy) % ny))
        return lax.ppermute(value, ("gx", "gy"), moves)

    if pairs * ny <= 4:
        steps = [(dx, dy) for dx in range(pairs) for dy in range(ny)]
        value = jnp.concatenate(
            [value] + [shifted(value, dx, dy) for dx, dy in steps[1:]], axis=0
        )
    else:
        value = jnp.concatenate([value] + [shifted(value, 0, dy) for dy in range(1, ny)], axis=0)
        value = jnp.concatenate([value] + [shifted(value, dx, 0) for dx in range(1, pairs)], axis=0)
    value, *beside = lax.optimization_barrier((value, *beside))
    return value, *beside


def from_other_core(value):
    return lax.ppermute(value, "gx", [(i, i ^ 1) for i in range(lax.axis_size("gx"))])


def call(kernel, name, outs, scratch, smem, operands, kept, limit, flops, fetched):
    n_in = len(operands)
    first = n_in - kept
    operands = [
        pltpu.with_memory_space_constraint(o, pltpu.HBM if fetched else pltpu.VMEM)
        if i >= (smem if fetched else first)
        else o
        for i, o in enumerate(operands)
    ]
    specs = [pl.BlockSpec(memory_space=pltpu.SMEM)] * smem + [
        pl.BlockSpec(memory_space=pltpu.HBM if fetched else pltpu.VMEM)
    ] * (n_in - smem)
    return pl.pallas_call(
        kernel,
        name=name,
        out_shape=outs,
        in_specs=specs,
        out_specs=[pl.BlockSpec(memory_space=pltpu.VMEM)] * len(outs),
        scratch_shapes=scratch,
        compiler_params=pltpu.CompilerParams(vmem_limit_bytes=limit),
        cost_estimate=pl.CostEstimate(flops=flops, bytes_accessed=2_000_000, transcendentals=0),
    )(*operands)


def shards(
    features,
    positions,
    counts,
    w_proj,
    w_mix,
    w_long,
    w_charge,
    charge_bias,
    w_energy,
    k_filter,
    k_index,
):
    own_rows = features[0, 0, 0]
    n, channels = own_rows.shape
    charge_ch = w_charge.shape[0]
    waves = k_index.shape[1]
    bases = w_proj.shape[0]
    sizes = tuple(lax.axis_size(a) for a in AXES)
    cells = sizes[0] * sizes[1] * sizes[2]
    half_cells = cells // 2
    group = max(g for g in (8, 4, 2, 1) if half_cells % g == 0)
    blocks = len(blocks_of(sizes))
    scale_long = 4.0 / math.sqrt(n * cells * waves)
    count = counts.reshape(1)
    meta = jnp.stack([lax.axis_index(a) for a in AXES]).astype(jnp.int32)
    shape = jax.ShapeDtypeStruct
    wide = 2 * ORDERS * charge_ch
    fits = cells <= 64
    limit = (24 if fits else 56) * 1024 * 1024
    held = pltpu.VMEM if fits else shape

    def run(kernel, name, outs, scratch, smem, operands, kept, flops, fetched=False):
        kept = kept if fits else 0
        if fetched:
            places = [pltpu.VMEM(o.shape, o.dtype) for o in operands[smem:]]
            scratch = [*places, pltpu.SemaphoreType.DMA((len(places),))]
        return call(kernel, name, outs, scratch, smem, operands, kept, limit, flops, fetched)

    (packed,) = run(
        pack_kernel,
        "pack",
        [held((n + 16, channels), BF16)],
        [],
        1,
        [count, own_rows, positions.reshape(3, 1, n)],
        0,
        1000,
        fetched=True,
    )
    filt, bias, energy_row, mixed = run(
        lambda *refs: fold_kernel(scale_long, *refs),
        "fold_filter",
        [
            held((ORDERS, 4 * charge_ch, 128), F32),
            held((charge_ch, n), F32),
            held((1, channels), F32),
            held((bases * channels, channels), BF16),
        ],
        [],
        0,
        [
            k_filter,
            k_index,
            charge_bias[None, :],
            w_energy[None, :],
            w_proj.reshape(bases * channels, channels),
            w_mix,
        ],
        0,
        1_000_000_000,
        fetched=True,
    )
    line = gather_line(packed, sizes[2])
    line, filt, bias, energy_row, mixed = lax.optimization_barrier((line, filt, bias, energy_row, mixed))
    (near,) = gather_cells(line, sizes, ())
    far = from_other_core(near)
    sums, part, places, charge, *kept = run(
        lambda *refs: charge_kernel(sizes, group, *refs),
        "charge_sums",
        [
            held((wide + 16, 256), F32),
            held((wide + 16 + charge_ch, 256), BF16),
            held((half_cells, 8, n), F32),
            held((charge_ch, n), F32),
        ]
        + ([held((half_cells, 256, n), BF16), held((half_cells, 16, n), F32)] if fits else []),
        [pltpu.VMEM((half_cells, charge_ch, n), F32)],
        1,
        [meta, near, w_charge, bias],
        3,
        3_000_000_000,
    )
    far_part = from_other_core(part)
    short, far_places, xcat = run(
        lambda *refs: message_kernel(sizes, *refs),
        "message",
        [
            held((n, channels), F32),
            held((half_cells, 8, n), F32),
            held((blocks * n, channels), BF16),
        ],
        [pltpu.VMEM((bases * n, blocks * n), BF16)],
        1,
        [meta, near, far, places, mixed],
        4,
        3_000_000_000,
    )
    grad, refined, field, neutral = run(
        lambda *refs: cotangent_kernel(sizes, *refs),
        "cotangents",
        [
            held((n, channels), BF16),
            held((n, channels), F32),
            held((wide, 256), BF16),
            held((charge_ch, n), F32),
        ],
        [],
        2,
        [
            count,
            meta,
            sums,
            part,
            far_part,
            places,
            far_places,
            charge,
            short,
            own_rows,
            w_long,
            energy_row,
            filt,
            *kept,
        ],
        11 + len(kept),
        3_000_000_000,
    )
    grad_line, grad = lax.optimization_barrier((gather_line(grad, sizes[2]), grad))
    updated, energy, force, lifted, planes, levels, *slopes = run(
        lambda *refs: own_kernel(sizes, *refs),
        "own_terms",
        [
            shape((n, channels), BF16),
            shape((1, n), F32),
            held((3, n), F32),
            held((bases * n, channels), BF16),
            held((256, 3 * n), BF16),
            held((16, n), F32),
        ]
        + ([held((bases * n, blocks * n), F32)] if fits else []),
        [pltpu.VMEM((bases * n, blocks * n), F32)],
        1,
        [
            meta,
            grad,
            field,
            places,
            far_places,
            xcat,
            refined,
            mixed,
            w_long,
            energy_row,
        ],
        9,
        4_000_000_000,
    )
    grad_near, force, lifted = gather_cells(grad_line, sizes, (force, lifted))
    grad_far = from_other_core(grad_near)
    back, back_part = run(
        lambda *refs: pull_kernel(sizes, group, *refs),
        "pull_sums",
        [held((wide, 256), F32), held((wide, 256), BF16)],
        [],
        1,
        [meta, grad_near, places, w_long, *kept],
        3 + len(kept),
        3_000_000_000,
    )
    far_back = from_other_core(back_part)
    (force,) = run(
        lambda *refs: react_kernel(sizes, *refs),
        "react",
        [held((3, n), F32)],
        [
            pltpu.VMEM((blocks * n, channels), BF16),
            pltpu.VMEM((bases * n, blocks * n), F32),
        ],
        1,
        [meta, grad_near, grad_far, places, far_places, lifted, force, *slopes],
        6 + len(slopes),
        3_000_000_000,
    )
    (forces,) = run(
        lambda *refs: finish_kernel(sizes, *refs),
        "finish",
        [shape((3, 1, n), F32)],
        [pltpu.VMEM((wide, 256), BF16)],
        0,
        [back, far_back, planes, levels, neutral, force, filt],
        7,
        2_000_000_000,
    )
    return (
        updated[None, None, None],
        energy[None, None],
        forces.reshape(positions.shape),
    )


def solution(mesh):
    cell = ("gx", "gy", "gz")
    in_specs = (P(*cell, None, None), P(*cell, None, None), P(*cell)) + (P(),) * 8
    out_specs = (P(*cell, None, None), P(*cell, None), P(*cell, None, None))
    return jax.shard_map(shards, mesh=mesh, in_specs=in_specs, out_specs=out_specs, check_vma=False)
```

```python
import itertools
import math

import jax
import jax.numpy as jnp
import numpy as np
from jax import lax
from jax.experimental import pallas as pl
from jax.experimental.pallas import tpu as pltpu
from jax.sharding import PartitionSpec as P

CUTOFF = 0.9
SCALE = 1.0 / (CUTOFF * CUTOFF)
GAMMAS = (1.0, 3.0, 8.0, 20.0)
AXES = ("gx", "gy", "gz")
ORDERS = 7
NT = (((1,), (1,)), ((), ()))
F32 = jnp.float32
BF16 = jnp.bfloat16


def turn_series():
    nodes = np.cos(np.pi * (np.arange(200) + 0.5) / 200)
    r2 = (nodes + 1.0) / 8.0
    r = np.sqrt(r2)
    out = []
    for values in (np.cos(2 * np.pi * r), np.sin(2 * np.pi * r) / r):
        cheb = np.polynomial.chebyshev.Chebyshev.fit(r2, values, 6, domain=[0.0, 0.25])
        out.append([float(c) for c in cheb.convert(kind=np.polynomial.Polynomial).coef])
    return out


COS_SERIES, SIN_SERIES = turn_series()


def dot(a, b):
    return jnp.dot(a, b, preferred_element_type=F32)


def dot_nt(a, b):
    return lax.dot_general(a, b, NT, preferred_element_type=F32)


def sigmoid(v):
    return 1.0 / (1.0 + jnp.exp(-v))


def cos_sin(turns):
    r = turns - jnp.floor(turns + 0.5)
    r2 = r * r
    c = jnp.full_like(r2, COS_SERIES[-1])
    for coef in COS_SERIES[-2::-1]:
        c = c * r2 + coef
    s = jnp.full_like(r2, SIN_SERIES[-1])
    for coef in SIN_SERIES[-2::-1]:
        s = s * r2 + coef
    return c, s * r


def axis_tables(pos, anchor, sizes):
    order = lax.broadcasted_iota(jnp.int32, (8, pos.shape[1]), 0).astype(F32)
    tables = []
    for a in range(3):
        row = (pos[a : a + 1, :] + anchor[a]) * (1.0 / sizes[a])
        tables.append(cos_sin(order * row))
    return tables


def plane_table(first, second):
    rows = []
    for f in first:
        for s in second:
            for a in range(8):
                rows.append(f[a : a + 1, :] * s)
    return jnp.concatenate(rows, axis=0)


def derivative(table, size):
    order = lax.broadcasted_iota(jnp.int32, table[0].shape, 0).astype(F32) * (2.0 * math.pi / size)
    return (-order * table[1], order * table[0])


def spread(weights, third):
    rows = []
    for f in third:
        for c in range(ORDERS):
            rows.append((weights * f[c : c + 1, :]).astype(BF16))
    return jnp.concatenate(rows, axis=0)


def filtered(load, filt_ref, out_ref, charge_ch):
    shift = ORDERS * charge_ch
    for c in range(ORDERS):
        lo, hi = c * charge_ch, (c + 1) * charge_ch
        f0, gfb, fc, gfbc = (filt_ref[c, w * charge_ch : (w + 1) * charge_ch, :] for w in range(4))
        cos_part, sin_part = load(0, c), load(1, c)
        a_c, b_c = cos_part[:, 0:128], cos_part[:, 128:256]
        a_s, b_s = sin_part[:, 0:128], sin_part[:, 128:256]
        ra_c, rb_c, ra_s, rb_s = (pltpu.roll(v, 64, 1) for v in (a_c, b_c, a_s, b_s))
        out_ref[lo:hi, 0:128] = (f0 * a_c + gfbc * ra_s - fc * b_s + gfb * rb_c).astype(BF16)
        out_ref[lo:hi, 128:256] = (f0 * b_c - gfb * ra_c + fc * a_s + gfbc * rb_s).astype(BF16)
        out_ref[shift + lo : shift + hi, 0:128] = (
            f0 * a_s + fc * b_c - gfbc * ra_c + gfb * rb_s
        ).astype(BF16)
        out_ref[shift + lo : shift + hi, 128:256] = (
            f0 * b_s - fc * a_c - gfb * ra_s - gfbc * rb_c
        ).astype(BF16)


def slope_planes(tables, sizes):
    tx, ty, _ = tables
    return jnp.concatenate(
        [
            plane_table(derivative(tx, sizes[0]), ty).astype(BF16),
            plane_table(tx, derivative(ty, sizes[1])).astype(BF16),
            plane_table(tx, ty).astype(BF16),
        ],
        axis=1,
    )


def field_slope(field, planes, tz, sizes, weights, charge_ch):
    n = tz[0].shape[1]
    spread_field = dot(field, planes)
    slope_z = derivative(tz, sizes[2])
    total = [jnp.zeros((charge_ch, n), F32) for _ in range(3)]
    for kind in range(2):
        for c in range(ORDERS):
            lo = (kind * ORDERS + c) * charge_ch
            part = spread_field[lo : lo + charge_ch, :]
            zrow, drow = tz[kind][c : c + 1, :], slope_z[kind][c : c + 1, :]
            total[0] = total[0] + zrow * part[:, 0:n]
            total[1] = total[1] + zrow * part[:, n : 2 * n]
            total[2] = total[2] + drow * part[:, 2 * n : 3 * n]
    return [jnp.sum(t * weights, axis=0, keepdims=True) for t in total]


def place_of(m, half, sizes):
    nx, ny, nz = sizes
    dz = lax.rem(m, nz)
    dy = lax.rem(m // nz, ny)
    dx = m // (nz * ny)
    start = lax.axis_index(AXES[0]) if half == 0 else lax.axis_index(AXES[0]) + 1 - 2 * lax.rem(lax.axis_index(AXES[0]), 2)
    cx = lax.rem(start - 2 * dx + nx, nx)
    cy = lax.rem(lax.axis_index(AXES[1]) - dy + ny, ny)
    cz = lax.rem(lax.axis_index(AXES[2]) - dz + nz, nz)
    return (cx.astype(F32), cy.astype(F32), cz.astype(F32))


def blocks_of(sizes):
    options = [((0, False), (1, True)) if n == 2 else ((0, False), (-1, False), (1, False)) for n in sizes]
    return list(itertools.product(*options))


def offsets(own_cols, others, block):
    result = []
    for a, (step, nearest) in enumerate(block):
        if nearest:
            d = others[a] - own_cols[a]
            d = d - jnp.where(d > 0.0, 1.0, -1.0)
        else:
            d = (others[a] + float(step)) - own_cols[a]
        result.append(d)
    return result


def pair_terms(offs, block, first_row):
    s = (offs[0] * offs[0] + offs[1] * offs[1] + offs[2] * offs[2]) * SCALE
    u = jnp.maximum(1.0 - s, 0.0)
    if all(step == 0 for step, _ in block):
        rows = lax.broadcasted_iota(jnp.int32, s.shape, 0) + first_row
        cols = lax.broadcasted_iota(jnp.int32, s.shape, 1)
        u = jnp.where(rows == cols, 0.0, u)
    e1 = jnp.exp(-s)
    e2 = e1 * e1
    e3 = e2 * e1
    e4 = e2 * e2
    e8 = e4 * e4
    e20 = e8 * e8 * e4
    return u, (e1, e3, e8, e20)


def columns(pos, n):
    return [jnp.transpose(jnp.broadcast_to(pos[a : a + 1, :], (n, n))) for a in range(3)]


def fetch(sources, places, sems):
    copies = [pltpu.make_async_copy(s, p, sems.at[i]) for i, (s, p) in enumerate(zip(sources, places))]
    for c in copies:
        c.start()
    for c in copies:
        c.wait()


def pack_kernel(
    count_ref,
    features_hbm,
    positions_hbm,
    out_ref,
    live_ref,
    features_ref,
    positions_ref,
    sems,
):
    fetch((features_hbm, positions_hbm), (features_ref, positions_ref), sems)
    n, channels = features_ref.shape
    live_col = lax.broadcasted_iota(jnp.int32, (n, channels), 0) < count_ref[0]
    live_ref[...] = live_col.astype(F32)
    rows = features_ref[...].astype(F32)
    out_ref[0:n, :] = jnp.where(live_col, rows, 0.0).astype(BF16)
    pos = jnp.concatenate([positions_ref[a] for a in range(3)], axis=0)
    coarse = pos.astype(BF16).astype(F32)
    fine = pos - coarse
    living = (lax.broadcasted_iota(jnp.int32, (1, n), 1) < count_ref[0]).astype(F32)
    blank = jnp.zeros((4, n), F32)
    tail = jnp.concatenate([coarse, living, blank, fine, jnp.zeros((5, n), F32)], axis=0)
    out_ref[n : n + 16, :] = tail.astype(BF16)


def fold_kernel(
    scale,
    filter_hbm,
    index_hbm,
    bias_hbm,
    energy_hbm,
    proj_hbm,
    mix_hbm,
    out_ref,
    column_ref,
    row_ref,
    mixed_ref,
    filter_ref,
    index_ref,
    bias_ref,
    energy_ref,
    proj_ref,
    mix_ref,
    sems,
):
    fetch(
        (filter_hbm, index_hbm, bias_hbm, energy_hbm, proj_hbm, mix_hbm),
        (filter_ref, index_ref, bias_ref, energy_ref, proj_ref, mix_ref),
        sems,
    )
    waves = filter_ref.shape[1]
    charge_ch = filter_ref.shape[0]
    row_ref[...] = energy_ref[...]
    diagonal = lax.broadcasted_iota(jnp.int32, (charge_ch, charge_ch), 0) == (
        lax.broadcasted_iota(jnp.int32, (charge_ch, charge_ch), 1)
    )
    column = jnp.sum(jnp.where(diagonal, bias_ref[...], 0.0), axis=1, keepdims=True)
    column_ref[...] = jnp.broadcast_to(column, column_ref.shape)
    mixed_ref[...] = dot(proj_ref[...], mix_ref[...]).astype(BF16)
    k = index_ref[...]
    positive = [jnp.where(k[a : a + 1, :] >= 0, 1.0, -1.0) for a in range(3)]
    sign_b = positive[0] * positive[1]
    sign_c = positive[0] * positive[2]
    size = jnp.abs(k)
    key = size[2:3, :] * 64 + size[0:1, :] * 8 + size[1:2, :]
    f = filter_ref[...] * scale
    stacked = jnp.concatenate([f, f * sign_b, f * sign_c, f * (sign_b * sign_c)], axis=0).astype(BF16)
    rows = lax.broadcasted_iota(jnp.int32, (ORDERS * 64, waves), 0)
    parts = dot_nt(stacked, jnp.where(rows == key, 1.0, 0.0).astype(BF16))
    turn = jnp.where(lax.broadcasted_iota(jnp.int32, (charge_ch, 128), 1) < 64, -1.0, 1.0)
    for c in range(ORDERS):
        part = parts[:, c * 64 : (c + 1) * 64]
        part = jnp.concatenate([part, part], axis=1)
        for w in range(4):
            piece = part[w * charge_ch : (w + 1) * charge_ch, :]
            out_ref[c, w * charge_ch : (w + 1) * charge_ch, :] = piece * turn if w % 2 == 1 else piece


def block_place(sizes, odd, block):
    nx, ny, nz = sizes
    dy, dz = (-block[1][0]) % ny, (-block[2][0]) % nz
    if block[0][0] == 0:
        return 0, dy * nz + dz
    dx = odd * (nx // 2 - 1) if block[0][0] == 1 else (1 - odd) * (1 % (nx // 2))
    return 1, (dx * ny + dy) * nz + dz


def add_groups(structure, groups, sums_ref):
    if groups <= 4:
        total = structure(0)
        for g in range(1, groups):
            total = total + structure(g)
        sums_ref[...] = total
        return
    sums_ref[...] = structure(0)

    def add_structure(g, _):
        sums_ref[...] += structure(g)
        return 0

    lax.fori_loop(1, groups, add_structure, 0)


def charge_kernel(
    sizes,
    group,
    near_ref,
    w_charge_ref,
    bias_ref,
    sums_ref,
    part_ref,
    places_ref,
    charge_ref,
    *rest,
):
    *kept, charge_scr = rest
    charge_ch, channels = w_charge_ref.shape
    cells = near_ref.shape[0]
    n = near_ref.shape[1] - 16
    wide = 2 * ORDERS * charge_ch
    groups = cells // group
    w_charge = w_charge_ref[...]
    bias = bias_ref[...]

    def add_charges(g, carry):
        total, live_total = carry
        for j in range(group):
            m = g * group + j
            tail = near_ref[m, n : n + 16, :].astype(F32)
            pos = tail[0:8, :] + tail[8:16, :]
            places_ref[m] = pos
            live = pos[3:4, :]
            v = dot_nt(w_charge, near_ref[m, 0:n, :]) + bias
            q = v * sigmoid(v) * live
            charge_scr[m] = q
            total = total + q
            live_total = live_total + live
        return total, live_total

    start = (jnp.zeros((charge_ch, n), F32), jnp.zeros((1, n), F32))
    if groups <= 4:
        for g in range(groups):
            start = add_charges(g, start)
        total, live_total = start
    else:
        total, live_total = lax.fori_loop(0, groups, add_charges, start)
    mean = jnp.sum(total, axis=1, keepdims=True) / jnp.sum(live_total, axis=1, keepdims=True)
    mean = mean.astype(BF16).astype(F32)
    charge_ref[...] = charge_scr[0]

    def structure(g):
        left, right = [], []
        for j in range(group):
            m = g * group + j
            pos = places_ref[m]
            tx, ty, tz = axis_tables(pos, place_of(m, 0, sizes), sizes)
            live = pos[3:4, :]
            living = jnp.concatenate([tz[0] * live, tz[1] * live], axis=0).astype(BF16)
            plane = plane_table(tx, ty).astype(BF16)
            if kept:
                kept[0][m] = plane
                kept[1][m] = jnp.concatenate(tz, axis=0)
            left.append(
                jnp.concatenate([spread((charge_scr[m] - mean) * live, tz), living], axis=0)
            )
            right.append(plane)
        return dot_nt(jnp.concatenate(left, axis=1), jnp.concatenate(right, axis=1))

    add_groups(structure, groups, sums_ref)
    part_ref[0 : wide + 16, :] = sums_ref[...].astype(BF16)
    part_ref[wide + 16 : wide + 16 + charge_ch, :] = jnp.broadcast_to(mean, (charge_ch, 256)).astype(
        BF16
    )


def message_kernel(
    sizes,
    near_ref,
    far_ref,
    near_places_ref,
    mixed_ref,
    short_ref,
    far_places_ref,
    xcat_ref,
    radial_scr,
):
    n = near_ref.shape[1] - 16
    halves = (near_ref, far_ref)
    places = (near_places_ref, far_places_ref)

    def add_place(m, _):
        tail = far_ref[m, n : n + 16, :].astype(F32)
        far_places_ref[m] = tail[0:8, :] + tail[8:16, :]
        return 0

    lax.fori_loop(0, far_ref.shape[0], add_place, 0, unroll=4)
    odd = lax.rem(lax.axis_index(AXES[0]), 2)
    own_cols = columns(near_places_ref[0], n)
    for t, block in enumerate(blocks_of(sizes)):
        half, m = block_place(sizes, odd, block)
        xcat_ref[t * n : (t + 1) * n, :] = halves[half][m, 0:n, :]
        pos = places[half][m]
        others = [pos[a : a + 1, :] for a in range(3)]
        for first in range(0, n, 32):
            cols = [c[first : first + 32, :] for c in own_cols]
            u, decays = pair_terms(offsets(cols, others, block), block, first)
            u2 = u * u
            for b in range(len(GAMMAS)):
                radial_scr[b * n + first : b * n + first + 32, t * n : (t + 1) * n] = (
                    decays[b] * u2
                ).astype(BF16)
    gathered = dot(radial_scr[...], xcat_ref[...]).astype(BF16)
    gathered = jnp.concatenate([gathered[b * n : (b + 1) * n, :] for b in range(len(GAMMAS))], axis=1)
    short_ref[...] = dot(gathered, mixed_ref[...])


def cotangent_kernel(
    sizes,
    live_ref,
    sums_ref,
    part_ref,
    far_part_ref,
    places_ref,
    far_places_ref,
    charge_ref,
    short_ref,
    features_ref,
    w_long_ref,
    w_energy_ref,
    filt_ref,
    *rest,
):
    *kept, grad_ref, refined_ref, field_ref, neutral_ref = rest
    n, channels = features_ref.shape
    charge_ch = w_long_ref.shape[0]
    wide = 2 * ORDERS * charge_ch
    own = places_ref[0]
    live_row = own[3:4, :]

    lives = [jnp.sum(r[...], axis=0)[3:4, :] for r in (places_ref, far_places_ref)]
    lives = [jnp.sum(v, axis=1, keepdims=True) for v in lives]
    tail = wide + 16
    bases = [r[tail : tail + charge_ch, 0:1].astype(F32) for r in (part_ref, far_part_ref)]
    rests = [sums_ref[0:charge_ch, 0:1], far_part_ref[0:charge_ch, 0:1].astype(F32)]
    mean = (bases[0] * lives[0] + rests[0] + bases[1] * lives[1] + rests[1]) / (lives[0] + lives[1])
    gaps = [b - mean for b in bases]
    far_living = far_part_ref[wide : wide + 16, :].astype(F32)

    def load(kind, c):
        lo = (kind * ORDERS + c) * charge_ch
        row = kind * 8 + c
        return (
            sums_ref[lo : lo + charge_ch, :]
            + far_part_ref[lo : lo + charge_ch, :].astype(F32)
            + gaps[0] * sums_ref[wide + row : wide + row + 1, :]
            + gaps[1] * far_living[row : row + 1, :]
        )

    filtered(load, filt_ref, field_ref, charge_ch)
    neutral_ref[...] = (charge_ref[...] - mean) * live_row
    if kept:
        plane = kept[0][0]
        tz = (kept[1][0, 0:8, :], kept[1][0, 8:16, :])
    else:
        tx, ty, tz = axis_tables(own, place_of(0, 0, sizes), sizes)
        plane = plane_table(tx, ty).astype(BF16)
    lifted = dot(field_ref[...], plane)
    potential = jnp.zeros((charge_ch, n), F32)
    for kind in range(2):
        for c in range(ORDERS):
            lo = (kind * ORDERS + c) * charge_ch
            potential = potential + tz[kind][c : c + 1, :] * lifted[lo : lo + charge_ch, :]
    pre_act = short_ref[...] + dot(jnp.transpose(potential).astype(BF16), w_long_ref[...])
    sig = sigmoid(pre_act)
    refined = features_ref[...].astype(F32) + pre_act * sig
    refined_ref[...] = refined
    sig_r = sigmoid(refined)
    grad = (
        w_energy_ref[...]
        * (sig_r * (1.0 + refined * (1.0 - sig_r)))
        * (sig * (1.0 + pre_act * (1.0 - sig)))
    )
    grad_ref[...] = (grad * live_ref[...]).astype(BF16)


def pair_force(sizes, places, strengths_ref, n, slopes_to=None, slopes_from=None):
    own_cols = columns(places[0][0], n)
    odd = lax.rem(lax.axis_index(AXES[0]), 2)
    blocks = blocks_of(sizes)
    parts = [[], [], []]
    for first in range(0, n, 32):
        cols = [c[first : first + 32, :] for c in own_cols]
        acc = [jnp.zeros((32, n), F32) for _ in range(3)]
        for t, block in enumerate(blocks):
            half, m = block_place(sizes, odd, block)
            pos = places[half][m]
            offs = offsets(cols, [pos[a : a + 1, :] for a in range(3)], block)
            if slopes_from is None:
                u, decays = pair_terms(offs, block, first)
            strength = jnp.zeros((32, n), F32)
            for b, g in enumerate(GAMMAS):
                lo = b * n + first
                part = strengths_ref[lo : lo + 32, t * n : (t + 1) * n]
                if slopes_from is None:
                    slope = decays[b] * (g * u + 2.0) * u
                else:
                    slope = slopes_from[lo : lo + 32, t * n : (t + 1) * n]
                if slopes_to is not None:
                    slopes_to[lo : lo + 32, t * n : (t + 1) * n] = slope
                strength = strength + slope * part
            for a in range(3):
                acc[a] = acc[a] + strength * offs[a]
        for a in range(3):
            parts[a].append(acc[a])
    return [
        (-2.0 * SCALE)
        * jnp.sum(jnp.transpose(jnp.concatenate(parts[a], axis=0)), axis=0, keepdims=True)
        for a in range(3)
    ]


def own_kernel(
    sizes,
    grad_ref,
    field_ref,
    places_ref,
    far_places_ref,
    xcat_ref,
    refined_ref,
    mixed_ref,
    w_long_ref,
    w_energy_ref,
    updated_ref,
    energy_ref,
    force_ref,
    lifted_ref,
    planes_ref,
    levels_ref,
    *rest,
):
    *slopes, strength_scr = rest
    n = grad_ref.shape[0]
    charge_ch = w_long_ref.shape[0]
    own = places_ref[0]
    refined = refined_ref[...]
    updated_ref[...] = refined.astype(BF16)
    energy_ref[...] = own[3:4, :] * jnp.sum(
        jnp.transpose(refined * sigmoid(refined) * w_energy_ref[...]), axis=0, keepdims=True
    )
    grad = grad_ref[...]
    channels = grad.shape[1]
    rows, lifted = [], []
    for b in range(len(GAMMAS)):
        mixed = mixed_ref[b * channels : (b + 1) * channels, :]
        rows.append(dot_nt(grad, mixed).astype(BF16))
        lifted.append(dot(xcat_ref[0:n, :], mixed).astype(BF16))
    lifted_ref[...] = jnp.concatenate(lifted, axis=0)
    strength_scr[...] = dot_nt(jnp.concatenate(rows, axis=0), xcat_ref[...])
    places = (places_ref, far_places_ref)
    near = pair_force(sizes, places, strength_scr, n, slopes[0] if slopes else None)
    pull = dot_nt(w_long_ref[...], grad)
    tables = axis_tables(own, place_of(0, 0, sizes), sizes)
    planes = slope_planes(tables, sizes)
    planes_ref[...] = planes
    levels_ref[...] = jnp.concatenate(tables[2], axis=0)
    slope = field_slope(field_ref[...], planes, tables[2], sizes, pull, charge_ch)
    force_ref[...] = jnp.concatenate([near[a] - slope[a] for a in range(3)], axis=0)


def pull_kernel(sizes, group, near_ref, places_ref, w_long_ref, *rest):
    *kept, sums_ref, part_ref = rest
    n = near_ref.shape[1]
    groups = near_ref.shape[0] // group

    def structure(g):
        left, right = [], []
        rows = jnp.concatenate([near_ref[g * group + j] for j in range(group)], axis=0)
        pulls = dot_nt(w_long_ref[...], rows)
        for j in range(group):
            m = g * group + j
            if kept:
                tz = (kept[1][m, 0:8, :], kept[1][m, 8:16, :])
                right.append(kept[0][m])
            else:
                pos = places_ref[m]
                tx, ty, tz = axis_tables(pos, place_of(m, 0, sizes), sizes)
                right.append(plane_table(tx, ty).astype(BF16))
            left.append(spread(pulls[:, j * n : (j + 1) * n], tz))
        return dot_nt(jnp.concatenate(left, axis=1), jnp.concatenate(right, axis=1))

    add_groups(structure, groups, sums_ref)
    part_ref[...] = sums_ref[...].astype(BF16)


def react_kernel(
    sizes,
    near_ref,
    far_ref,
    places_ref,
    far_places_ref,
    lifted_ref,
    force_ref,
    *rest,
):
    *slopes, out_ref, gcat_scr, strength_scr = rest
    n = lifted_ref.shape[1]
    halves = (near_ref, far_ref)
    odd = lax.rem(lax.axis_index(AXES[0]), 2)
    for t, block in enumerate(blocks_of(sizes)):
        half, m = block_place(sizes, odd, block)
        gcat_scr[t * n : (t + 1) * n, :] = halves[half][m]
    strength_scr[...] = dot_nt(lifted_ref[...], gcat_scr[...])
    places = (places_ref, far_places_ref)
    near = pair_force(sizes, places, strength_scr, n, None, slopes[0] if slopes else None)
    out_ref[...] = force_ref[...] + jnp.concatenate(near, axis=0)


def finish_kernel(
    sizes,
    sums_ref,
    far_part_ref,
    planes_ref,
    levels_ref,
    neutral_ref,
    force_ref,
    filt_ref,
    out_ref,
    field_scr,
):
    charge_ch = neutral_ref.shape[0]

    def load(kind, c):
        lo = (kind * ORDERS + c) * charge_ch
        return sums_ref[lo : lo + charge_ch, :] + far_part_ref[lo : lo + charge_ch, :].astype(F32)

    filtered(load, filt_ref, field_scr, charge_ch)
    tz = (levels_ref[0:8, :], levels_ref[8:16, :])
    slope = field_slope(field_scr[...], planes_ref[...], tz, sizes, neutral_ref[...], charge_ch)
    for a in range(3):
        out_ref[a] = force_ref[a : a + 1, :] - slope[a]


def gather_line(rows, nz):
    value = rows[None]
    return jnp.concatenate(
        [value]
        + [
            lax.ppermute(value, "gz", [(i, (i + s) % nz) for i in range(nz)])
            for s in range(1, nz)
        ],
        axis=0,
    )


def gather_cells(value, sizes, beside):
    nx, ny, nz = sizes
    pairs = nx // 2

    def shifted(value, dx, dy):
        moves = []
        for i in range(nx):
            for j in range(ny):
                moves.append((i * ny + j, (i + 2 * dx) % nx * ny + (j + dy) % ny))
        return lax.ppermute(value, ("gx", "gy"), moves)

    if pairs * ny <= 4:
        steps = [(dx, dy) for dx in range(pairs) for dy in range(ny)]
        value = jnp.concatenate(
            [value] + [shifted(value, dx, dy) for dx, dy in steps[1:]], axis=0
        )
    else:
        value = jnp.concatenate([value] + [shifted(value, 0, dy) for dy in range(1, ny)], axis=0)
        value = jnp.concatenate([value] + [shifted(value, dx, 0) for dx in range(1, pairs)], axis=0)
    value, *beside = lax.optimization_barrier((value, *beside))
    return value, *beside


def from_other_core(value):
    return lax.ppermute(value, "gx", [(i, i ^ 1) for i in range(lax.axis_size("gx"))])


def call(kernel, name, outs, scratch, operands, kept, limit, flops, fetched):
    n_in = len(operands)
    first = n_in - kept
    operands = [
        pltpu.with_memory_space_constraint(o, pltpu.HBM if fetched else pltpu.VMEM)
        if (fetched and o.size > 1) or i >= first
        else o
        for i, o in enumerate(operands)
    ]
    specs = [
        pl.BlockSpec(
            memory_space=pltpu.SMEM if o.size == 1 else pltpu.HBM if fetched else pltpu.VMEM
        )
        for o in operands
    ]
    return pl.pallas_call(
        kernel,
        name=name,
        out_shape=outs,
        in_specs=specs,
        out_specs=[pl.BlockSpec(memory_space=pltpu.VMEM)] * len(outs),
        scratch_shapes=scratch,
        compiler_params=pltpu.CompilerParams(vmem_limit_bytes=limit),
        cost_estimate=pl.CostEstimate(flops=flops, bytes_accessed=2_000_000, transcendentals=0),
    )(*operands)


def shards(
    features,
    positions,
    counts,
    w_proj,
    w_mix,
    w_long,
    w_charge,
    charge_bias,
    w_energy,
    k_filter,
    k_index,
):
    own_rows = features[0, 0, 0]
    n, channels = own_rows.shape
    charge_ch = w_charge.shape[0]
    waves = k_index.shape[1]
    bases = w_proj.shape[0]
    sizes = tuple(lax.axis_size(a) for a in AXES)
    cells = sizes[0] * sizes[1] * sizes[2]
    half_cells = cells // 2
    group = max(g for g in (8, 4, 2, 1) if half_cells % g == 0)
    blocks = len(blocks_of(sizes))
    scale_long = 4.0 / math.sqrt(n * cells * waves)
    count = counts.reshape(1)
    shape = jax.ShapeDtypeStruct
    wide = 2 * ORDERS * charge_ch
    fits = cells <= 64
    limit = (24 if fits else 56) * 1024 * 1024
    held = pltpu.VMEM if fits else shape

    def run(kernel, name, outs, scratch, operands, kept, flops, fetched=False):
        kept = kept if fits else 0
        if fetched:
            places = [pltpu.VMEM(o.shape, o.dtype) for o in operands if o.size > 1]
            scratch = [*places, pltpu.SemaphoreType.DMA((len(places),))]
        return call(kernel, name, outs, scratch, operands, kept, limit, flops, fetched)

    packed, live = run(
        pack_kernel,
        "pack",
        [held((n + 16, channels), BF16), held((n, channels), F32)],
        [],
        [count, own_rows, positions.reshape(3, 1, n)],
        0,
        1000,
        fetched=True,
    )
    filt, bias, energy_row, mixed = run(
        lambda *refs: fold_kernel(scale_long, *refs),
        "fold_filter",
        [
            held((ORDERS, 4 * charge_ch, 128), F32),
            held((charge_ch, n), F32),
            held((1, channels), F32),
            held((bases * channels, channels), BF16),
        ],
        [],
        [
            k_filter,
            k_index,
            charge_bias[None, :],
            w_energy[None, :],
            w_proj.reshape(bases * channels, channels),
            w_mix,
        ],
        0,
        1_000_000_000,
        fetched=True,
    )
    line = gather_line(packed, sizes[2])
    line, filt, bias, energy_row, mixed = lax.optimization_barrier((line, filt, bias, energy_row, mixed))
    (near,) = gather_cells(line, sizes, ())
    far = from_other_core(near)
    sums, part, places, charge, *kept = run(
        lambda *refs: charge_kernel(sizes, group, *refs),
        "charge_sums",
        [
            held((wide + 16, 256), F32),
            held((wide + 16 + charge_ch, 256), BF16),
            held((half_cells, 8, n), F32),
            held((charge_ch, n), F32),
        ]
        + ([held((half_cells, 256, n), BF16), held((half_cells, 16, n), F32)] if fits else []),
        [pltpu.VMEM((half_cells, charge_ch, n), F32)],
        [near, w_charge, bias],
        3,
        3_000_000_000,
    )
    far_part = from_other_core(part)
    short, far_places, xcat = run(
        lambda *refs: message_kernel(sizes, *refs),
        "message",
        [
            held((n, channels), F32),
            held((half_cells, 8, n), F32),
            held((blocks * n, channels), BF16),
        ],
        [pltpu.VMEM((bases * n, blocks * n), BF16)],
        [near, far, places, mixed],
        4,
        3_000_000_000,
    )
    grad, refined, field, neutral = run(
        lambda *refs: cotangent_kernel(sizes, *refs),
        "cotangents",
        [
            held((n, channels), BF16),
            held((n, channels), F32),
            held((wide, 256), BF16),
            held((charge_ch, n), F32),
        ],
        [],
        [
            live,
            sums,
            part,
            far_part,
            places,
            far_places,
            charge,
            short,
            own_rows,
            w_long,
            energy_row,
            filt,
            *kept,
        ],
        12 + len(kept),
        3_000_000_000,
    )
    grad_line, grad = lax.optimization_barrier((gather_line(grad, sizes[2]), grad))
    updated, energy, force, lifted, planes, levels, *slopes = run(
        lambda *refs: own_kernel(sizes, *refs),
        "own_terms",
        [
            shape((n, channels), BF16),
            shape((1, n), F32),
            held((3, n), F32),
            held((bases * n, channels), BF16),
            held((256, 3 * n), BF16),
            held((16, n), F32),
        ]
        + ([held((bases * n, blocks * n), F32)] if fits else []),
        [pltpu.VMEM((bases * n, blocks * n), F32)],
        [
            grad,
            field,
            places,
            far_places,
            xcat,
            refined,
            mixed,
            w_long,
            energy_row,
        ],
        9,
        4_000_000_000,
    )
    grad_near, force, lifted = gather_cells(grad_line, sizes, (force, lifted))
    grad_far = from_other_core(grad_near)
    back, back_part = run(
        lambda *refs: pull_kernel(sizes, group, *refs),
        "pull_sums",
        [held((wide, 256), F32), held((wide, 256), BF16)],
        [],
        [grad_near, places, w_long, *kept],
        3 + len(kept),
        3_000_000_000,
    )
    far_back = from_other_core(back_part)
    (force,) = run(
        lambda *refs: react_kernel(sizes, *refs),
        "react",
        [held((3, n), F32)],
        [
            pltpu.VMEM((blocks * n, channels), BF16),
            pltpu.VMEM((bases * n, blocks * n), F32),
        ],
        [grad_near, grad_far, places, far_places, lifted, force, *slopes],
        6 + len(slopes),
        3_000_000_000,
    )
    (forces,) = run(
        lambda *refs: finish_kernel(sizes, *refs),
        "finish",
        [shape((3, 1, n), F32)],
        [pltpu.VMEM((wide, 256), BF16)],
        [back, far_back, planes, levels, neutral, force, filt],
        7,
        2_000_000_000,
    )
    return (
        updated[None, None, None],
        energy[None, None],
        forces.reshape(positions.shape),
    )


def solution(mesh):
    cell = ("gx", "gy", "gz")
    in_specs = (P(*cell, None, None), P(*cell, None, None), P(*cell)) + (P(),) * 8
    out_specs = (P(*cell, None, None), P(*cell, None), P(*cell, None, None))
    return jax.shard_map(shards, mesh=mesh, in_specs=in_specs, out_specs=out_specs, check_vma=False)
```

```python
import itertools
import math

import jax
import jax.numpy as jnp
import numpy as np
from jax import lax
from jax.experimental import pallas as pl
from jax.experimental.pallas import tpu as pltpu
from jax.sharding import PartitionSpec as P

CUTOFF = 0.9
SCALE = 1.0 / (CUTOFF * CUTOFF)
GAMMAS = (1.0, 3.0, 8.0, 20.0)
AXES = ("gx", "gy", "gz")
ORDERS = 7
NT = (((1,), (1,)), ((), ()))
F32 = jnp.float32
BF16 = jnp.bfloat16


def turn_series():
    nodes = np.cos(np.pi * (np.arange(200) + 0.5) / 200)
    r2 = (nodes + 1.0) / 8.0
    r = np.sqrt(r2)
    out = []
    for values in (np.cos(2 * np.pi * r), np.sin(2 * np.pi * r) / r):
        cheb = np.polynomial.chebyshev.Chebyshev.fit(r2, values, 6, domain=[0.0, 0.25])
        out.append([float(c) for c in cheb.convert(kind=np.polynomial.Polynomial).coef])
    return out


COS_SERIES, SIN_SERIES = turn_series()


def dot(a, b):
    return jnp.dot(a, b, preferred_element_type=F32)


def dot_nt(a, b):
    return lax.dot_general(a, b, NT, preferred_element_type=F32)


def sigmoid(v):
    return 1.0 / (1.0 + jnp.exp(-v))


def cos_sin(turns):
    r = turns - jnp.floor(turns + 0.5)
    r2 = r * r
    c = jnp.full_like(r2, COS_SERIES[-1])
    for coef in COS_SERIES[-2::-1]:
        c = c * r2 + coef
    s = jnp.full_like(r2, SIN_SERIES[-1])
    for coef in SIN_SERIES[-2::-1]:
        s = s * r2 + coef
    return c, s * r


def axis_tables(pos, anchor, sizes):
    order = lax.broadcasted_iota(jnp.int32, (8, pos.shape[1]), 0).astype(F32)
    tables = []
    for a in range(3):
        row = (pos[a : a + 1, :] + anchor[a]) * (1.0 / sizes[a])
        tables.append(cos_sin(order * row))
    return tables


def plane_table(first, second):
    rows = []
    for f in first:
        for s in second:
            for a in range(8):
                rows.append(f[a : a + 1, :] * s)
    return jnp.concatenate(rows, axis=0)


def derivative(table, size):
    order = lax.broadcasted_iota(jnp.int32, table[0].shape, 0).astype(F32) * (2.0 * math.pi / size)
    return (-order * table[1], order * table[0])


def spread(weights, third):
    rows = []
    for f in third:
        for c in range(ORDERS):
            rows.append((weights * f[c : c + 1, :]).astype(BF16))
    return jnp.concatenate(rows, axis=0)


def filtered(load, filt_ref, out_ref, charge_ch):
    shift = ORDERS * charge_ch
    for c in range(ORDERS):
        lo, hi = c * charge_ch, (c + 1) * charge_ch
        f0, gfb, fc, gfbc = (filt_ref[c, w * charge_ch : (w + 1) * charge_ch, :] for w in range(4))
        cos_part, sin_part = load(0, c), load(1, c)
        a_c, b_c = cos_part[:, 0:128], cos_part[:, 128:256]
        a_s, b_s = sin_part[:, 0:128], sin_part[:, 128:256]
        ra_c, rb_c, ra_s, rb_s = (pltpu.roll(v, 64, 1) for v in (a_c, b_c, a_s, b_s))
        out_ref[lo:hi, 0:128] = (f0 * a_c + gfbc * ra_s - fc * b_s + gfb * rb_c).astype(BF16)
        out_ref[lo:hi, 128:256] = (f0 * b_c - gfb * ra_c + fc * a_s + gfbc * rb_s).astype(BF16)
        out_ref[shift + lo : shift + hi, 0:128] = (
            f0 * a_s + fc * b_c - gfbc * ra_c + gfb * rb_s
        ).astype(BF16)
        out_ref[shift + lo : shift + hi, 128:256] = (
            f0 * b_s - fc * a_c - gfb * ra_s - gfbc * rb_c
        ).astype(BF16)


def slope_planes(tables, sizes):
    tx, ty, _ = tables
    return jnp.concatenate(
        [
            plane_table(derivative(tx, sizes[0]), ty).astype(BF16),
            plane_table(tx, derivative(ty, sizes[1])).astype(BF16),
            plane_table(tx, ty).astype(BF16),
        ],
        axis=1,
    )


def field_slope(field, planes, tz, sizes, weights, charge_ch):
    n = tz[0].shape[1]
    spread_field = dot(field, planes)
    slope_z = derivative(tz, sizes[2])
    total = [jnp.zeros((charge_ch, n), F32) for _ in range(3)]
    for kind in range(2):
        for c in range(ORDERS):
            lo = (kind * ORDERS + c) * charge_ch
            part = spread_field[lo : lo + charge_ch, :]
            zrow, drow = tz[kind][c : c + 1, :], slope_z[kind][c : c + 1, :]
            total[0] = total[0] + zrow * part[:, 0:n]
            total[1] = total[1] + zrow * part[:, n : 2 * n]
            total[2] = total[2] + drow * part[:, 2 * n : 3 * n]
    return [jnp.sum(t * weights, axis=0, keepdims=True) for t in total]


def place_of(m, half, sizes):
    nx, ny, nz = sizes
    dz = lax.rem(m, nz)
    dy = lax.rem(m // nz, ny)
    dx = m // (nz * ny)
    start = lax.axis_index(AXES[0]) if half == 0 else lax.axis_index(AXES[0]) + 1 - 2 * lax.rem(lax.axis_index(AXES[0]), 2)
    cx = lax.rem(start - 2 * dx + nx, nx)
    cy = lax.rem(lax.axis_index(AXES[1]) - dy + ny, ny)
    cz = lax.rem(lax.axis_index(AXES[2]) - dz + nz, nz)
    return (cx.astype(F32), cy.astype(F32), cz.astype(F32))


def blocks_of(sizes):
    options = [((0, False), (1, True)) if n == 2 else ((0, False), (-1, False), (1, False)) for n in sizes]
    return list(itertools.product(*options))


def offsets(own_cols, others, block):
    result = []
    for a, (step, nearest) in enumerate(block):
        if nearest:
            d = others[a] - own_cols[a]
            d = d - jnp.where(d > 0.0, 1.0, -1.0)
        else:
            d = (others[a] + float(step)) - own_cols[a]
        result.append(d)
    return result


def pair_terms(offs, block, first_row):
    s = (offs[0] * offs[0] + offs[1] * offs[1] + offs[2] * offs[2]) * SCALE
    u = jnp.maximum(1.0 - s, 0.0)
    if all(step == 0 for step, _ in block):
        rows = lax.broadcasted_iota(jnp.int32, s.shape, 0) + first_row
        cols = lax.broadcasted_iota(jnp.int32, s.shape, 1)
        u = jnp.where(rows == cols, 0.0, u)
    e1 = jnp.exp(-s)
    e2 = e1 * e1
    e3 = e2 * e1
    e4 = e2 * e2
    e8 = e4 * e4
    e20 = e8 * e8 * e4
    return u, (e1, e3, e8, e20)


def columns(pos, n):
    return [jnp.transpose(jnp.broadcast_to(pos[a : a + 1, :], (n, n))) for a in range(3)]


def fetch(sources, places, sems):
    copies = [pltpu.make_async_copy(s, p, sems.at[i]) for i, (s, p) in enumerate(zip(sources, places))]
    for c in copies:
        c.start()
    for c in copies:
        c.wait()


def pack_kernel(
    count_ref,
    features_hbm,
    positions_hbm,
    w_charge_hbm,
    bias_hbm,
    out_ref,
    slim_ref,
    live_ref,
    column_ref,
    features_ref,
    positions_ref,
    w_charge_ref,
    bias_ref,
    sems,
):
    fetch(
        (features_hbm, positions_hbm, w_charge_hbm, bias_hbm),
        (features_ref, positions_ref, w_charge_ref, bias_ref),
        sems,
    )
    n, channels = features_ref.shape
    live_col = lax.broadcasted_iota(jnp.int32, (n, channels), 0) < count_ref[0]
    live_ref[...] = live_col.astype(F32)
    rows = features_ref[...].astype(F32)
    out_ref[0:n, :] = jnp.where(live_col, rows, 0.0).astype(BF16)
    pos = jnp.concatenate([positions_ref[a] for a in range(3)], axis=0)
    coarse = pos.astype(BF16).astype(F32)
    fine = pos - coarse
    living = (lax.broadcasted_iota(jnp.int32, (1, n), 1) < count_ref[0]).astype(F32)
    blank = jnp.zeros((4, n), F32)
    tail = jnp.concatenate([coarse, living, blank, fine, jnp.zeros((5, n), F32)], axis=0)
    out_ref[n : n + 16, :] = tail.astype(BF16)
    charge_ch = w_charge_ref.shape[0]
    diagonal = lax.broadcasted_iota(jnp.int32, (charge_ch, charge_ch), 0) == (
        lax.broadcasted_iota(jnp.int32, (charge_ch, charge_ch), 1)
    )
    column = jnp.sum(jnp.where(diagonal, bias_ref[...], 0.0), axis=1, keepdims=True)
    column_ref[...] = jnp.broadcast_to(column, column_ref.shape)
    v = dot_nt(w_charge_ref[...], out_ref[0:n, :]) + column
    slim_ref[0:charge_ch, :] = (v * sigmoid(v) * living).astype(BF16)
    slim_ref[charge_ch : charge_ch + 16, :] = tail.astype(BF16)


def fold_kernel(
    scale,
    filter_hbm,
    index_hbm,
    energy_hbm,
    proj_hbm,
    mix_hbm,
    out_ref,
    row_ref,
    mixed_ref,
    filter_ref,
    index_ref,
    energy_ref,
    proj_ref,
    mix_ref,
    sems,
):
    fetch(
        (filter_hbm, index_hbm, energy_hbm, proj_hbm, mix_hbm),
        (filter_ref, index_ref, energy_ref, proj_ref, mix_ref),
        sems,
    )
    waves = filter_ref.shape[1]
    charge_ch = filter_ref.shape[0]
    row_ref[...] = energy_ref[...]
    mixed_ref[...] = dot(proj_ref[...], mix_ref[...]).astype(BF16)
    k = index_ref[...]
    positive = [jnp.where(k[a : a + 1, :] >= 0, 1.0, -1.0) for a in range(3)]
    sign_b = positive[0] * positive[1]
    sign_c = positive[0] * positive[2]
    size = jnp.abs(k)
    key = size[2:3, :] * 64 + size[0:1, :] * 8 + size[1:2, :]
    f = filter_ref[...] * scale
    stacked = jnp.concatenate([f, f * sign_b, f * sign_c, f * (sign_b * sign_c)], axis=0).astype(BF16)
    rows = lax.broadcasted_iota(jnp.int32, (ORDERS * 64, waves), 0)
    parts = dot_nt(stacked, jnp.where(rows == key, 1.0, 0.0).astype(BF16))
    turn = jnp.where(lax.broadcasted_iota(jnp.int32, (charge_ch, 128), 1) < 64, -1.0, 1.0)
    for c in range(ORDERS):
        part = parts[:, c * 64 : (c + 1) * 64]
        part = jnp.concatenate([part, part], axis=1)
        for w in range(4):
            piece = part[w * charge_ch : (w + 1) * charge_ch, :]
            out_ref[c, w * charge_ch : (w + 1) * charge_ch, :] = piece * turn if w % 2 == 1 else piece


def full_steps(nz):
    return sorted({0, 1 % nz, nz - 1})


def row_of(step, nz, full_rows, slim_rows):
    full = full_steps(nz)
    if step in full:
        return full.index(step) * full_rows
    return len(full) * full_rows + (step - 2) * slim_rows


def place_rows(ref, q, step, nz, n, charge_ch):
    lo = row_of(step, nz, n + 16, charge_ch + 16) + (n if step in full_steps(nz) else charge_ch)
    tail = ref[q, lo : lo + 16, :].astype(F32)
    return tail[0:8, :] + tail[8:16, :]


def block_place(sizes, odd, block):
    nx, ny, nz = sizes
    dy, dz = (-block[1][0]) % ny, (-block[2][0]) % nz
    if block[0][0] == 0:
        return 0, dy, dz
    dx = odd * (nx // 2 - 1) if block[0][0] == 1 else (1 - odd) * (1 % (nx // 2))
    return 1, dx * ny + dy, dz


def add_groups(structure, groups, sums_ref):
    if groups <= 4:
        total = structure(0)
        for g in range(1, groups):
            total = total + structure(g)
        sums_ref[...] = total
        return
    sums_ref[...] = structure(0)

    def add_structure(g, _):
        sums_ref[...] += structure(g)
        return 0

    lax.fori_loop(1, groups, add_structure, 0)


def charge_kernel(
    sizes,
    group,
    near_ref,
    w_charge_ref,
    bias_ref,
    sums_ref,
    part_ref,
    places_ref,
    charge_ref,
    *rest,
):
    *kept, charge_scr = rest
    charge_ch, channels = w_charge_ref.shape
    nz = sizes[2]
    n = places_ref.shape[2]
    wide = 2 * ORDERS * charge_ch
    groups = near_ref.shape[0] // group
    members = [(r, step) for r in range(group) for step in range(nz)]
    w_charge = w_charge_ref[...]
    bias = bias_ref[...]

    def add_charges(g, carry):
        total, live_total = carry
        for r, step in members:
            row = g * group + r
            m = row * nz + step
            pos = place_rows(near_ref, row, step, nz, n, charge_ch)
            places_ref[m] = pos
            live = pos[3:4, :]
            lo = row_of(step, nz, n + 16, charge_ch + 16)
            if step in full_steps(nz):
                v = dot_nt(w_charge, near_ref[row, lo : lo + n, :]) + bias
                q = v * sigmoid(v) * live
            else:
                q = near_ref[row, lo : lo + charge_ch, :].astype(F32)
            charge_scr[m] = q
            total = total + q
            live_total = live_total + live
        return total, live_total

    start = (jnp.zeros((charge_ch, n), F32), jnp.zeros((1, n), F32))
    if groups <= 4:
        for g in range(groups):
            start = add_charges(g, start)
        total, live_total = start
    else:
        total, live_total = lax.fori_loop(0, groups, add_charges, start)
    mean = jnp.sum(total, axis=1, keepdims=True) / jnp.sum(live_total, axis=1, keepdims=True)
    mean = mean.astype(BF16).astype(F32)
    charge_ref[...] = charge_scr[0]

    def structure(g):
        left, right = [], []
        for r, step in members:
            m = (g * group + r) * nz + step
            pos = places_ref[m]
            tx, ty, tz = axis_tables(pos, place_of(m, 0, sizes), sizes)
            live = pos[3:4, :]
            living = jnp.concatenate([tz[0] * live, tz[1] * live], axis=0).astype(BF16)
            plane = plane_table(tx, ty).astype(BF16)
            if kept:
                kept[0][m] = plane
                kept[1][m] = jnp.concatenate(tz, axis=0)
            left.append(
                jnp.concatenate([spread((charge_scr[m] - mean) * live, tz), living], axis=0)
            )
            right.append(plane)
        return dot_nt(jnp.concatenate(left, axis=1), jnp.concatenate(right, axis=1))

    add_groups(structure, groups, sums_ref)
    part_ref[0 : wide + 16, :] = sums_ref[...].astype(BF16)
    part_ref[wide + 16 : wide + 16 + charge_ch, :] = jnp.broadcast_to(mean, (charge_ch, 256)).astype(
        BF16
    )


def message_kernel(
    sizes,
    charge_ch,
    near_ref,
    far_ref,
    near_places_ref,
    mixed_ref,
    short_ref,
    far_places_ref,
    xcat_ref,
    radial_scr,
):
    n = short_ref.shape[0]
    nz = sizes[2]
    halves = (near_ref, far_ref)
    places = (near_places_ref, far_places_ref)

    def add_place(row, _):
        for step in range(nz):
            far_places_ref[row * nz + step] = place_rows(far_ref, row, step, nz, n, charge_ch)
        return 0

    lax.fori_loop(0, far_ref.shape[0], add_place, 0, unroll=min(4, far_ref.shape[0]))
    odd = lax.rem(lax.axis_index(AXES[0]), 2)
    own_cols = columns(near_places_ref[0], n)
    for t, block in enumerate(blocks_of(sizes)):
        half, row, step = block_place(sizes, odd, block)
        lo = row_of(step, nz, n + 16, 0)
        xcat_ref[t * n : (t + 1) * n, :] = halves[half][row, lo : lo + n, :]
        pos = places[half][row * nz + step]
        others = [pos[a : a + 1, :] for a in range(3)]
        for first in range(0, n, 32):
            cols = [c[first : first + 32, :] for c in own_cols]
            u, decays = pair_terms(offsets(cols, others, block), block, first)
            u2 = u * u
            for b in range(len(GAMMAS)):
                radial_scr[b * n + first : b * n + first + 32, t * n : (t + 1) * n] = (
                    decays[b] * u2
                ).astype(BF16)
    gathered = dot(radial_scr[...], xcat_ref[...]).astype(BF16)
    gathered = jnp.concatenate([gathered[b * n : (b + 1) * n, :] for b in range(len(GAMMAS))], axis=1)
    short_ref[...] = dot(gathered, mixed_ref[...])


def cotangent_kernel(
    sizes,
    live_ref,
    sums_ref,
    part_ref,
    far_part_ref,
    places_ref,
    far_places_ref,
    charge_ref,
    short_ref,
    features_ref,
    w_long_ref,
    w_energy_ref,
    filt_ref,
    *rest,
):
    *kept, grad_ref, pull_ref, refined_ref, field_ref, neutral_ref = rest
    n, channels = features_ref.shape
    charge_ch = w_long_ref.shape[0]
    wide = 2 * ORDERS * charge_ch
    own = places_ref[0]
    live_row = own[3:4, :]

    lives = [jnp.sum(r[...], axis=0)[3:4, :] for r in (places_ref, far_places_ref)]
    lives = [jnp.sum(v, axis=1, keepdims=True) for v in lives]
    tail = wide + 16
    bases = [r[tail : tail + charge_ch, 0:1].astype(F32) for r in (part_ref, far_part_ref)]
    rests = [sums_ref[0:charge_ch, 0:1], far_part_ref[0:charge_ch, 0:1].astype(F32)]
    mean = (bases[0] * lives[0] + rests[0] + bases[1] * lives[1] + rests[1]) / (lives[0] + lives[1])
    gaps = [b - mean for b in bases]
    far_living = far_part_ref[wide : wide + 16, :].astype(F32)

    def load(kind, c):
        lo = (kind * ORDERS + c) * charge_ch
        row = kind * 8 + c
        return (
            sums_ref[lo : lo + charge_ch, :]
            + far_part_ref[lo : lo + charge_ch, :].astype(F32)
            + gaps[0] * sums_ref[wide + row : wide + row + 1, :]
            + gaps[1] * far_living[row : row + 1, :]
        )

    filtered(load, filt_ref, field_ref, charge_ch)
    neutral_ref[...] = (charge_ref[...] - mean) * live_row
    if kept:
        plane = kept[0][0]
        tz = (kept[1][0, 0:8, :], kept[1][0, 8:16, :])
    else:
        tx, ty, tz = axis_tables(own, place_of(0, 0, sizes), sizes)
        plane = plane_table(tx, ty).astype(BF16)
    lifted = dot(field_ref[...], plane)
    potential = jnp.zeros((charge_ch, n), F32)
    for kind in range(2):
        for c in range(ORDERS):
            lo = (kind * ORDERS + c) * charge_ch
            potential = potential + tz[kind][c : c + 1, :] * lifted[lo : lo + charge_ch, :]
    pre_act = short_ref[...] + dot(jnp.transpose(potential).astype(BF16), w_long_ref[...])
    sig = sigmoid(pre_act)
    refined = features_ref[...].astype(F32) + pre_act * sig
    refined_ref[...] = refined
    sig_r = sigmoid(refined)
    grad = (
        w_energy_ref[...]
        * (sig_r * (1.0 + refined * (1.0 - sig_r)))
        * (sig * (1.0 + pre_act * (1.0 - sig)))
    )
    grad = (grad * live_ref[...]).astype(BF16)
    grad_ref[...] = grad
    pull_ref[...] = dot_nt(w_long_ref[...], grad).astype(BF16)


def pair_force(sizes, places, strengths_ref, n, slopes_to=None, slopes_from=None):
    own_cols = columns(places[0][0], n)
    odd = lax.rem(lax.axis_index(AXES[0]), 2)
    blocks = blocks_of(sizes)
    parts = [[], [], []]
    for first in range(0, n, 32):
        cols = [c[first : first + 32, :] for c in own_cols]
        acc = [jnp.zeros((32, n), F32) for _ in range(3)]
        for t, block in enumerate(blocks):
            half, row, step = block_place(sizes, odd, block)
            pos = places[half][row * sizes[2] + step]
            offs = offsets(cols, [pos[a : a + 1, :] for a in range(3)], block)
            if slopes_from is None:
                u, decays = pair_terms(offs, block, first)
            strength = jnp.zeros((32, n), F32)
            for b, g in enumerate(GAMMAS):
                lo = b * n + first
                part = strengths_ref[lo : lo + 32, t * n : (t + 1) * n]
                if slopes_from is None:
                    slope = decays[b] * (g * u + 2.0) * u
                else:
                    slope = slopes_from[lo : lo + 32, t * n : (t + 1) * n]
                if slopes_to is not None:
                    slopes_to[lo : lo + 32, t * n : (t + 1) * n] = slope
                strength = strength + slope * part
            for a in range(3):
                acc[a] = acc[a] + strength * offs[a]
        for a in range(3):
            parts[a].append(acc[a])
    return [
        (-2.0 * SCALE)
        * jnp.sum(jnp.transpose(jnp.concatenate(parts[a], axis=0)), axis=0, keepdims=True)
        for a in range(3)
    ]


def own_kernel(
    sizes,
    grad_ref,
    field_ref,
    places_ref,
    far_places_ref,
    xcat_ref,
    refined_ref,
    mixed_ref,
    w_long_ref,
    w_energy_ref,
    updated_ref,
    energy_ref,
    force_ref,
    lifted_ref,
    planes_ref,
    levels_ref,
    *rest,
):
    *slopes, strength_scr = rest
    n = grad_ref.shape[0]
    charge_ch = w_long_ref.shape[0]
    own = places_ref[0]
    refined = refined_ref[...]
    updated_ref[...] = refined.astype(BF16)
    energy_ref[...] = own[3:4, :] * jnp.sum(
        jnp.transpose(refined * sigmoid(refined) * w_energy_ref[...]), axis=0, keepdims=True
    )
    grad = grad_ref[...]
    channels = grad.shape[1]
    rows, lifted = [], []
    for b in range(len(GAMMAS)):
        mixed = mixed_ref[b * channels : (b + 1) * channels, :]
        rows.append(dot_nt(grad, mixed).astype(BF16))
        lifted.append(dot(xcat_ref[0:n, :], mixed).astype(BF16))
    lifted_ref[...] = jnp.concatenate(lifted, axis=0)
    strength_scr[...] = dot_nt(jnp.concatenate(rows, axis=0), xcat_ref[...])
    places = (places_ref, far_places_ref)
    near = pair_force(sizes, places, strength_scr, n, slopes[0] if slopes else None)
    pull = dot_nt(w_long_ref[...], grad)
    tables = axis_tables(own, place_of(0, 0, sizes), sizes)
    planes = slope_planes(tables, sizes)
    planes_ref[...] = planes
    levels_ref[...] = jnp.concatenate(tables[2], axis=0)
    slope = field_slope(field_ref[...], planes, tables[2], sizes, pull, charge_ch)
    force_ref[...] = jnp.concatenate([near[a] - slope[a] for a in range(3)], axis=0)


def pull_kernel(sizes, group, near_ref, places_ref, w_long_ref, *rest):
    *kept, sums_ref, part_ref = rest
    charge_ch = w_long_ref.shape[0]
    n = places_ref.shape[2]
    nz = sizes[2]
    whole = len(full_steps(nz)) * n
    groups = near_ref.shape[0] // group

    def structure(g):
        left, right = [], []
        rows = jnp.concatenate([near_ref[g * group + r, 0:whole, :] for r in range(group)], axis=0)
        pulls = dot_nt(w_long_ref[...], rows)
        for r in range(group):
            for step in range(nz):
                m = (g * group + r) * nz + step
                lo = row_of(step, nz, n, charge_ch)
                if step in full_steps(nz):
                    pull = pulls[:, r * whole + lo : r * whole + lo + n]
                else:
                    pull = near_ref[g * group + r, lo : lo + charge_ch, :].astype(F32)
                if kept:
                    tz = (kept[1][m, 0:8, :], kept[1][m, 8:16, :])
                    right.append(kept[0][m])
                else:
                    tx, ty, tz = axis_tables(places_ref[m], place_of(m, 0, sizes), sizes)
                    right.append(plane_table(tx, ty).astype(BF16))
                left.append(spread(pull, tz))
        return dot_nt(jnp.concatenate(left, axis=1), jnp.concatenate(right, axis=1))

    add_groups(structure, groups, sums_ref)
    part_ref[...] = sums_ref[...].astype(BF16)


def react_kernel(
    sizes,
    near_ref,
    far_ref,
    places_ref,
    far_places_ref,
    lifted_ref,
    force_ref,
    *rest,
):
    *slopes, out_ref, gcat_scr, strength_scr = rest
    n = force_ref.shape[1]
    halves = (near_ref, far_ref)
    odd = lax.rem(lax.axis_index(AXES[0]), 2)
    for t, block in enumerate(blocks_of(sizes)):
        half, row, step = block_place(sizes, odd, block)
        lo = row_of(step, sizes[2], n, 0)
        gcat_scr[t * n : (t + 1) * n, :] = halves[half][row, lo : lo + n, :]
    strength_scr[...] = dot_nt(lifted_ref[...], gcat_scr[...])
    places = (places_ref, far_places_ref)
    near = pair_force(sizes, places, strength_scr, n, None, slopes[0] if slopes else None)
    out_ref[...] = force_ref[...] + jnp.concatenate(near, axis=0)


def finish_kernel(
    sizes,
    sums_ref,
    far_part_ref,
    planes_ref,
    levels_ref,
    neutral_ref,
    force_ref,
    filt_ref,
    out_ref,
    field_scr,
):
    charge_ch = neutral_ref.shape[0]

    def load(kind, c):
        lo = (kind * ORDERS + c) * charge_ch
        return sums_ref[lo : lo + charge_ch, :] + far_part_ref[lo : lo + charge_ch, :].astype(F32)

    filtered(load, filt_ref, field_scr, charge_ch)
    tz = (levels_ref[0:8, :], levels_ref[8:16, :])
    slope = field_slope(field_scr[...], planes_ref[...], tz, sizes, neutral_ref[...], charge_ch)
    for a in range(3):
        out_ref[a] = force_ref[a : a + 1, :] - slope[a]


def gather_line(full, slim, nz):
    def moved(step):
        rows = full if step in full_steps(nz) else slim
        return lax.ppermute(rows, "gz", [(i, (i + step) % nz) for i in range(nz)])

    steps = sorted(range(1, nz), key=lambda step: step not in full_steps(nz))
    return jnp.concatenate([full] + [moved(step) for step in steps], axis=0)[None]


def gather_cells(value, sizes, beside):
    nx, ny, nz = sizes
    pairs = nx // 2

    def shifted(value, dx, dy):
        moves = []
        for i in range(nx):
            for j in range(ny):
                moves.append((i * ny + j, (i + 2 * dx) % nx * ny + (j + dy) % ny))
        return lax.ppermute(value, ("gx", "gy"), moves)

    if pairs * ny <= 4:
        steps = [(dx, dy) for dx in range(pairs) for dy in range(ny)]
        value = jnp.concatenate(
            [value] + [shifted(value, dx, dy) for dx, dy in steps[1:]], axis=0
        )
    else:
        value = jnp.concatenate([value] + [shifted(value, 0, dy) for dy in range(1, ny)], axis=0)
        value = jnp.concatenate([value] + [shifted(value, dx, 0) for dx in range(1, pairs)], axis=0)
    value, *beside = lax.optimization_barrier((value, *beside))
    return value, *beside


def from_other_core(value):
    return lax.ppermute(value, "gx", [(i, i ^ 1) for i in range(lax.axis_size("gx"))])


def call(kernel, name, outs, scratch, operands, kept, limit, flops, fetched):
    n_in = len(operands)
    first = n_in - kept
    operands = [
        pltpu.with_memory_space_constraint(o, pltpu.HBM if fetched else pltpu.VMEM)
        if (fetched and o.size > 1) or i >= first
        else o
        for i, o in enumerate(operands)
    ]
    specs = [
        pl.BlockSpec(
            memory_space=pltpu.SMEM if o.size == 1 else pltpu.HBM if fetched else pltpu.VMEM
        )
        for o in operands
    ]
    return pl.pallas_call(
        kernel,
        name=name,
        out_shape=outs,
        in_specs=specs,
        out_specs=[pl.BlockSpec(memory_space=pltpu.VMEM)] * len(outs),
        scratch_shapes=scratch,
        compiler_params=pltpu.CompilerParams(vmem_limit_bytes=limit),
        cost_estimate=pl.CostEstimate(flops=flops, bytes_accessed=2_000_000, transcendentals=0),
    )(*operands)


def shards(
    features,
    positions,
    counts,
    w_proj,
    w_mix,
    w_long,
    w_charge,
    charge_bias,
    w_energy,
    k_filter,
    k_index,
):
    own_rows = features[0, 0, 0]
    n, channels = own_rows.shape
    charge_ch = w_charge.shape[0]
    waves = k_index.shape[1]
    bases = w_proj.shape[0]
    sizes = tuple(lax.axis_size(a) for a in AXES)
    cells = sizes[0] * sizes[1] * sizes[2]
    half_cells = cells // 2
    lines = half_cells // sizes[2]
    group = 2 if sizes[2] <= 4 and lines % 2 == 0 else 1
    blocks = len(blocks_of(sizes))
    scale_long = 4.0 / math.sqrt(n * cells * waves)
    count = counts.reshape(1)
    shape = jax.ShapeDtypeStruct
    wide = 2 * ORDERS * charge_ch
    fits = cells <= 64
    limit = (24 if fits else 56) * 1024 * 1024
    held = pltpu.VMEM if fits else shape

    def run(kernel, name, outs, scratch, operands, kept, flops, fetched=False):
        kept = kept if fits else 0
        if fetched:
            places = [pltpu.VMEM(o.shape, o.dtype) for o in operands if o.size > 1]
            scratch = [*places, pltpu.SemaphoreType.DMA((len(places),))]
        return call(kernel, name, outs, scratch, operands, kept, limit, flops, fetched)

    packed, slim, live, bias = run(
        pack_kernel,
        "pack",
        [
            held((n + 16, channels), BF16),
            held((charge_ch + 16, n), BF16),
            held((n, channels), F32),
            held((charge_ch, n), F32),
        ],
        [],
        [count, own_rows, positions.reshape(3, 1, n), w_charge, charge_bias[None, :]],
        0,
        1000,
        fetched=True,
    )
    filt, energy_row, mixed = run(
        lambda *refs: fold_kernel(scale_long, *refs),
        "fold_filter",
        [
            held((ORDERS, 4 * charge_ch, 128), F32),
            held((1, channels), F32),
            held((bases * channels, channels), BF16),
        ],
        [],
        [
            k_filter,
            k_index,
            w_energy[None, :],
            w_proj.reshape(bases * channels, channels),
            w_mix,
        ],
        0,
        1_000_000_000,
        fetched=True,
    )
    line = gather_line(packed, slim, sizes[2])
    line, filt, energy_row, mixed = lax.optimization_barrier((line, filt, energy_row, mixed))
    (near,) = gather_cells(line, sizes, ())
    far = from_other_core(near)
    sums, part, places, charge, *kept = run(
        lambda *refs: charge_kernel(sizes, group, *refs),
        "charge_sums",
        [
            held((wide + 16, 256), F32),
            held((wide + 16 + charge_ch, 256), BF16),
            held((half_cells, 8, n), F32),
            held((charge_ch, n), F32),
        ]
        + ([held((half_cells, 256, n), BF16), held((half_cells, 16, n), F32)] if fits else []),
        [pltpu.VMEM((half_cells, charge_ch, n), F32)],
        [near, w_charge, bias],
        3,
        3_000_000_000,
    )
    far_part = from_other_core(part)
    short, far_places, xcat = run(
        lambda *refs: message_kernel(sizes, charge_ch, *refs),
        "message",
        [
            held((n, channels), F32),
            held((half_cells, 8, n), F32),
            held((blocks * n, channels), BF16),
        ],
        [pltpu.VMEM((bases * n, blocks * n), BF16)],
        [near, far, places, mixed],
        4,
        3_000_000_000,
    )
    grad, pull, refined, field, neutral = run(
        lambda *refs: cotangent_kernel(sizes, *refs),
        "cotangents",
        [
            held((n, channels), BF16),
            held((charge_ch, n), BF16),
            held((n, channels), F32),
            held((wide, 256), BF16),
            held((charge_ch, n), F32),
        ],
        [],
        [
            live,
            sums,
            part,
            far_part,
            places,
            far_places,
            charge,
            short,
            own_rows,
            w_long,
            energy_row,
            filt,
            *kept,
        ],
        12 + len(kept),
        3_000_000_000,
    )
    grad_line, grad = lax.optimization_barrier((gather_line(grad, pull, sizes[2]), grad))
    updated, energy, force, lifted, planes, levels, *slopes = run(
        lambda *refs: own_kernel(sizes, *refs),
        "own_terms",
        [
            shape((n, channels), BF16),
            shape((1, n), F32),
            held((3, n), F32),
            held((bases * n, channels), BF16),
            held((256, 3 * n), BF16),
            held((16, n), F32),
        ]
        + ([held((bases * n, blocks * n), F32)] if fits else []),
        [pltpu.VMEM((bases * n, blocks * n), F32)],
        [
            grad,
            field,
            places,
            far_places,
            xcat,
            refined,
            mixed,
            w_long,
            energy_row,
        ],
        9,
        4_000_000_000,
    )
    grad_near, force, lifted = gather_cells(grad_line, sizes, (force, lifted))
    grad_far = from_other_core(grad_near)
    back, back_part = run(
        lambda *refs: pull_kernel(sizes, group, *refs),
        "pull_sums",
        [held((wide, 256), F32), held((wide, 256), BF16)],
        [],
        [grad_near, places, w_long, *kept],
        3 + len(kept),
        3_000_000_000,
    )
    far_back = from_other_core(back_part)
    (force,) = run(
        lambda *refs: react_kernel(sizes, *refs),
        "react",
        [held((3, n), F32)],
        [
            pltpu.VMEM((blocks * n, channels), BF16),
            pltpu.VMEM((bases * n, blocks * n), F32),
        ],
        [grad_near, grad_far, places, far_places, lifted, force, *slopes],
        6 + len(slopes),
        3_000_000_000,
    )
    (forces,) = run(
        lambda *refs: finish_kernel(sizes, *refs),
        "finish",
        [shape((3, 1, n), F32)],
        [pltpu.VMEM((wide, 256), BF16)],
        [back, far_back, planes, levels, neutral, force, filt],
        7,
        2_000_000_000,
    )
    return (
        updated[None, None, None],
        energy[None, None],
        forces.reshape(positions.shape),
    )


def solution(mesh):
    cell = ("gx", "gy", "gz")
    in_specs = (P(*cell, None, None), P(*cell, None, None), P(*cell)) + (P(),) * 8
    out_specs = (P(*cell, None, None), P(*cell, None), P(*cell, None, None))
    return jax.shard_map(shards, mesh=mesh, in_specs=in_specs, out_specs=out_specs, check_vma=False)
```

```python
import itertools
import math

import jax
import jax.numpy as jnp
import numpy as np
from jax import lax
from jax.experimental import pallas as pl
from jax.experimental.pallas import tpu as pltpu
from jax.sharding import PartitionSpec as P

CUTOFF = 0.9
SCALE = 1.0 / (CUTOFF * CUTOFF)
GAMMAS = (1.0, 3.0, 8.0, 20.0)
AXES = ("gx", "gy", "gz")
ORDERS = 7
NT = (((1,), (1,)), ((), ()))
F32 = jnp.float32
BF16 = jnp.bfloat16


def turn_series():
    nodes = np.cos(np.pi * (np.arange(200) + 0.5) / 200)
    r2 = (nodes + 1.0) / 8.0
    r = np.sqrt(r2)
    out = []
    for values in (np.cos(2 * np.pi * r), np.sin(2 * np.pi * r) / r):
        cheb = np.polynomial.chebyshev.Chebyshev.fit(r2, values, 6, domain=[0.0, 0.25])
        out.append([float(c) for c in cheb.convert(kind=np.polynomial.Polynomial).coef])
    return out


COS_SERIES, SIN_SERIES = turn_series()


def dot(a, b):
    return jnp.dot(a, b, preferred_element_type=F32)


def dot_nt(a, b):
    return lax.dot_general(a, b, NT, preferred_element_type=F32)


def sigmoid(v):
    return 1.0 / (1.0 + jnp.exp(-v))


def cos_sin(turns):
    r = turns - jnp.floor(turns + 0.5)
    r2 = r * r
    c = jnp.full_like(r2, COS_SERIES[-1])
    for coef in COS_SERIES[-2::-1]:
        c = c * r2 + coef
    s = jnp.full_like(r2, SIN_SERIES[-1])
    for coef in SIN_SERIES[-2::-1]:
        s = s * r2 + coef
    return c, s * r


def axis_tables(pos, anchor, sizes):
    order = lax.broadcasted_iota(jnp.int32, (8, pos.shape[1]), 0).astype(F32)
    tables = []
    for a in range(3):
        row = (pos[a : a + 1, :] + anchor[a]) * (1.0 / sizes[a])
        tables.append(cos_sin(order * row))
    return tables


def plane_table(first, second):
    rows = []
    for f in first:
        for s in second:
            for a in range(8):
                rows.append(f[a : a + 1, :] * s)
    return jnp.concatenate(rows, axis=0)


def derivative(table, size):
    order = lax.broadcasted_iota(jnp.int32, table[0].shape, 0).astype(F32) * (2.0 * math.pi / size)
    return (-order * table[1], order * table[0])


def spread(weights, third):
    rows = []
    for f in third:
        for c in range(ORDERS):
            rows.append((weights * f[c : c + 1, :]).astype(BF16))
    return jnp.concatenate(rows, axis=0)


def filtered(load, filt_ref, out_ref, charge_ch):
    shift = ORDERS * charge_ch
    for c in range(ORDERS):
        lo, hi = c * charge_ch, (c + 1) * charge_ch
        f0, gfb, fc, gfbc = (filt_ref[c, w * charge_ch : (w + 1) * charge_ch, :] for w in range(4))
        cos_part, sin_part = load(0, c), load(1, c)
        a_c, b_c = cos_part[:, 0:128], cos_part[:, 128:256]
        a_s, b_s = sin_part[:, 0:128], sin_part[:, 128:256]
        ra_c, rb_c, ra_s, rb_s = (pltpu.roll(v, 64, 1) for v in (a_c, b_c, a_s, b_s))
        out_ref[lo:hi, 0:128] = (f0 * a_c + gfbc * ra_s - fc * b_s + gfb * rb_c).astype(BF16)
        out_ref[lo:hi, 128:256] = (f0 * b_c - gfb * ra_c + fc * a_s + gfbc * rb_s).astype(BF16)
        out_ref[shift + lo : shift + hi, 0:128] = (
            f0 * a_s + fc * b_c - gfbc * ra_c + gfb * rb_s
        ).astype(BF16)
        out_ref[shift + lo : shift + hi, 128:256] = (
            f0 * b_s - fc * a_c - gfb * ra_s - gfbc * rb_c
        ).astype(BF16)


def slope_planes(tables, sizes):
    tx, ty, _ = tables
    return jnp.concatenate(
        [
            plane_table(derivative(tx, sizes[0]), ty).astype(BF16),
            plane_table(tx, derivative(ty, sizes[1])).astype(BF16),
            plane_table(tx, ty).astype(BF16),
        ],
        axis=1,
    )


def field_slope(field, planes, tz, sizes, weights, charge_ch):
    n = tz[0].shape[1]
    spread_field = dot(field, planes)
    slope_z = derivative(tz, sizes[2])
    total = [jnp.zeros((charge_ch, n), F32) for _ in range(3)]
    for kind in range(2):
        for c in range(ORDERS):
            lo = (kind * ORDERS + c) * charge_ch
            part = spread_field[lo : lo + charge_ch, :]
            zrow, drow = tz[kind][c : c + 1, :], slope_z[kind][c : c + 1, :]
            total[0] = total[0] + zrow * part[:, 0:n]
            total[1] = total[1] + zrow * part[:, n : 2 * n]
            total[2] = total[2] + drow * part[:, 2 * n : 3 * n]
    return [jnp.sum(t * weights, axis=0, keepdims=True) for t in total]


def place_of(m, half, sizes):
    nx, ny, nz = sizes
    dz = lax.rem(m, nz)
    dy = lax.rem(m // nz, ny)
    dx = m // (nz * ny)
    start = lax.axis_index(AXES[0]) if half == 0 else lax.axis_index(AXES[0]) + 1 - 2 * lax.rem(lax.axis_index(AXES[0]), 2)
    cx = lax.rem(start - 2 * dx + nx, nx)
    cy = lax.rem(lax.axis_index(AXES[1]) - dy + ny, ny)
    cz = lax.rem(lax.axis_index(AXES[2]) - dz + nz, nz)
    return (cx.astype(F32), cy.astype(F32), cz.astype(F32))


def blocks_of(sizes):
    options = [((0, False), (1, True)) if n == 2 else ((0, False), (-1, False), (1, False)) for n in sizes]
    blocks = itertools.product(*options)
    return sorted(blocks, key=lambda block: block[0][0] != 0 or block[1][0] != 0)


def offsets(own_cols, others, block):
    result = []
    for a, (step, nearest) in enumerate(block):
        if nearest:
            d = others[a] - own_cols[a]
            d = d - jnp.where(d > 0.0, 1.0, -1.0)
        else:
            d = (others[a] + float(step)) - own_cols[a]
        result.append(d)
    return result


def pair_terms(offs, block, first_row):
    s = (offs[0] * offs[0] + offs[1] * offs[1] + offs[2] * offs[2]) * SCALE
    u = jnp.maximum(1.0 - s, 0.0)
    if all(step == 0 for step, _ in block):
        rows = lax.broadcasted_iota(jnp.int32, s.shape, 0) + first_row
        cols = lax.broadcasted_iota(jnp.int32, s.shape, 1)
        u = jnp.where(rows == cols, 0.0, u)
    e1 = jnp.exp(-s)
    e2 = e1 * e1
    e3 = e2 * e1
    e4 = e2 * e2
    e8 = e4 * e4
    e20 = e8 * e8 * e4
    return u, (e1, e3, e8, e20)


def columns(pos, n):
    return [jnp.transpose(jnp.broadcast_to(pos[a : a + 1, :], (n, n))) for a in range(3)]


def fetch(sources, places, sems):
    copies = [pltpu.make_async_copy(s, p, sems.at[i]) for i, (s, p) in enumerate(zip(sources, places))]
    for c in copies:
        c.start()
    for c in copies:
        c.wait()


def pack_kernel(
    count_ref,
    features_hbm,
    positions_hbm,
    w_charge_hbm,
    bias_hbm,
    out_ref,
    slim_ref,
    live_ref,
    column_ref,
    features_ref,
    positions_ref,
    w_charge_ref,
    bias_ref,
    sems,
):
    fetch(
        (features_hbm, positions_hbm, w_charge_hbm, bias_hbm),
        (features_ref, positions_ref, w_charge_ref, bias_ref),
        sems,
    )
    n, channels = features_ref.shape
    live_col = lax.broadcasted_iota(jnp.int32, (n, channels), 0) < count_ref[0]
    live_ref[...] = live_col.astype(F32)
    rows = features_ref[...].astype(F32)
    out_ref[0:n, :] = jnp.where(live_col, rows, 0.0).astype(BF16)
    pos = jnp.concatenate([positions_ref[a] for a in range(3)], axis=0)
    coarse = pos.astype(BF16).astype(F32)
    fine = pos - coarse
    living = (lax.broadcasted_iota(jnp.int32, (1, n), 1) < count_ref[0]).astype(F32)
    blank = jnp.zeros((4, n), F32)
    tail = jnp.concatenate([coarse, living, blank, fine, jnp.zeros((5, n), F32)], axis=0)
    out_ref[n : n + 16, :] = tail.astype(BF16)
    charge_ch = w_charge_ref.shape[0]
    diagonal = lax.broadcasted_iota(jnp.int32, (charge_ch, charge_ch), 0) == (
        lax.broadcasted_iota(jnp.int32, (charge_ch, charge_ch), 1)
    )
    column = jnp.sum(jnp.where(diagonal, bias_ref[...], 0.0), axis=1, keepdims=True)
    column_ref[...] = jnp.broadcast_to(column, column_ref.shape)
    v = dot_nt(w_charge_ref[...], out_ref[0:n, :]) + column
    slim_ref[0:charge_ch, :] = (v * sigmoid(v) * living).astype(BF16)
    slim_ref[charge_ch : charge_ch + 16, :] = tail.astype(BF16)


def fold_kernel(
    scale,
    filter_hbm,
    index_hbm,
    energy_hbm,
    proj_hbm,
    mix_hbm,
    out_ref,
    row_ref,
    mixed_ref,
    filter_ref,
    index_ref,
    energy_ref,
    proj_ref,
    mix_ref,
    sems,
):
    fetch(
        (filter_hbm, index_hbm, energy_hbm, proj_hbm, mix_hbm),
        (filter_ref, index_ref, energy_ref, proj_ref, mix_ref),
        sems,
    )
    waves = filter_ref.shape[1]
    charge_ch = filter_ref.shape[0]
    row_ref[...] = energy_ref[...]
    mixed_ref[...] = dot(proj_ref[...], mix_ref[...]).astype(BF16)
    k = index_ref[...]
    positive = [jnp.where(k[a : a + 1, :] >= 0, 1.0, -1.0) for a in range(3)]
    sign_b = positive[0] * positive[1]
    sign_c = positive[0] * positive[2]
    size = jnp.abs(k)
    key = size[2:3, :] * 64 + size[0:1, :] * 8 + size[1:2, :]
    f = filter_ref[...] * scale
    stacked = jnp.concatenate([f, f * sign_b, f * sign_c, f * (sign_b * sign_c)], axis=0).astype(BF16)
    rows = lax.broadcasted_iota(jnp.int32, (ORDERS * 64, waves), 0)
    parts = dot_nt(stacked, jnp.where(rows == key, 1.0, 0.0).astype(BF16))
    turn = jnp.where(lax.broadcasted_iota(jnp.int32, (charge_ch, 128), 1) < 64, -1.0, 1.0)
    for c in range(ORDERS):
        part = parts[:, c * 64 : (c + 1) * 64]
        part = jnp.concatenate([part, part], axis=1)
        for w in range(4):
            piece = part[w * charge_ch : (w + 1) * charge_ch, :]
            out_ref[c, w * charge_ch : (w + 1) * charge_ch, :] = piece * turn if w % 2 == 1 else piece


def full_steps(nz):
    return sorted({0, 1 % nz, nz - 1})


def row_of(step, nz, full_rows, slim_rows):
    full = full_steps(nz)
    if step in full:
        return full.index(step) * full_rows
    return len(full) * full_rows + (step - 2) * slim_rows


def place_rows(ref, q, step, nz, n, charge_ch):
    lo = row_of(step, nz, n + 16, charge_ch + 16) + (n if step in full_steps(nz) else charge_ch)
    tail = ref[q, lo : lo + 16, :].astype(F32)
    return tail[0:8, :] + tail[8:16, :]


def block_place(sizes, odd, block):
    nx, ny, nz = sizes
    dy, dz = (-block[1][0]) % ny, (-block[2][0]) % nz
    if block[0][0] == 0:
        return 0, dy, dz
    dx = odd * (nx // 2 - 1) if block[0][0] == 1 else (1 - odd) * (1 % (nx // 2))
    return 1, dx * ny + dy, dz


def add_groups(structure, rows, group, sums_ref, first_ref):
    steps = (rows - 1) // group
    if steps <= 4:
        total = first_ref[...]
        for g in range(steps):
            total = total + structure(1 + g * group)
        sums_ref[...] = total
        return
    sums_ref[...] = first_ref[...]

    def add_structure(g, _):
        sums_ref[...] += structure(1 + g * group)
        return 0

    lax.fori_loop(0, steps, add_structure, 0)


def cell_charges(ref, row, step, sizes, w_charge, bias, n):
    charge_ch = w_charge.shape[0]
    nz = sizes[2]
    pos = place_rows(ref, row, step, nz, n, charge_ch)
    lo = row_of(step, nz, n + 16, charge_ch + 16)
    if step in full_steps(nz):
        v = dot_nt(w_charge, ref[row, lo : lo + n, :]) + bias
        return pos, v * sigmoid(v) * pos[3:4, :]
    return pos, ref[row, lo : lo + charge_ch, :].astype(F32)


def charge_sides(pos, charge, m, sizes, base):
    tx, ty, tz = axis_tables(pos, place_of(m, 0, sizes), sizes)
    live = pos[3:4, :]
    living = jnp.concatenate([tz[0] * live, tz[1] * live], axis=0).astype(BF16)
    left = jnp.concatenate([spread((charge - base) * live, tz), living], axis=0)
    return left, plane_table(tx, ty).astype(BF16), jnp.concatenate(tz, axis=0)


def block_radials(pos, block, own_cols, store, n):
    others = [pos[a : a + 1, :] for a in range(3)]
    for first in range(0, n, 32):
        cols = [c[first : first + 32, :] for c in own_cols]
        u, decays = pair_terms(offsets(cols, others, block), block, first)
        u2 = u * u
        for b in range(len(GAMMAS)):
            store(b * n + first, (decays[b] * u2).astype(BF16))


def line_blocks(sizes):
    return [b for b in blocks_of(sizes) if b[0][0] == 0 and b[1][0] == 0]


def line_kernel(
    sizes,
    line_ref,
    w_charge_ref,
    bias_ref,
    sums_ref,
    base_ref,
    places_ref,
    charge_ref,
    gathered_ref,
    planes_ref,
    levels_ref,
    radial_scr,
    xcat_scr,
):
    nz = sizes[2]
    n = places_ref.shape[2]
    w_charge = w_charge_ref[...]
    bias = bias_ref[...]
    cells = [cell_charges(line_ref, 0, step, sizes, w_charge, bias, n) for step in range(nz)]
    charge_ref[...] = cells[0][1]
    total = sum(q for _, q in cells)
    lives = sum(pos[3:4, :] for pos, _ in cells)
    base = jnp.sum(total, axis=1, keepdims=True) / jnp.sum(lives, axis=1, keepdims=True)
    base = base.astype(BF16).astype(F32)
    base_ref[...] = jnp.broadcast_to(base, base_ref.shape)
    left, right = [], []
    for step, (pos, q) in enumerate(cells):
        places_ref[step] = pos
        side, plane, level = charge_sides(pos, q, step, sizes, base)
        planes_ref[step] = plane
        levels_ref[step] = level
        left.append(side)
        right.append(plane)
    sums_ref[...] = dot_nt(jnp.concatenate(left, axis=1), jnp.concatenate(right, axis=1))
    own_cols = columns(cells[0][0], n)
    for t, block in enumerate(line_blocks(sizes)):
        step = (-block[2][0]) % nz

        def store(row, value, t=t):
            radial_scr[row : row + 32, t * n : (t + 1) * n] = value

        block_radials(cells[step][0], block, own_cols, store, n)
        lo = row_of(step, nz, n + 16, 0)
        xcat_scr[t * n : (t + 1) * n, :] = line_ref[0, lo : lo + n, :]
    gathered_ref[...] = dot(radial_scr[...], xcat_scr[...])


def charge_kernel(
    sizes,
    group,
    near_ref,
    line_sums_ref,
    base_ref,
    line_places_ref,
    w_charge_ref,
    bias_ref,
    sums_ref,
    part_ref,
    places_ref,
    *kept,
):
    charge_ch, channels = w_charge_ref.shape
    nz = sizes[2]
    n = places_ref.shape[2]
    wide = 2 * ORDERS * charge_ch
    w_charge = w_charge_ref[...]
    bias = bias_ref[...]
    base = base_ref[...]
    places_ref[0:nz] = line_places_ref[...]

    def structure(row):
        left, right = [], []
        for r in range(group):
            for step in range(nz):
                pos, q = cell_charges(near_ref, row + r, step, sizes, w_charge, bias, n)
                m = (row + r) * nz + step
                places_ref[m] = pos
                side, plane, level = charge_sides(pos, q, m, sizes, base)
                if kept:
                    kept[0][m - nz] = plane
                    kept[1][m - nz] = level
                left.append(side)
                right.append(plane)
        return dot_nt(jnp.concatenate(left, axis=1), jnp.concatenate(right, axis=1))

    add_groups(structure, near_ref.shape[0], group, sums_ref, line_sums_ref)
    part_ref[0 : wide + 16, :] = sums_ref[...].astype(BF16)
    part_ref[wide + 16 : wide + 16 + charge_ch, :] = jnp.concatenate([base, base], axis=1).astype(BF16)


def message_kernel(
    sizes,
    charge_ch,
    near_ref,
    far_ref,
    near_places_ref,
    mixed_ref,
    line_gathered_ref,
    short_ref,
    far_places_ref,
    xcat_ref,
    radial_scr,
):
    n = short_ref.shape[0]
    nz = sizes[2]
    halves = (near_ref, far_ref)
    places = (near_places_ref, far_places_ref)

    def add_place(row, _):
        for step in range(nz):
            far_places_ref[row * nz + step] = place_rows(far_ref, row, step, nz, n, charge_ch)
        return 0

    lax.fori_loop(0, far_ref.shape[0], add_place, 0, unroll=min(4, far_ref.shape[0]))
    odd = lax.rem(lax.axis_index(AXES[0]), 2)
    own_cols = columns(near_places_ref[0], n)
    done = 0
    for t, block in enumerate(blocks_of(sizes)):
        half, row, step = block_place(sizes, odd, block)
        lo = row_of(step, nz, n + 16, 0)
        xcat_ref[t * n : (t + 1) * n, :] = halves[half][row, lo : lo + n, :]
        pos = places[half][row * nz + step]
        if block in line_blocks(sizes):
            continue

        def store(place, value, t=done):
            radial_scr[place : place + 32, t * n : (t + 1) * n] = value

        block_radials(pos, block, own_cols, store, n)
        done += 1
    rest = xcat_ref[len(line_blocks(sizes)) * n :, :]
    gathered = (line_gathered_ref[...] + dot(radial_scr[...], rest)).astype(BF16)
    gathered = jnp.concatenate([gathered[b * n : (b + 1) * n, :] for b in range(len(GAMMAS))], axis=1)
    short_ref[...] = dot(gathered, mixed_ref[...])


def cotangent_kernel(
    sizes,
    live_ref,
    sums_ref,
    part_ref,
    far_part_ref,
    places_ref,
    far_places_ref,
    charge_ref,
    short_ref,
    features_ref,
    w_long_ref,
    w_energy_ref,
    filt_ref,
    *rest,
):
    planes_ref, levels_ref, grad_ref, pull_ref, refined_ref, field_ref, neutral_ref = rest
    n, channels = features_ref.shape
    charge_ch = w_long_ref.shape[0]
    wide = 2 * ORDERS * charge_ch
    own = places_ref[0]
    live_row = own[3:4, :]

    lives = [jnp.sum(r[...], axis=0)[3:4, :] for r in (places_ref, far_places_ref)]
    lives = [jnp.sum(v, axis=1, keepdims=True) for v in lives]
    tail = wide + 16
    bases = [r[tail : tail + charge_ch, 0:1].astype(F32) for r in (part_ref, far_part_ref)]
    rests = [sums_ref[0:charge_ch, 0:1], far_part_ref[0:charge_ch, 0:1].astype(F32)]
    mean = (bases[0] * lives[0] + rests[0] + bases[1] * lives[1] + rests[1]) / (lives[0] + lives[1])
    gaps = [b - mean for b in bases]
    far_living = far_part_ref[wide : wide + 16, :].astype(F32)

    def load(kind, c):
        lo = (kind * ORDERS + c) * charge_ch
        row = kind * 8 + c
        return (
            sums_ref[lo : lo + charge_ch, :]
            + far_part_ref[lo : lo + charge_ch, :].astype(F32)
            + gaps[0] * sums_ref[wide + row : wide + row + 1, :]
            + gaps[1] * far_living[row : row + 1, :]
        )

    filtered(load, filt_ref, field_ref, charge_ch)
    neutral_ref[...] = (charge_ref[...] - mean) * live_row
    plane = planes_ref[0]
    tz = (levels_ref[0, 0:8, :], levels_ref[0, 8:16, :])
    lifted = dot(field_ref[...], plane)
    potential = jnp.zeros((charge_ch, n), F32)
    for kind in range(2):
        for c in range(ORDERS):
            lo = (kind * ORDERS + c) * charge_ch
            potential = potential + tz[kind][c : c + 1, :] * lifted[lo : lo + charge_ch, :]
    pre_act = short_ref[...] + dot(jnp.transpose(potential).astype(BF16), w_long_ref[...])
    sig = sigmoid(pre_act)
    refined = features_ref[...].astype(F32) + pre_act * sig
    refined_ref[...] = refined
    sig_r = sigmoid(refined)
    grad = (
        w_energy_ref[...]
        * (sig_r * (1.0 + refined * (1.0 - sig_r)))
        * (sig * (1.0 + pre_act * (1.0 - sig)))
    )
    grad = (grad * live_ref[...]).astype(BF16)
    grad_ref[...] = grad
    pull_ref[...] = dot_nt(w_long_ref[...], grad).astype(BF16)


def pair_force(sizes, places, strengths_ref, n, slopes_to=None, slopes_from=None):
    own_cols = columns(places[0][0], n)
    odd = lax.rem(lax.axis_index(AXES[0]), 2)
    blocks = blocks_of(sizes)
    parts = [[], [], []]
    for first in range(0, n, 32):
        cols = [c[first : first + 32, :] for c in own_cols]
        acc = [jnp.zeros((32, n), F32) for _ in range(3)]
        for t, block in enumerate(blocks):
            half, row, step = block_place(sizes, odd, block)
            pos = places[half][row * sizes[2] + step]
            offs = offsets(cols, [pos[a : a + 1, :] for a in range(3)], block)
            if slopes_from is None:
                u, decays = pair_terms(offs, block, first)
            strength = jnp.zeros((32, n), F32)
            for b, g in enumerate(GAMMAS):
                lo = b * n + first
                part = strengths_ref[lo : lo + 32, t * n : (t + 1) * n]
                if slopes_from is None:
                    slope = decays[b] * (g * u + 2.0) * u
                else:
                    slope = slopes_from[lo : lo + 32, t * n : (t + 1) * n]
                if slopes_to is not None:
                    slopes_to[lo : lo + 32, t * n : (t + 1) * n] = slope
                strength = strength + slope * part
            for a in range(3):
                acc[a] = acc[a] + strength * offs[a]
        for a in range(3):
            parts[a].append(acc[a])
    return [
        (-2.0 * SCALE)
        * jnp.sum(jnp.transpose(jnp.concatenate(parts[a], axis=0)), axis=0, keepdims=True)
        for a in range(3)
    ]


def own_kernel(
    sizes,
    grad_ref,
    field_ref,
    places_ref,
    far_places_ref,
    xcat_ref,
    refined_ref,
    mixed_ref,
    w_long_ref,
    w_energy_ref,
    updated_ref,
    energy_ref,
    force_ref,
    lifted_ref,
    planes_ref,
    levels_ref,
    *rest,
):
    *slopes, strength_scr = rest
    n = grad_ref.shape[0]
    charge_ch = w_long_ref.shape[0]
    own = places_ref[0]
    refined = refined_ref[...]
    updated_ref[...] = refined.astype(BF16)
    energy_ref[...] = own[3:4, :] * jnp.sum(
        jnp.transpose(refined * sigmoid(refined) * w_energy_ref[...]), axis=0, keepdims=True
    )
    grad = grad_ref[...]
    channels = grad.shape[1]
    rows, lifted = [], []
    for b in range(len(GAMMAS)):
        mixed = mixed_ref[b * channels : (b + 1) * channels, :]
        rows.append(dot_nt(grad, mixed).astype(BF16))
        lifted.append(dot(xcat_ref[0:n, :], mixed).astype(BF16))
    lifted_ref[...] = jnp.concatenate(lifted, axis=0)
    strength_scr[...] = dot_nt(jnp.concatenate(rows, axis=0), xcat_ref[...])
    places = (places_ref, far_places_ref)
    near = pair_force(sizes, places, strength_scr, n, slopes[0] if slopes else None)
    pull = dot_nt(w_long_ref[...], grad)
    tables = axis_tables(own, place_of(0, 0, sizes), sizes)
    planes = slope_planes(tables, sizes)
    planes_ref[...] = planes
    levels_ref[...] = jnp.concatenate(tables[2], axis=0)
    slope = field_slope(field_ref[...], planes, tables[2], sizes, pull, charge_ch)
    force_ref[...] = jnp.concatenate([near[a] - slope[a] for a in range(3)], axis=0)


def pull_sides(ref, row, sizes, w_long, tables, n):
    charge_ch = w_long.shape[0]
    nz = sizes[2]
    pulls = dot_nt(w_long, ref[row, 0 : len(full_steps(nz)) * n, :])
    left, right = [], []
    for step in range(nz):
        lo = row_of(step, nz, n, charge_ch)
        if step in full_steps(nz):
            pull = pulls[:, lo : lo + n]
        else:
            pull = ref[row, lo : lo + charge_ch, :].astype(F32)
        plane, tz = tables(row, step)
        left.append(spread(pull, tz))
        right.append(plane)
    return left, right


def line_pull_kernel(sizes, line_ref, planes_ref, levels_ref, w_long_ref, sums_ref):
    n = levels_ref.shape[2]

    def tables(row, step):
        return planes_ref[step], (levels_ref[step, 0:8, :], levels_ref[step, 8:16, :])

    left, right = pull_sides(line_ref, 0, sizes, w_long_ref[...], tables, n)
    sums_ref[...] = dot_nt(jnp.concatenate(left, axis=1), jnp.concatenate(right, axis=1))


def pull_kernel(sizes, group, near_ref, line_sums_ref, places_ref, w_long_ref, *rest):
    *kept, sums_ref, part_ref = rest
    nz = sizes[2]
    n = places_ref.shape[2]

    def tables(row, step):
        m = row * nz + step
        if kept:
            return kept[0][m - nz], (kept[1][m - nz, 0:8, :], kept[1][m - nz, 8:16, :])
        tx, ty, tz = axis_tables(places_ref[m], place_of(m, 0, sizes), sizes)
        return plane_table(tx, ty).astype(BF16), tz

    def structure(row):
        left, right = [], []
        for r in range(group):
            sides = pull_sides(near_ref, row + r, sizes, w_long_ref[...], tables, n)
            left += sides[0]
            right += sides[1]
        return dot_nt(jnp.concatenate(left, axis=1), jnp.concatenate(right, axis=1))

    add_groups(structure, near_ref.shape[0], group, sums_ref, line_sums_ref)
    part_ref[...] = sums_ref[...].astype(BF16)


def react_kernel(
    sizes,
    near_ref,
    far_ref,
    places_ref,
    far_places_ref,
    lifted_ref,
    force_ref,
    *rest,
):
    *slopes, out_ref, gcat_scr, strength_scr = rest
    n = force_ref.shape[1]
    halves = (near_ref, far_ref)
    odd = lax.rem(lax.axis_index(AXES[0]), 2)
    for t, block in enumerate(blocks_of(sizes)):
        half, row, step = block_place(sizes, odd, block)
        lo = row_of(step, sizes[2], n, 0)
        gcat_scr[t * n : (t + 1) * n, :] = halves[half][row, lo : lo + n, :]
    strength_scr[...] = dot_nt(lifted_ref[...], gcat_scr[...])
    places = (places_ref, far_places_ref)
    near = pair_force(sizes, places, strength_scr, n, None, slopes[0] if slopes else None)
    out_ref[...] = force_ref[...] + jnp.concatenate(near, axis=0)


def finish_kernel(
    sizes,
    sums_ref,
    far_part_ref,
    planes_ref,
    levels_ref,
    neutral_ref,
    force_ref,
    filt_ref,
    out_ref,
    field_scr,
):
    charge_ch = neutral_ref.shape[0]

    def load(kind, c):
        lo = (kind * ORDERS + c) * charge_ch
        return sums_ref[lo : lo + charge_ch, :] + far_part_ref[lo : lo + charge_ch, :].astype(F32)

    filtered(load, filt_ref, field_scr, charge_ch)
    tz = (levels_ref[0:8, :], levels_ref[8:16, :])
    slope = field_slope(field_scr[...], planes_ref[...], tz, sizes, neutral_ref[...], charge_ch)
    for a in range(3):
        out_ref[a] = force_ref[a : a + 1, :] - slope[a]


def gather_line(full, slim, nz):
    def moved(step):
        rows = full if step in full_steps(nz) else slim
        return lax.ppermute(rows, "gz", [(i, (i + step) % nz) for i in range(nz)])

    steps = sorted(range(1, nz), key=lambda step: step not in full_steps(nz))
    return jnp.concatenate([full] + [moved(step) for step in steps], axis=0)[None]


def gather_cells(value, sizes, beside):
    nx, ny, nz = sizes
    pairs = nx // 2

    def shifted(value, dx, dy):
        moves = []
        for i in range(nx):
            for j in range(ny):
                moves.append((i * ny + j, (i + 2 * dx) % nx * ny + (j + dy) % ny))
        return lax.ppermute(value, ("gx", "gy"), moves)

    if pairs * ny <= 4:
        steps = [(dx, dy) for dx in range(pairs) for dy in range(ny)]
        value = jnp.concatenate(
            [value] + [shifted(value, dx, dy) for dx, dy in steps[1:]], axis=0
        )
    else:
        value = jnp.concatenate([value] + [shifted(value, 0, dy) for dy in range(1, ny)], axis=0)
        value = jnp.concatenate([value] + [shifted(value, dx, 0) for dx in range(1, pairs)], axis=0)
    value, *beside = lax.optimization_barrier((value, *beside))
    return value, *beside


def from_other_core(value):
    return lax.ppermute(value, "gx", [(i, i ^ 1) for i in range(lax.axis_size("gx"))])


def call(kernel, name, outs, scratch, operands, kept, limit, flops, fetched):
    n_in = len(operands)
    first = n_in - kept
    operands = [
        pltpu.with_memory_space_constraint(o, pltpu.HBM if fetched else pltpu.VMEM)
        if (fetched and o.size > 1) or i >= first
        else o
        for i, o in enumerate(operands)
    ]
    specs = [
        pl.BlockSpec(
            memory_space=pltpu.SMEM if o.size == 1 else pltpu.HBM if fetched else pltpu.VMEM
        )
        for o in operands
    ]
    return pl.pallas_call(
        kernel,
        name=name,
        out_shape=outs,
        in_specs=specs,
        out_specs=[pl.BlockSpec(memory_space=pltpu.VMEM)] * len(outs),
        scratch_shapes=scratch,
        compiler_params=pltpu.CompilerParams(vmem_limit_bytes=limit),
        cost_estimate=pl.CostEstimate(flops=flops, bytes_accessed=2_000_000, transcendentals=0),
    )(*operands)


def shards(
    features,
    positions,
    counts,
    w_proj,
    w_mix,
    w_long,
    w_charge,
    charge_bias,
    w_energy,
    k_filter,
    k_index,
):
    own_rows = features[0, 0, 0]
    n, channels = own_rows.shape
    charge_ch = w_charge.shape[0]
    waves = k_index.shape[1]
    bases = w_proj.shape[0]
    sizes = tuple(lax.axis_size(a) for a in AXES)
    cells = sizes[0] * sizes[1] * sizes[2]
    half_cells = cells // 2
    lines = half_cells // sizes[2]
    group = lines - 1 if cells <= 32 else 1
    near_line = len(line_blocks(sizes))
    blocks = len(blocks_of(sizes))
    scale_long = 4.0 / math.sqrt(n * cells * waves)
    count = counts.reshape(1)
    shape = jax.ShapeDtypeStruct
    wide = 2 * ORDERS * charge_ch
    fits = cells <= 64
    limit = (24 if fits else 56) * 1024 * 1024
    held = pltpu.VMEM if fits else shape

    def run(kernel, name, outs, scratch, operands, kept, flops, fetched=False):
        kept = kept if fits else 0
        if fetched:
            places = [pltpu.VMEM(o.shape, o.dtype) for o in operands if o.size > 1]
            scratch = [*places, pltpu.SemaphoreType.DMA((len(places),))]
        return call(kernel, name, outs, scratch, operands, kept, limit, flops, fetched)

    packed, slim, live, bias = run(
        pack_kernel,
        "pack",
        [
            held((n + 16, channels), BF16),
            held((charge_ch + 16, n), BF16),
            held((n, channels), F32),
            held((charge_ch, n), F32),
        ],
        [],
        [count, own_rows, positions.reshape(3, 1, n), w_charge, charge_bias[None, :]],
        0,
        1000,
        fetched=True,
    )
    filt, energy_row, mixed = run(
        lambda *refs: fold_kernel(scale_long, *refs),
        "fold_filter",
        [
            held((ORDERS, 4 * charge_ch, 128), F32),
            held((1, channels), F32),
            held((bases * channels, channels), BF16),
        ],
        [],
        [
            k_filter,
            k_index,
            w_energy[None, :],
            w_proj.reshape(bases * channels, channels),
            w_mix,
        ],
        0,
        1_000_000_000,
        fetched=True,
    )
    line = gather_line(packed, slim, sizes[2])
    line, filt, energy_row, mixed = lax.optimization_barrier((line, filt, energy_row, mixed))
    line_sums, base, line_places, charge, line_gathered, line_planes, line_levels = run(
        lambda *refs: line_kernel(sizes, *refs),
        "line_sums",
        [
            held((wide + 16, 256), F32),
            held((charge_ch, n), F32),
            held((sizes[2], 8, n), F32),
            held((charge_ch, n), F32),
            held((bases * n, channels), F32),
            held((sizes[2], 256, n), BF16),
            held((sizes[2], 16, n), F32),
        ],
        [
            pltpu.VMEM((bases * n, near_line * n), BF16),
            pltpu.VMEM((near_line * n, channels), BF16),
        ],
        [line, w_charge, bias],
        3,
        1_000_000_000,
    )
    near, line_sums = gather_cells(line, sizes, (line_sums,))
    far = from_other_core(near)
    sums, part, places, *kept = run(
        lambda *refs: charge_kernel(sizes, group, *refs),
        "charge_sums",
        [
            held((wide + 16, 256), F32),
            held((wide + 16 + charge_ch, 256), BF16),
            held((half_cells, 8, n), F32),
        ]
        + (
            [
                held((half_cells - sizes[2], 256, n), BF16),
                held((half_cells - sizes[2], 16, n), F32),
            ]
            if fits
            else []
        ),
        [],
        [near, line_sums, base, line_places, w_charge, bias],
        6,
        3_000_000_000,
    )
    far_part = from_other_core(part)
    short, far_places, xcat = run(
        lambda *refs: message_kernel(sizes, charge_ch, *refs),
        "message",
        [
            held((n, channels), F32),
            held((half_cells, 8, n), F32),
            held((blocks * n, channels), BF16),
        ],
        [pltpu.VMEM((bases * n, (blocks - near_line) * n), BF16)],
        [near, far, places, mixed, line_gathered],
        5,
        3_000_000_000,
    )
    grad, pull, refined, field, neutral = run(
        lambda *refs: cotangent_kernel(sizes, *refs),
        "cotangents",
        [
            held((n, channels), BF16),
            held((charge_ch, n), BF16),
            held((n, channels), F32),
            held((wide, 256), BF16),
            held((charge_ch, n), F32),
        ],
        [],
        [
            live,
            sums,
            part,
            far_part,
            places,
            far_places,
            charge,
            short,
            own_rows,
            w_long,
            energy_row,
            filt,
            line_planes,
            line_levels,
        ],
        14,
        3_000_000_000,
    )
    grad_line, grad = lax.optimization_barrier((gather_line(grad, pull, sizes[2]), grad))
    updated, energy, force, lifted, planes, levels, *slopes = run(
        lambda *refs: own_kernel(sizes, *refs),
        "own_terms",
        [
            shape((n, channels), BF16),
            shape((1, n), F32),
            held((3, n), F32),
            held((bases * n, channels), BF16),
            held((256, 3 * n), BF16),
            held((16, n), F32),
        ]
        + ([held((bases * n, blocks * n), F32)] if fits else []),
        [pltpu.VMEM((bases * n, blocks * n), F32)],
        [
            grad,
            field,
            places,
            far_places,
            xcat,
            refined,
            mixed,
            w_long,
            energy_row,
        ],
        9,
        4_000_000_000,
    )
    (line_back,) = run(
        lambda *refs: line_pull_kernel(sizes, *refs),
        "line_pulls",
        [held((wide, 256), F32)],
        [],
        [grad_line, line_planes, line_levels, w_long],
        4,
        1_000_000_000,
    )
    grad_near, force, lifted, line_back = gather_cells(grad_line, sizes, (force, lifted, line_back))
    grad_far = from_other_core(grad_near)
    back, back_part = run(
        lambda *refs: pull_kernel(sizes, group, *refs),
        "pull_sums",
        [held((wide, 256), F32), held((wide, 256), BF16)],
        [],
        [grad_near, line_back, places, w_long, *kept],
        4 + len(kept),
        3_000_000_000,
    )
    far_back = from_other_core(back_part)
    (force,) = run(
        lambda *refs: react_kernel(sizes, *refs),
        "react",
        [held((3, n), F32)],
        [
            pltpu.VMEM((blocks * n, channels), BF16),
            pltpu.VMEM((bases * n, blocks * n), F32),
        ],
        [grad_near, grad_far, places, far_places, lifted, force, *slopes],
        6 + len(slopes),
        3_000_000_000,
    )
    (forces,) = run(
        lambda *refs: finish_kernel(sizes, *refs),
        "finish",
        [shape((3, 1, n), F32)],
        [pltpu.VMEM((wide, 256), BF16)],
        [back, far_back, planes, levels, neutral, force, filt],
        7,
        2_000_000_000,
    )
    return (
        updated[None, None, None],
        energy[None, None],
        forces.reshape(positions.shape),
    )


def solution(mesh):
    cell = ("gx", "gy", "gz")
    in_specs = (P(*cell, None, None), P(*cell, None, None), P(*cell)) + (P(),) * 8
    out_specs = (P(*cell, None, None), P(*cell, None), P(*cell, None, None))
    return jax.shard_map(shards, mesh=mesh, in_specs=in_specs, out_specs=out_specs, check_vma=False)
```

```python
import itertools
import math

import jax
import jax.numpy as jnp
import numpy as np
from jax import lax
from jax.experimental import pallas as pl
from jax.experimental.pallas import tpu as pltpu
from jax.sharding import PartitionSpec as P

CUTOFF = 0.9
SCALE = 1.0 / (CUTOFF * CUTOFF)
GAMMAS = (1.0, 3.0, 8.0, 20.0)
AXES = ("gx", "gy", "gz")
ORDERS = 7
NT = (((1,), (1,)), ((), ()))
F32 = jnp.float32
BF16 = jnp.bfloat16


def turn_series():
    nodes = np.cos(np.pi * (np.arange(200) + 0.5) / 200)
    r2 = (nodes + 1.0) / 8.0
    r = np.sqrt(r2)
    out = []
    for values in (np.cos(2 * np.pi * r), np.sin(2 * np.pi * r) / r):
        cheb = np.polynomial.chebyshev.Chebyshev.fit(r2, values, 6, domain=[0.0, 0.25])
        out.append([float(c) for c in cheb.convert(kind=np.polynomial.Polynomial).coef])
    return out


COS_SERIES, SIN_SERIES = turn_series()


def dot(a, b):
    return jnp.dot(a, b, preferred_element_type=F32)


def dot_nt(a, b):
    return lax.dot_general(a, b, NT, preferred_element_type=F32)


def sigmoid(v):
    return 1.0 / (1.0 + jnp.exp(-v))


def cos_sin(turns):
    r = turns - jnp.floor(turns + 0.5)
    r2 = r * r
    c = jnp.full_like(r2, COS_SERIES[-1])
    for coef in COS_SERIES[-2::-1]:
        c = c * r2 + coef
    s = jnp.full_like(r2, SIN_SERIES[-1])
    for coef in SIN_SERIES[-2::-1]:
        s = s * r2 + coef
    return c, s * r


def axis_tables(pos, anchor, sizes):
    order = lax.broadcasted_iota(jnp.int32, (8, pos.shape[1]), 0).astype(F32)
    tables = []
    for a in range(3):
        row = (pos[a : a + 1, :] + anchor[a]) * (1.0 / sizes[a])
        tables.append(cos_sin(order * row))
    return tables


def plane_table(first, second):
    rows = []
    for f in first:
        for s in second:
            for a in range(8):
                rows.append(f[a : a + 1, :] * s)
    return jnp.concatenate(rows, axis=0)


def derivative(table, size):
    order = lax.broadcasted_iota(jnp.int32, table[0].shape, 0).astype(F32) * (2.0 * math.pi / size)
    return (-order * table[1], order * table[0])


def spread(weights, third):
    rows = []
    for f in third:
        for c in range(ORDERS):
            rows.append((weights * f[c : c + 1, :]).astype(BF16))
    return jnp.concatenate(rows, axis=0)


def filtered(load, filt_ref, out_ref, charge_ch):
    shift = ORDERS * charge_ch
    for c in range(ORDERS):
        lo, hi = c * charge_ch, (c + 1) * charge_ch
        f0, gfb, fc, gfbc = (filt_ref[c, w * charge_ch : (w + 1) * charge_ch, :] for w in range(4))
        cos_part, sin_part = load(0, c), load(1, c)
        a_c, b_c = cos_part[:, 0:128], cos_part[:, 128:256]
        a_s, b_s = sin_part[:, 0:128], sin_part[:, 128:256]
        ra_c, rb_c, ra_s, rb_s = (pltpu.roll(v, 64, 1) for v in (a_c, b_c, a_s, b_s))
        out_ref[lo:hi, 0:128] = (f0 * a_c + gfbc * ra_s - fc * b_s + gfb * rb_c).astype(BF16)
        out_ref[lo:hi, 128:256] = (f0 * b_c - gfb * ra_c + fc * a_s + gfbc * rb_s).astype(BF16)
        out_ref[shift + lo : shift + hi, 0:128] = (
            f0 * a_s + fc * b_c - gfbc * ra_c + gfb * rb_s
        ).astype(BF16)
        out_ref[shift + lo : shift + hi, 128:256] = (
            f0 * b_s - fc * a_c - gfb * ra_s - gfbc * rb_c
        ).astype(BF16)


def slope_planes(tables, sizes):
    tx, ty, _ = tables
    return jnp.concatenate(
        [
            plane_table(derivative(tx, sizes[0]), ty).astype(BF16),
            plane_table(tx, derivative(ty, sizes[1])).astype(BF16),
            plane_table(tx, ty).astype(BF16),
        ],
        axis=1,
    )


def field_slope(field, planes, tz, sizes, weights, charge_ch):
    n = tz[0].shape[1]
    spread_field = dot(field, planes)
    slope_z = derivative(tz, sizes[2])
    total = [jnp.zeros((charge_ch, n), F32) for _ in range(3)]
    for kind in range(2):
        for c in range(ORDERS):
            lo = (kind * ORDERS + c) * charge_ch
            part = spread_field[lo : lo + charge_ch, :]
            zrow, drow = tz[kind][c : c + 1, :], slope_z[kind][c : c + 1, :]
            total[0] = total[0] + zrow * part[:, 0:n]
            total[1] = total[1] + zrow * part[:, n : 2 * n]
            total[2] = total[2] + drow * part[:, 2 * n : 3 * n]
    return [jnp.sum(t * weights, axis=0, keepdims=True) for t in total]


def place_of(m, half, sizes):
    nx, ny, nz = sizes
    dz = lax.rem(m, nz)
    dy = lax.rem(m // nz, ny)
    dx = m // (nz * ny)
    start = lax.axis_index(AXES[0]) if half == 0 else lax.axis_index(AXES[0]) + 1 - 2 * lax.rem(lax.axis_index(AXES[0]), 2)
    cx = lax.rem(start - 2 * dx + nx, nx)
    cy = lax.rem(lax.axis_index(AXES[1]) - dy + ny, ny)
    z = lax.axis_index(AXES[2])
    cz = jnp.bitwise_xor(z, dz) if in_pairs(nz) else lax.rem(z - dz + nz, nz)
    return (cx.astype(F32), cy.astype(F32), cz.astype(F32))


def blocks_of(sizes):
    options = [((0, False), (1, True)) if n == 2 else ((0, False), (-1, False), (1, False)) for n in sizes]
    blocks = itertools.product(*options)
    return sorted(blocks, key=lambda block: block[0][0] != 0 or block[1][0] != 0)


def offsets(own_cols, others, block):
    result = []
    for a, (step, nearest) in enumerate(block):
        if nearest:
            d = others[a] - own_cols[a]
            d = d - jnp.where(d > 0.0, 1.0, -1.0)
        else:
            d = (others[a] + float(step)) - own_cols[a]
        result.append(d)
    return result


def pair_terms(offs, block, first_row):
    s = (offs[0] * offs[0] + offs[1] * offs[1] + offs[2] * offs[2]) * SCALE
    u = jnp.maximum(1.0 - s, 0.0)
    if all(step == 0 for step, _ in block):
        rows = lax.broadcasted_iota(jnp.int32, s.shape, 0) + first_row
        cols = lax.broadcasted_iota(jnp.int32, s.shape, 1)
        u = jnp.where(rows == cols, 0.0, u)
    e1 = jnp.exp(-s)
    e2 = e1 * e1
    e3 = e2 * e1
    e4 = e2 * e2
    e8 = e4 * e4
    e20 = e8 * e8 * e4
    return u, (e1, e3, e8, e20)


def columns(pos, n):
    return [jnp.transpose(jnp.broadcast_to(pos[a : a + 1, :], (n, n))) for a in range(3)]


def fetch(sources, places, sems):
    copies = [pltpu.make_async_copy(s, p, sems.at[i]) for i, (s, p) in enumerate(zip(sources, places))]
    for c in copies:
        c.start()
    for c in copies:
        c.wait()


def pack_kernel(
    count_ref,
    features_hbm,
    positions_hbm,
    w_charge_hbm,
    bias_hbm,
    out_ref,
    slim_ref,
    live_ref,
    column_ref,
    features_ref,
    positions_ref,
    w_charge_ref,
    bias_ref,
    sems,
):
    fetch(
        (features_hbm, positions_hbm, w_charge_hbm, bias_hbm),
        (features_ref, positions_ref, w_charge_ref, bias_ref),
        sems,
    )
    n, channels = features_ref.shape
    live_col = lax.broadcasted_iota(jnp.int32, (n, channels), 0) < count_ref[0]
    live_ref[...] = live_col.astype(F32)
    rows = features_ref[...].astype(F32)
    out_ref[0:n, :] = jnp.where(live_col, rows, 0.0).astype(BF16)
    pos = jnp.concatenate([positions_ref[a] for a in range(3)], axis=0)
    coarse = pos.astype(BF16).astype(F32)
    fine = pos - coarse
    living = (lax.broadcasted_iota(jnp.int32, (1, n), 1) < count_ref[0]).astype(F32)
    blank = jnp.zeros((4, n), F32)
    tail = jnp.concatenate([coarse, living, blank, fine, jnp.zeros((5, n), F32)], axis=0)
    out_ref[n : n + 16, :] = tail.astype(BF16)
    charge_ch = w_charge_ref.shape[0]
    diagonal = lax.broadcasted_iota(jnp.int32, (charge_ch, charge_ch), 0) == (
        lax.broadcasted_iota(jnp.int32, (charge_ch, charge_ch), 1)
    )
    column = jnp.sum(jnp.where(diagonal, bias_ref[...], 0.0), axis=1, keepdims=True)
    column_ref[...] = jnp.broadcast_to(column, column_ref.shape)
    v = dot_nt(w_charge_ref[...], out_ref[0:n, :]) + column
    slim_ref[0:charge_ch, :] = (v * sigmoid(v) * living).astype(BF16)
    slim_ref[charge_ch : charge_ch + 16, :] = tail.astype(BF16)


def fold_kernel(
    scale,
    filter_hbm,
    index_hbm,
    energy_hbm,
    proj_hbm,
    mix_hbm,
    out_ref,
    row_ref,
    mixed_ref,
    filter_ref,
    index_ref,
    energy_ref,
    proj_ref,
    mix_ref,
    sems,
):
    fetch(
        (filter_hbm, index_hbm, energy_hbm, proj_hbm, mix_hbm),
        (filter_ref, index_ref, energy_ref, proj_ref, mix_ref),
        sems,
    )
    waves = filter_ref.shape[1]
    charge_ch = filter_ref.shape[0]
    row_ref[...] = energy_ref[...]
    mixed_ref[...] = dot(proj_ref[...], mix_ref[...]).astype(BF16)
    k = index_ref[...]
    positive = [jnp.where(k[a : a + 1, :] >= 0, 1.0, -1.0) for a in range(3)]
    sign_b = positive[0] * positive[1]
    sign_c = positive[0] * positive[2]
    size = jnp.abs(k)
    key = size[2:3, :] * 64 + size[0:1, :] * 8 + size[1:2, :]
    f = filter_ref[...] * scale
    stacked = jnp.concatenate([f, f * sign_b, f * sign_c, f * (sign_b * sign_c)], axis=0).astype(BF16)
    rows = lax.broadcasted_iota(jnp.int32, (ORDERS * 64, waves), 0)
    parts = dot_nt(stacked, jnp.where(rows == key, 1.0, 0.0).astype(BF16))
    turn = jnp.where(lax.broadcasted_iota(jnp.int32, (charge_ch, 128), 1) < 64, -1.0, 1.0)
    for c in range(ORDERS):
        part = parts[:, c * 64 : (c + 1) * 64]
        part = jnp.concatenate([part, part], axis=1)
        for w in range(4):
            piece = part[w * charge_ch : (w + 1) * charge_ch, :]
            out_ref[c, w * charge_ch : (w + 1) * charge_ch, :] = piece * turn if w % 2 == 1 else piece


def full_steps(nz):
    return sorted({0, 1 % nz, nz - 1})


def in_pairs(nz):
    return nz == 4


def row_of(step, nz, full_rows, slim_rows):
    full = full_steps(nz)
    if not isinstance(step, int):
        return pl.multiple_of(lax.div(step + 1, 2) * full_rows, 16)
    if step in full:
        return full.index(step) * full_rows
    return len(full) * full_rows + (step - 2) * slim_rows


def place_rows(ref, q, step, nz, n, charge_ch):
    lo = row_of(step, nz, n + 16, charge_ch + 16) + (n if step in full_steps(nz) else charge_ch)
    tail = ref[q, lo : lo + 16, :].astype(F32)
    return tail[0:8, :] + tail[8:16, :]


def block_place(sizes, odd, block):
    nx, ny, nz = sizes
    dy, dz = (-block[1][0]) % ny, (-block[2][0]) % nz
    if in_pairs(nz) and dz:
        dz = 2 - block[2][0] * (1 - 2 * lax.rem(lax.axis_index(AXES[2]), 2))
    if block[0][0] == 0:
        return 0, dy, dz
    dx = odd * (nx // 2 - 1) if block[0][0] == 1 else (1 - odd) * (1 % (nx // 2))
    return 1, dx * ny + dy, dz


def add_groups(structure, rows, group, sums_ref, first_ref):
    steps = (rows - 1) // group
    if steps <= 4:
        total = first_ref[...]
        for g in range(steps):
            total = total + structure(1 + g * group)
        sums_ref[...] = total
        return
    sums_ref[...] = first_ref[...]

    def add_structure(g, _):
        sums_ref[...] += structure(1 + g * group)
        return 0

    lax.fori_loop(0, steps, add_structure, 0)


def cell_charges(ref, row, step, sizes, w_charge, bias, n):
    charge_ch = w_charge.shape[0]
    nz = sizes[2]
    pos = place_rows(ref, row, step, nz, n, charge_ch)
    lo = row_of(step, nz, n + 16, charge_ch + 16)
    if step in full_steps(nz):
        v = dot_nt(w_charge, ref[row, lo : lo + n, :]) + bias
        return pos, v * sigmoid(v) * pos[3:4, :]
    return pos, ref[row, lo : lo + charge_ch, :].astype(F32)


def charge_sides(pos, charge, m, sizes, base):
    tx, ty, tz = axis_tables(pos, place_of(m, 0, sizes), sizes)
    live = pos[3:4, :]
    living = jnp.concatenate([tz[0] * live, tz[1] * live], axis=0).astype(BF16)
    left = jnp.concatenate([spread((charge - base) * live, tz), living], axis=0)
    return left, plane_table(tx, ty).astype(BF16), jnp.concatenate(tz, axis=0)


def block_radials(pos, block, own_cols, store, n):
    others = [pos[a : a + 1, :] for a in range(3)]
    for first in range(0, n, 32):
        cols = [c[first : first + 32, :] for c in own_cols]
        u, decays = pair_terms(offsets(cols, others, block), block, first)
        u2 = u * u
        for b in range(len(GAMMAS)):
            store(b * n + first, (decays[b] * u2).astype(BF16))


def line_blocks(sizes):
    return [b for b in blocks_of(sizes) if b[0][0] == 0 and b[1][0] == 0]


def line_kernel(
    sizes,
    line_ref,
    w_charge_ref,
    bias_ref,
    sums_ref,
    base_ref,
    places_ref,
    charge_ref,
    gathered_ref,
    planes_ref,
    levels_ref,
    radial_scr,
    xcat_scr,
):
    nz = sizes[2]
    n = places_ref.shape[2]
    w_charge = w_charge_ref[...]
    bias = bias_ref[...]
    cells = [cell_charges(line_ref, 0, step, sizes, w_charge, bias, n) for step in range(nz)]
    charge_ref[...] = cells[0][1]
    total = sum(q for _, q in cells)
    lives = sum(pos[3:4, :] for pos, _ in cells)
    base = jnp.sum(total, axis=1, keepdims=True) / jnp.sum(lives, axis=1, keepdims=True)
    base = base.astype(BF16).astype(F32)
    base_ref[...] = jnp.broadcast_to(base, base_ref.shape)
    left, right = [], []
    for step, (pos, q) in enumerate(cells):
        places_ref[step] = pos
        side, plane, level = charge_sides(pos, q, step, sizes, base)
        planes_ref[step] = plane
        levels_ref[step] = level
        left.append(side)
        right.append(plane)
    sums_ref[...] = dot_nt(jnp.concatenate(left, axis=1), jnp.concatenate(right, axis=1))
    own_cols = columns(cells[0][0], n)
    for t, block in enumerate(line_blocks(sizes)):
        step = block_place(sizes, 0, block)[2]

        def store(row, value, t=t):
            radial_scr[row : row + 32, t * n : (t + 1) * n] = value

        block_radials(places_ref[step], block, own_cols, store, n)
        lo = row_of(step, nz, n + 16, 0)
        xcat_scr[t * n : (t + 1) * n, :] = line_ref[0, pl.ds(lo, n), :]
    gathered_ref[...] = dot(radial_scr[...], xcat_scr[...])


def charge_kernel(
    sizes,
    group,
    near_ref,
    line_sums_ref,
    base_ref,
    line_places_ref,
    w_charge_ref,
    bias_ref,
    sums_ref,
    part_ref,
    places_ref,
    *kept,
):
    charge_ch, channels = w_charge_ref.shape
    nz = sizes[2]
    n = places_ref.shape[2]
    wide = 2 * ORDERS * charge_ch
    w_charge = w_charge_ref[...]
    bias = bias_ref[...]
    base = base_ref[...]
    places_ref[0:nz] = line_places_ref[...]

    def structure(row):
        left, right = [], []
        for r in range(group):
            for step in range(nz):
                pos, q = cell_charges(near_ref, row + r, step, sizes, w_charge, bias, n)
                m = (row + r) * nz + step
                places_ref[m] = pos
                side, plane, level = charge_sides(pos, q, m, sizes, base)
                if kept:
                    kept[0][m - nz] = plane
                    kept[1][m - nz] = level
                left.append(side)
                right.append(plane)
        return dot_nt(jnp.concatenate(left, axis=1), jnp.concatenate(right, axis=1))

    add_groups(structure, near_ref.shape[0], group, sums_ref, line_sums_ref)
    part_ref[0 : wide + 16, :] = sums_ref[...].astype(BF16)
    part_ref[wide + 16 : wide + 16 + charge_ch, :] = jnp.concatenate([base, base], axis=1).astype(BF16)


def message_kernel(
    sizes,
    charge_ch,
    near_ref,
    far_ref,
    near_places_ref,
    mixed_ref,
    line_gathered_ref,
    short_ref,
    far_places_ref,
    xcat_ref,
    radial_scr,
):
    n = short_ref.shape[0]
    nz = sizes[2]
    halves = (near_ref, far_ref)
    places = (near_places_ref, far_places_ref)

    def add_place(row, _):
        for step in range(nz):
            far_places_ref[row * nz + step] = place_rows(far_ref, row, step, nz, n, charge_ch)
        return 0

    lax.fori_loop(0, far_ref.shape[0], add_place, 0, unroll=min(4, far_ref.shape[0]))
    odd = lax.rem(lax.axis_index(AXES[0]), 2)
    own_cols = columns(near_places_ref[0], n)
    done = 0
    for t, block in enumerate(blocks_of(sizes)):
        half, row, step = block_place(sizes, odd, block)
        lo = row_of(step, nz, n + 16, 0)
        xcat_ref[t * n : (t + 1) * n, :] = halves[half][row, pl.ds(lo, n), :]
        pos = places[half][row * nz + step]
        if block in line_blocks(sizes):
            continue

        def store(place, value, t=done):
            radial_scr[place : place + 32, t * n : (t + 1) * n] = value

        block_radials(pos, block, own_cols, store, n)
        done += 1
    rest = xcat_ref[len(line_blocks(sizes)) * n :, :]
    gathered = (line_gathered_ref[...] + dot(radial_scr[...], rest)).astype(BF16)
    gathered = jnp.concatenate([gathered[b * n : (b + 1) * n, :] for b in range(len(GAMMAS))], axis=1)
    short_ref[...] = dot(gathered, mixed_ref[...])


def cotangent_kernel(
    sizes,
    live_ref,
    sums_ref,
    part_ref,
    far_part_ref,
    places_ref,
    far_places_ref,
    charge_ref,
    short_ref,
    features_ref,
    w_long_ref,
    w_energy_ref,
    filt_ref,
    *rest,
):
    planes_ref, levels_ref, grad_ref, pull_ref, refined_ref, field_ref, neutral_ref = rest
    n, channels = features_ref.shape
    charge_ch = w_long_ref.shape[0]
    wide = 2 * ORDERS * charge_ch
    own = places_ref[0]
    live_row = own[3:4, :]

    lives = [jnp.sum(r[...], axis=0)[3:4, :] for r in (places_ref, far_places_ref)]
    lives = [jnp.sum(v, axis=1, keepdims=True) for v in lives]
    tail = wide + 16
    bases = [r[tail : tail + charge_ch, 0:1].astype(F32) for r in (part_ref, far_part_ref)]
    rests = [sums_ref[0:charge_ch, 0:1], far_part_ref[0:charge_ch, 0:1].astype(F32)]
    mean = (bases[0] * lives[0] + rests[0] + bases[1] * lives[1] + rests[1]) / (lives[0] + lives[1])
    gaps = [b - mean for b in bases]
    far_living = far_part_ref[wide : wide + 16, :].astype(F32)

    def load(kind, c):
        lo = (kind * ORDERS + c) * charge_ch
        row = kind * 8 + c
        return (
            sums_ref[lo : lo + charge_ch, :]
            + far_part_ref[lo : lo + charge_ch, :].astype(F32)
            + gaps[0] * sums_ref[wide + row : wide + row + 1, :]
            + gaps[1] * far_living[row : row + 1, :]
        )

    filtered(load, filt_ref, field_ref, charge_ch)
    neutral_ref[...] = (charge_ref[...] - mean) * live_row
    plane = planes_ref[0]
    tz = (levels_ref[0, 0:8, :], levels_ref[0, 8:16, :])
    lifted = dot(field_ref[...], plane)
    potential = jnp.zeros((charge_ch, n), F32)
    for kind in range(2):
        for c in range(ORDERS):
            lo = (kind * ORDERS + c) * charge_ch
            potential = potential + tz[kind][c : c + 1, :] * lifted[lo : lo + charge_ch, :]
    pre_act = short_ref[...] + dot(jnp.transpose(potential).astype(BF16), w_long_ref[...])
    sig = sigmoid(pre_act)
    refined = features_ref[...].astype(F32) + pre_act * sig
    refined_ref[...] = refined
    sig_r = sigmoid(refined)
    grad = (
        w_energy_ref[...]
        * (sig_r * (1.0 + refined * (1.0 - sig_r)))
        * (sig * (1.0 + pre_act * (1.0 - sig)))
    )
    grad = (grad * live_ref[...]).astype(BF16)
    grad_ref[...] = grad
    pull_ref[...] = dot_nt(w_long_ref[...], grad).astype(BF16)


def pair_force(sizes, places, strengths_ref, n, slopes_to=None, slopes_from=None):
    own_cols = columns(places[0][0], n)
    odd = lax.rem(lax.axis_index(AXES[0]), 2)
    blocks = blocks_of(sizes)
    parts = [[], [], []]
    for first in range(0, n, 32):
        cols = [c[first : first + 32, :] for c in own_cols]
        acc = [jnp.zeros((32, n), F32) for _ in range(3)]
        for t, block in enumerate(blocks):
            half, row, step = block_place(sizes, odd, block)
            pos = places[half][row * sizes[2] + step]
            offs = offsets(cols, [pos[a : a + 1, :] for a in range(3)], block)
            if slopes_from is None:
                u, decays = pair_terms(offs, block, first)
            strength = jnp.zeros((32, n), F32)
            for b, g in enumerate(GAMMAS):
                lo = b * n + first
                part = strengths_ref[lo : lo + 32, t * n : (t + 1) * n]
                if slopes_from is None:
                    slope = decays[b] * (g * u + 2.0) * u
                else:
                    slope = slopes_from[lo : lo + 32, t * n : (t + 1) * n]
                if slopes_to is not None:
                    slopes_to[lo : lo + 32, t * n : (t + 1) * n] = slope
                strength = strength + slope * part
            for a in range(3):
                acc[a] = acc[a] + strength * offs[a]
        for a in range(3):
            parts[a].append(acc[a])
    return [
        (-2.0 * SCALE)
        * jnp.sum(jnp.transpose(jnp.concatenate(parts[a], axis=0)), axis=0, keepdims=True)
        for a in range(3)
    ]


def own_kernel(
    sizes,
    grad_ref,
    field_ref,
    places_ref,
    far_places_ref,
    xcat_ref,
    refined_ref,
    mixed_ref,
    w_long_ref,
    w_energy_ref,
    updated_ref,
    energy_ref,
    force_ref,
    lifted_ref,
    planes_ref,
    levels_ref,
    *rest,
):
    *slopes, strength_scr = rest
    n = grad_ref.shape[0]
    charge_ch = w_long_ref.shape[0]
    own = places_ref[0]
    refined = refined_ref[...]
    updated_ref[...] = refined.astype(BF16)
    energy_ref[...] = own[3:4, :] * jnp.sum(
        jnp.transpose(refined * sigmoid(refined) * w_energy_ref[...]), axis=0, keepdims=True
    )
    grad = grad_ref[...]
    channels = grad.shape[1]
    rows, lifted = [], []
    for b in range(len(GAMMAS)):
        mixed = mixed_ref[b * channels : (b + 1) * channels, :]
        rows.append(dot_nt(grad, mixed).astype(BF16))
        lifted.append(dot(xcat_ref[0:n, :], mixed).astype(BF16))
    lifted_ref[...] = jnp.concatenate(lifted, axis=0)
    strength_scr[...] = dot_nt(jnp.concatenate(rows, axis=0), xcat_ref[...])
    places = (places_ref, far_places_ref)
    near = pair_force(sizes, places, strength_scr, n, slopes[0] if slopes else None)
    pull = dot_nt(w_long_ref[...], grad)
    tables = axis_tables(own, place_of(0, 0, sizes), sizes)
    planes = slope_planes(tables, sizes)
    planes_ref[...] = planes
    levels_ref[...] = jnp.concatenate(tables[2], axis=0)
    slope = field_slope(field_ref[...], planes, tables[2], sizes, pull, charge_ch)
    force_ref[...] = jnp.concatenate([near[a] - slope[a] for a in range(3)], axis=0)


def pull_sides(ref, row, sizes, w_long, tables, n):
    charge_ch = w_long.shape[0]
    nz = sizes[2]
    pulls = dot_nt(w_long, ref[row, 0 : len(full_steps(nz)) * n, :])
    left, right = [], []
    for step in range(nz):
        lo = row_of(step, nz, n, charge_ch)
        if step in full_steps(nz):
            pull = pulls[:, lo : lo + n]
        else:
            pull = ref[row, lo : lo + charge_ch, :].astype(F32)
        plane, tz = tables(row, step)
        left.append(spread(pull, tz))
        right.append(plane)
    return left, right


def line_pull_kernel(sizes, line_ref, planes_ref, levels_ref, w_long_ref, sums_ref):
    n = levels_ref.shape[2]

    def tables(row, step):
        return planes_ref[step], (levels_ref[step, 0:8, :], levels_ref[step, 8:16, :])

    left, right = pull_sides(line_ref, 0, sizes, w_long_ref[...], tables, n)
    sums_ref[...] = dot_nt(jnp.concatenate(left, axis=1), jnp.concatenate(right, axis=1))


def pull_kernel(sizes, group, near_ref, line_sums_ref, places_ref, w_long_ref, *rest):
    *kept, sums_ref, part_ref = rest
    nz = sizes[2]
    n = places_ref.shape[2]

    def tables(row, step):
        m = row * nz + step
        if kept:
            return kept[0][m - nz], (kept[1][m - nz, 0:8, :], kept[1][m - nz, 8:16, :])
        tx, ty, tz = axis_tables(places_ref[m], place_of(m, 0, sizes), sizes)
        return plane_table(tx, ty).astype(BF16), tz

    def structure(row):
        left, right = [], []
        for r in range(group):
            sides = pull_sides(near_ref, row + r, sizes, w_long_ref[...], tables, n)
            left += sides[0]
            right += sides[1]
        return dot_nt(jnp.concatenate(left, axis=1), jnp.concatenate(right, axis=1))

    add_groups(structure, near_ref.shape[0], group, sums_ref, line_sums_ref)
    part_ref[...] = sums_ref[...].astype(BF16)


def react_kernel(
    sizes,
    near_ref,
    far_ref,
    places_ref,
    far_places_ref,
    lifted_ref,
    force_ref,
    *rest,
):
    *slopes, out_ref, gcat_scr, strength_scr = rest
    n = force_ref.shape[1]
    halves = (near_ref, far_ref)
    odd = lax.rem(lax.axis_index(AXES[0]), 2)
    for t, block in enumerate(blocks_of(sizes)):
        half, row, step = block_place(sizes, odd, block)
        lo = row_of(step, sizes[2], n, 0)
        gcat_scr[t * n : (t + 1) * n, :] = halves[half][row, pl.ds(lo, n), :]
    strength_scr[...] = dot_nt(lifted_ref[...], gcat_scr[...])
    places = (places_ref, far_places_ref)
    near = pair_force(sizes, places, strength_scr, n, None, slopes[0] if slopes else None)
    out_ref[...] = force_ref[...] + jnp.concatenate(near, axis=0)


def finish_kernel(
    sizes,
    sums_ref,
    far_part_ref,
    planes_ref,
    levels_ref,
    neutral_ref,
    force_ref,
    filt_ref,
    out_ref,
    field_scr,
):
    charge_ch = neutral_ref.shape[0]

    def load(kind, c):
        lo = (kind * ORDERS + c) * charge_ch
        return sums_ref[lo : lo + charge_ch, :] + far_part_ref[lo : lo + charge_ch, :].astype(F32)

    filtered(load, filt_ref, field_scr, charge_ch)
    tz = (levels_ref[0:8, :], levels_ref[8:16, :])
    slope = field_slope(field_scr[...], planes_ref[...], tz, sizes, neutral_ref[...], charge_ch)
    for a in range(3):
        out_ref[a] = force_ref[a : a + 1, :] - slope[a]


def gather_line(full, slim, nz):
    def moved(step):
        rows = full if step in full_steps(nz) else slim
        return lax.ppermute(
            rows, "gz", [(i, i ^ step if in_pairs(nz) else (i + step) % nz) for i in range(nz)]
        )

    steps = sorted(range(1, nz), key=lambda step: step not in full_steps(nz))
    return jnp.concatenate([full] + [moved(step) for step in steps], axis=0)[None]


def gather_cells(value, sizes, beside):
    nx, ny, nz = sizes
    pairs = nx // 2

    def shifted(value, dx, dy):
        moves = []
        for i in range(nx):
            for j in range(ny):
                moves.append((i * ny + j, (i + 2 * dx) % nx * ny + (j + dy) % ny))
        return lax.ppermute(value, ("gx", "gy"), moves)

    if pairs * ny <= 4:
        steps = [(dx, dy) for dx in range(pairs) for dy in range(ny)]
        value = jnp.concatenate(
            [value] + [shifted(value, dx, dy) for dx, dy in steps[1:]], axis=0
        )
    else:
        value = jnp.concatenate([value] + [shifted(value, 0, dy) for dy in range(1, ny)], axis=0)
        value = jnp.concatenate([value] + [shifted(value, dx, 0) for dx in range(1, pairs)], axis=0)
    value, *beside = lax.optimization_barrier((value, *beside))
    return value, *beside


def from_other_core(value):
    return lax.ppermute(value, "gx", [(i, i ^ 1) for i in range(lax.axis_size("gx"))])


def call(kernel, name, outs, scratch, operands, kept, limit, flops, fetched):
    n_in = len(operands)
    first = n_in - kept
    operands = [
        pltpu.with_memory_space_constraint(o, pltpu.HBM if fetched else pltpu.VMEM)
        if (fetched and o.size > 1) or i >= first
        else o
        for i, o in enumerate(operands)
    ]
    specs = [
        pl.BlockSpec(
            memory_space=pltpu.SMEM if o.size == 1 else pltpu.HBM if fetched else pltpu.VMEM
        )
        for o in operands
    ]
    return pl.pallas_call(
        kernel,
        name=name,
        out_shape=outs,
        in_specs=specs,
        out_specs=[pl.BlockSpec(memory_space=pltpu.VMEM)] * len(outs),
        scratch_shapes=scratch,
        compiler_params=pltpu.CompilerParams(vmem_limit_bytes=limit),
        cost_estimate=pl.CostEstimate(flops=flops, bytes_accessed=2_000_000, transcendentals=0),
    )(*operands)


def shards(
    features,
    positions,
    counts,
    w_proj,
    w_mix,
    w_long,
    w_charge,
    charge_bias,
    w_energy,
    k_filter,
    k_index,
):
    own_rows = features[0, 0, 0]
    n, channels = own_rows.shape
    charge_ch = w_charge.shape[0]
    waves = k_index.shape[1]
    bases = w_proj.shape[0]
    sizes = tuple(lax.axis_size(a) for a in AXES)
    cells = sizes[0] * sizes[1] * sizes[2]
    half_cells = cells // 2
    lines = half_cells // sizes[2]
    group = lines - 1 if cells <= 32 else 1
    near_line = len(line_blocks(sizes))
    blocks = len(blocks_of(sizes))
    scale_long = 4.0 / math.sqrt(n * cells * waves)
    count = counts.reshape(1)
    shape = jax.ShapeDtypeStruct
    wide = 2 * ORDERS * charge_ch
    fits = cells <= 64
    limit = (24 if fits else 56) * 1024 * 1024
    held = pltpu.VMEM if fits else shape

    def run(kernel, name, outs, scratch, operands, kept, flops, fetched=False):
        kept = kept if fits else 0
        if fetched:
            places = [pltpu.VMEM(o.shape, o.dtype) for o in operands if o.size > 1]
            scratch = [*places, pltpu.SemaphoreType.DMA((len(places),))]
        return call(kernel, name, outs, scratch, operands, kept, limit, flops, fetched)

    packed, slim, live, bias = run(
        pack_kernel,
        "pack",
        [
            held((n + 16, channels), BF16),
            held((charge_ch + 16, n), BF16),
            held((n, channels), F32),
            held((charge_ch, n), F32),
        ],
        [],
        [count, own_rows, positions.reshape(3, 1, n), w_charge, charge_bias[None, :]],
        0,
        1000,
        fetched=True,
    )
    filt, energy_row, mixed = run(
        lambda *refs: fold_kernel(scale_long, *refs),
        "fold_filter",
        [
            held((ORDERS, 4 * charge_ch, 128), F32),
            held((1, channels), F32),
            held((bases * channels, channels), BF16),
        ],
        [],
        [
            k_filter,
            k_index,
            w_energy[None, :],
            w_proj.reshape(bases * channels, channels),
            w_mix,
        ],
        0,
        1_000_000_000,
        fetched=True,
    )
    line = gather_line(packed, slim, sizes[2])
    line, filt, energy_row, mixed = lax.optimization_barrier((line, filt, energy_row, mixed))
    line_sums, base, line_places, charge, line_gathered, line_planes, line_levels = run(
        lambda *refs: line_kernel(sizes, *refs),
        "line_sums",
        [
            held((wide + 16, 256), F32),
            held((charge_ch, n), F32),
            held((sizes[2], 8, n), F32),
            held((charge_ch, n), F32),
            held((bases * n, channels), F32),
            held((sizes[2], 256, n), BF16),
            held((sizes[2], 16, n), F32),
        ],
        [
            pltpu.VMEM((bases * n, near_line * n), BF16),
            pltpu.VMEM((near_line * n, channels), BF16),
        ],
        [line, w_charge, bias],
        3,
        1_000_000_000,
    )
    near, line_sums = gather_cells(line, sizes, (line_sums,))
    far = from_other_core(near)
    sums, part, places, *kept = run(
        lambda *refs: charge_kernel(sizes, group, *refs),
        "charge_sums",
        [
            held((wide + 16, 256), F32),
            held((wide + 16 + charge_ch, 256), BF16),
            held((half_cells, 8, n), F32),
        ]
        + (
            [
                held((half_cells - sizes[2], 256, n), BF16),
                held((half_cells - sizes[2], 16, n), F32),
            ]
            if fits
            else []
        ),
        [],
        [near, line_sums, base, line_places, w_charge, bias],
        6,
        3_000_000_000,
    )
    far_part = from_other_core(part)
    short, far_places, xcat = run(
        lambda *refs: message_kernel(sizes, charge_ch, *refs),
        "message",
        [
            held((n, channels), F32),
            held((half_cells, 8, n), F32),
            held((blocks * n, channels), BF16),
        ],
        [pltpu.VMEM((bases * n, (blocks - near_line) * n), BF16)],
        [near, far, places, mixed, line_gathered],
        5,
        3_000_000_000,
    )
    grad, pull, refined, field, neutral = run(
        lambda *refs: cotangent_kernel(sizes, *refs),
        "cotangents",
        [
            held((n, channels), BF16),
            held((charge_ch, n), BF16),
            held((n, channels), F32),
            held((wide, 256), BF16),
            held((charge_ch, n), F32),
        ],
        [],
        [
            live,
            sums,
            part,
            far_part,
            places,
            far_places,
            charge,
            short,
            own_rows,
            w_long,
            energy_row,
            filt,
            line_planes,
            line_levels,
        ],
        14,
        3_000_000_000,
    )
    grad_line, grad = lax.optimization_barrier((gather_line(grad, pull, sizes[2]), grad))
    updated, energy, force, lifted, planes, levels, *slopes = run(
        lambda *refs: own_kernel(sizes, *refs),
        "own_terms",
        [
            shape((n, channels), BF16),
            shape((1, n), F32),
            held((3, n), F32),
            held((bases * n, channels), BF16),
            held((256, 3 * n), BF16),
            held((16, n), F32),
        ]
        + ([held((bases * n, blocks * n), F32)] if fits else []),
        [pltpu.VMEM((bases * n, blocks * n), F32)],
        [
            grad,
            field,
            places,
            far_places,
            xcat,
            refined,
            mixed,
            w_long,
            energy_row,
        ],
        9,
        4_000_000_000,
    )
    (line_back,) = run(
        lambda *refs: line_pull_kernel(sizes, *refs),
        "line_pulls",
        [held((wide, 256), F32)],
        [],
        [grad_line, line_planes, line_levels, w_long],
        4,
        1_000_000_000,
    )
    grad_near, force, lifted, line_back = gather_cells(grad_line, sizes, (force, lifted, line_back))
    grad_far = from_other_core(grad_near)
    back, back_part = run(
        lambda *refs: pull_kernel(sizes, group, *refs),
        "pull_sums",
        [held((wide, 256), F32), held((wide, 256), BF16)],
        [],
        [grad_near, line_back, places, w_long, *kept],
        4 + len(kept),
        3_000_000_000,
    )
    far_back = from_other_core(back_part)
    (force,) = run(
        lambda *refs: react_kernel(sizes, *refs),
        "react",
        [held((3, n), F32)],
        [
            pltpu.VMEM((blocks * n, channels), BF16),
            pltpu.VMEM((bases * n, blocks * n), F32),
        ],
        [grad_near, grad_far, places, far_places, lifted, force, *slopes],
        6 + len(slopes),
        3_000_000_000,
    )
    (forces,) = run(
        lambda *refs: finish_kernel(sizes, *refs),
        "finish",
        [shape((3, 1, n), F32)],
        [pltpu.VMEM((wide, 256), BF16)],
        [back, far_back, planes, levels, neutral, force, filt],
        7,
        2_000_000_000,
    )
    return (
        updated[None, None, None],
        energy[None, None],
        forces.reshape(positions.shape),
    )


def solution(mesh):
    cell = ("gx", "gy", "gz")
    in_specs = (P(*cell, None, None), P(*cell, None, None), P(*cell)) + (P(),) * 8
    out_specs = (P(*cell, None, None), P(*cell, None), P(*cell, None, None))
    return jax.shard_map(shards, mesh=mesh, in_specs=in_specs, out_specs=out_specs, check_vma=False)
```
